128 devices in a mesh: row: 16 (over x, z), col: 8 (over y, core).
Axes of the slice: x: 4, y: 4, z: 4, core: 2. Of those that a mesh axis runs over, the one named last changes fastest.
Arguments:
- blocks: bfloat16 [16, 8, 96, 256, 256], P('row', 'col'), may hold values from -6 to 6
- sketch: bfloat16 [262144, 128], P('col'), may hold values from -6 to 6
- block_row: int32 [16, 8, 96], P('row', 'col'), may hold values from 0 to 127, as said below
- block_col: int32 [16, 8, 96], P('row', 'col'), may hold values from 0 to 127
- counts: int32 [16, 8], P('row', 'col'), may hold values from 12 to 96, as said below
Outputs:
- q_scaled: float32 [524288, 128], P(('row', 'col'))
- z_out: float32 [8, 32768, 128], P('col', 'row')
The draws below stay inside these ranges and needn't reach their ends.
Inputs may be any that keep to these rules, and one draw needn't show every extreme that they name: `block_row`: block row of a slot among the 128 block rows of its device. `counts`: slots at or beyond a device's count are not part of the matrix.
All inputs are finite; a program needn't handle non-finite values.
Results may differ from the reference program's by a relative error of at most 0.0019.
Values may be sent and summed in bfloat16 or wider, within the bound.
No kernel may reach another device: no remote copies, remote signals or barrier semaphores. Data moves between devices by JAX's collectives and lax.ppermute only.
A program may use at most 192 MiB of HBM per device.

```python
import math
import jax
import jax.numpy as jnp
from jax import lax

B = 256
K = 128
BR = 128
BC = 128
NBLK = 96
N_COLS = 262144
N_ROW = 16
N_COL = 8


def draw_block_row(key, part):
    key = jax.random.fold_in(key, 11)
    first, second, third = jax.random.split(key, 3)
    pick_one = jax.random.randint(first, (N_ROW, N_COL, NBLK), 0, BR)
    pick_two = jax.random.randint(second, (N_ROW, N_COL, NBLK), 0, BR)
    ranked = jnp.minimum(pick_one, pick_two)
    orders = jax.vmap(lambda single: jax.random.permutation(single, BR))(jax.random.split(third, N_ROW * N_COL))
    orders = orders.reshape(N_ROW, N_COL, BR)
    return jnp.take_along_axis(orders, ranked, axis=2).astype(jnp.int32)


def draw_counts(key, part):
    key = jax.random.fold_in(key, 13)
    first, second, third = jax.random.split(key, 3)
    levels = jax.random.permutation(first, N_ROW) % 4 + 1
    dropped = jax.random.randint(second, (N_ROW, N_COL), 0, NBLK // 8 + 1)
    live_total = jnp.clip(levels[:, None] * (NBLK // 4) - dropped, NBLK // 8, NBLK)
    chosen_device = jax.random.randint(third, (), 0, N_ROW * N_COL)
    flat_index = jnp.arange(N_ROW * N_COL).reshape(N_ROW, N_COL)
    return jnp.where(flat_index == chosen_device, NBLK, live_total).astype(jnp.int32)


def touch_ends(result, stream_key, smallest, largest):
    spot = [jax.random.randint(jax.random.fold_in(stream_key, axis), (), 0, length) for axis, length in enumerate(result.shape)]
    main_axis = result.shape.index(max(result.shape))
    next_to = spot[:main_axis] + [(spot[main_axis] + 1) % result.shape[main_axis]] + spot[main_axis + 1:]
    return result.at[tuple(spot)].set(smallest).at[tuple(next_to)].set(largest)


def block_levels(own_key, dims, cuts, least, largest):
    def one(position, parts):
        heights = jax.random.uniform(jax.random.fold_in(jax.random.fold_in(own_key, 6), position), (parts,), jnp.float32, least / len(cuts), largest / len(cuts))
        return jnp.repeat(jnp.exp(heights), dims[position] // parts).reshape((-1,) + (1,) * (len(dims) - position - 1))

    factor_of = one(*cuts[0])
    for cut in cuts[1:]:
        factor_of = factor_of * one(*cut)
    return factor_of


def normal_values(key, shape, spread, bound, cuts=(), held_as=jnp.bfloat16):
    loudness = block_levels(key, shape, cuts, -0.22, 0.18) if cuts else 1.0
    drawn = jax.random.normal(key, shape, jnp.float32) * spread * loudness
    return jnp.minimum(jnp.maximum(drawn, -bound), bound).astype(held_as)


def setup_inputs(seed: int = 0) -> dict:
    seeds = jax.random.split(jax.random.key(seed), 6)
    blocks = normal_values(seeds[0], (N_ROW, N_COL, NBLK, B, B), 1.0, 6.0, ((0, 16), (1, 8)))
    sketch = normal_values(seeds[1], (N_COLS, K), 1.0, 6.0, ((0, 8),))
    block_row = draw_block_row(jax.random.fold_in(seeds[5], 71), 0)
    block_col = touch_ends(jax.random.randint(seeds[3], (N_ROW, N_COL, NBLK), 0, BC), jax.random.fold_in(seeds[3], 1), 0, BC - 1).astype(jnp.int32)
    counts = draw_counts(jax.random.fold_in(seeds[5], 71), 0)
    return {"blocks": blocks, "sketch": sketch, "block_row": block_row, "block_col": block_col, "counts": counts}


def reference(blocks, sketch, block_row, block_col, counts):
    highest = lax.Precision.HIGHEST
    flat_blocks = blocks.reshape(N_ROW * N_COL, NBLK, B, B)
    row_targets = (block_row + (jnp.arange(N_ROW, dtype=jnp.int32) * BR)[:, None, None]).astype(jnp.int32).reshape(N_ROW * N_COL, NBLK)
    col_targets = (block_col + (jnp.arange(N_COL, dtype=jnp.int32) * BC)[None, :, None]).astype(jnp.int32).reshape(N_ROW * N_COL, NBLK)
    live_mask = (jnp.arange(NBLK, dtype=jnp.int32)[None, None, :] < counts[:, :, None]).astype(jnp.float32).reshape(N_ROW * N_COL, NBLK)
    sketch_table = sketch.reshape(N_COL * BC, B, K)

    def add_rows(running, slot_data):
        tile_set, rows_at, cols_at, alive = slot_data
        chosen = sketch_table[cols_at].astype(jnp.float32)
        product = jnp.einsum('sij,sjk->sik', tile_set.astype(jnp.float32), chosen, precision=highest)
        return (running.at[rows_at].add(product * alive[:, None, None]), None)
    y_start = jnp.zeros((N_ROW * BR, B, K), jnp.float32)
    y_full, _ = lax.scan(add_rows, y_start, (flat_blocks, row_targets, col_targets, live_mask))
    y_full = y_full.reshape(N_ROW * BR * B, K)
    gram = jnp.dot(y_full.T.astype(jnp.float32), y_full.astype(jnp.float32), precision=highest, preferred_element_type=jnp.float32)
    lower_factor = jnp.linalg.cholesky(gram)
    q_full = lax.linalg.triangular_solve(lower_factor, y_full, left_side=False, lower=True, transpose_a=True)
    q_scaled = q_full * math.sqrt(N_ROW * BR * B)
    q_half = q_full.astype(jnp.bfloat16)
    q_table = q_half.reshape(N_ROW * BR, B, K)

    def add_cols(running, slot_data):
        tile_set, rows_at, cols_at, alive = slot_data
        chosen = q_table[rows_at].astype(jnp.float32)
        product = jnp.einsum('sij,sik->sjk', tile_set.astype(jnp.float32), chosen, precision=highest)
        return (running.at[cols_at].add(product * alive[:, None, None]), None)
    z_start = jnp.zeros((N_COL * BC, B, K), jnp.float32)
    z_full, _ = lax.scan(add_cols, z_start, (flat_blocks, row_targets, col_targets, live_mask))
    return (q_scaled, z_full.reshape(N_COL, BC * B, K))
```

```python
import math

import jax
import jax.numpy as jnp
from jax import lax
from jax.experimental import pallas as pl
from jax.experimental.pallas import tpu as pltpu
from jax.sharding import PartitionSpec as P

B = 256
K = 128
BR = 128
BC = 128
NBLK = 96
AHEAD = 24
VMEM_BYTES = 56 * 1024 * 1024
f32 = jnp.float32
f16 = jnp.float16


def ring(shift):
    return [(c, ((c // 2 + shift) % 4) * 2 + c % 2) for c in range(8)]


def along_x(shift):
    return [(r, ((r // 4 + shift) % 4) * 4 + r % 4) for r in range(16)]


def along_z(shift):
    return [(r, (r // 4) * 4 + (r % 4 + shift) % 4) for r in range(16)]


PAIR = [(c, c ^ 1) for c in range(8)]


def y_kernel(rows, cols, info, blocks, sketch, out, stat, order, block_buf, sketch_buf, sems):
    count, core, here = info[0], info[1], info[2]

    def pick(s, n):
        order[n] = s
        return n + jnp.where(((rows[s] >> 4) & 1) == core, 1, 0)

    order[0] = 0
    total = lax.fori_loop(0, count, pick, 0)

    def copies(j):
        s = order[j]
        return (
            pltpu.make_async_copy(blocks.at[s], block_buf.at[j], sems.at[0, j]),
            pltpu.make_async_copy(sketch.at[cols[s]], sketch_buf.at[j], sems.at[1, j]),
        )

    def begin(j, _):
        for copy in copies(j):
            copy.start()
        return 0

    lax.fori_loop(0, jnp.minimum(total, AHEAD), begin, 0)

    def clear(t, _):
        out[t] = jnp.zeros((B, K), f32)
        return 0

    lax.fori_loop(0, BR // 2, clear, 0)

    def step(j, carry):
        bound, largest = carry

        @pl.when(j + AHEAD < total)
        def _():
            begin(j + AHEAD, 0)

        for copy in copies(j):
            copy.wait()
        row = rows[order[j]]
        target = ((((row >> 5) - here) & 3) << 4) | (row & 15)
        tile = block_buf[j]
        product = jnp.dot(tile, sketch_buf[j], preferred_element_type=f32)
        out[target] += product
        bound = bound + jnp.max(jnp.abs(product).reshape(B // 8, 8, K), axis=0)
        largest = jnp.maximum(largest, jnp.max(jnp.abs(tile).reshape(B // 16, 16, B), axis=0))
        return bound, largest

    bound, largest = lax.fori_loop(
        0, total, step, (jnp.zeros((8, K), f32), jnp.zeros((16, B), jnp.bfloat16))
    )
    stat[0] = bound
    wide = largest.astype(f32)
    stat[1] = jnp.maximum(
        jnp.maximum(wide[:8, :K], wide[8:, :K]), jnp.maximum(wide[:8, K:], wide[8:, K:])
    )


def partial_rows(rows, cols, info, blocks, sketch):
    return pl.pallas_call(
        y_kernel,
        out_shape=(
            jax.ShapeDtypeStruct((BR // 2, B, K), f32),
            jax.ShapeDtypeStruct((2, 8, K), f32),
        ),
        in_specs=[pl.BlockSpec(memory_space=pltpu.SMEM)] * 3
        + [pl.BlockSpec(memory_space=pl.ANY)] * 2,
        out_specs=(
            pl.BlockSpec(memory_space=pltpu.VMEM),
            pl.BlockSpec(memory_space=pltpu.VMEM),
        ),
        scratch_shapes=[
            pltpu.SMEM((NBLK + 1,), jnp.int32),
            pltpu.VMEM((NBLK, B, B), jnp.bfloat16),
            pltpu.VMEM((NBLK, B, K), jnp.bfloat16),
            pltpu.SemaphoreType.DMA((2, NBLK)),
        ],
        compiler_params=pltpu.CompilerParams(vmem_limit_bytes=VMEM_BYTES),
        cost_estimate=pl.CostEstimate(
            flops=NBLK * B * B * K, bytes_accessed=18 * 1024 * 1024, transcendentals=0
        ),
        name="partial_rows",
    )(rows, cols, info, blocks, sketch)


def z_kernel(half, rows, cols, info, blocks, *rest):
    tables, (out, order, block_buf, y_buf, sems) = rest[:16], rest[16:]
    count, core, here_y, here_x, here_z = info[0], info[1], info[2], info[3], info[4]

    def pick(s, n):
        order[n] = s
        return n + jnp.where(((cols[s] >> 2) & 1) == half, 1, 0)

    order[0] = 0
    total = lax.fori_loop(0, count, pick, 0)

    def block_copy(j):
        return pltpu.make_async_copy(blocks.at[order[j]], block_buf.at[j], sems.at[0, j])

    def y_copy(j, table, inner):
        return pltpu.make_async_copy(table.at[inner], y_buf.at[j], sems.at[1, j])

    def begin(j, _):
        block_copy(j).start()
        row = rows[order[j]]
        source = (
            ((((row >> 4) & 1) ^ core) << 3) | ((((row >> 5) - here_y) & 3) << 1) | ((row >> 3) & 1)
        )

        def choose(low, size):
            if size == 1:
                y_copy(j, tables[low], row & 7).start()
                return
            mid = low + size // 2
            pl.when(source < mid)(lambda: choose(low, size // 2))
            pl.when(source >= mid)(lambda: choose(mid, size // 2))

        choose(0, 16)
        return 0

    lax.fori_loop(0, jnp.minimum(total, AHEAD), begin, 0)

    def clear(t, _):
        out[t] = jnp.zeros((B, K), f32)
        return 0

    lax.fori_loop(0, BC // 2, clear, 0)

    def step(j, _):
        @pl.when(j + AHEAD < total)
        def _():
            begin(j + AHEAD, 0)

        block_copy(j).wait()
        y_copy(j, tables[0], 0).wait()
        col = cols[order[j]]
        rel_x = ((col >> 5) - here_x) & 3
        rel_z = ((col >> 3) - here_z) & 3
        if half == 0:
            target = (rel_x << 4) | (rel_z << 2) | (col & 3)
        else:
            target = (rel_z << 4) | (rel_x << 2) | (col & 3)
        value = y_buf[j]
        high = value.astype(jnp.bfloat16)
        low = (value - high.astype(f32)).astype(jnp.bfloat16)
        both = jnp.concatenate([high, low], axis=1)
        product = lax.dot_general(
            block_buf[j], both, (((0,), (0,)), ((), ())), preferred_element_type=f32
        )
        out[target] += product[:, :K] + product[:, K:]
        return 0

    lax.fori_loop(0, total, step, 0)


def partial_cols(half, rows, cols, info, blocks, tables):
    def kernel(*refs):
        z_kernel(half, *refs)

    return pl.pallas_call(
        kernel,
        out_shape=jax.ShapeDtypeStruct((BC // 2, B, K), f32),
        in_specs=[pl.BlockSpec(memory_space=pltpu.SMEM)] * 3
        + [pl.BlockSpec(memory_space=pl.ANY)] * 17,
        out_specs=pl.BlockSpec(memory_space=pltpu.VMEM),
        scratch_shapes=[
            pltpu.SMEM((NBLK + 1,), jnp.int32),
            pltpu.VMEM((NBLK, B, B), jnp.bfloat16),
            pltpu.VMEM((NBLK, B, K), f32),
            pltpu.SemaphoreType.DMA((2, NBLK)),
        ],
        compiler_params=pltpu.CompilerParams(vmem_limit_bytes=VMEM_BYTES),
        cost_estimate=pl.CostEstimate(
            flops=NBLK * B * B * K * 2, bytes_accessed=22 * 1024 * 1024, transcendentals=0
        ),
        name="partial_cols",
    )(rows, cols, info, blocks, *tables)


def scale_for(bound):
    return jnp.exp2(jnp.ceil(jnp.log2(jnp.maximum(bound, 1e-30))) - 15.0)


def ring_sum(pieces, send, scale):
    inverse = 1.0 / scale

    def pack(value):
        return (value * inverse).astype(f16)

    def unpack(value):
        return value.astype(f32) * scale

    far_up = send(pack(pieces[2][0]), 1)
    far_down = send(pack(pieces[2][1]), -1)
    near_up = send(pack(pieces[1][1]), 1)
    near_down = send(pack(pieces[3][0]), -1)
    sum_up = send(pack(pieces[1][0] + unpack(far_up)), 1)
    sum_down = send(pack(pieces[3][1] + unpack(far_down)), -1)
    return (
        pieces[0][0] + unpack(near_down) + unpack(sum_up),
        pieces[0][1] + unpack(near_up) + unpack(sum_down),
    )


def body(blocks, sketch, block_row, block_col, counts):
    highest = lax.Precision.HIGHEST
    blocks = blocks[0, 0]
    rows, cols = block_row[0, 0], block_col[0, 0]
    count = counts[0, 0]
    row_at, col_at = lax.axis_index("row"), lax.axis_index("col")
    here_x, here_z = row_at // 4, row_at % 4
    here_y, core = col_at // 2, col_at % 2
    sketch_table = sketch.reshape(BC, B, K)

    def send_core(value):
        return lax.ppermute(value, "col", PAIR)

    def send_y(value, shift):
        return lax.ppermute(value, "col", ring(shift))

    def send_x(value, shift):
        return lax.ppermute(value, "row", along_x(shift))

    def send_z(value, shift):
        return lax.ppermute(value, "row", along_z(shift))

    other_half, other_stat = partial_rows(
        rows, cols, jnp.stack([count, 1 - core, here_y]), blocks, sketch_table
    )
    from_pair = send_core(other_half)
    own_half, own_stat = partial_rows(
        rows, cols, jnp.stack([count, core, here_y]), blocks, sketch_table
    )
    stat = jnp.maximum(other_stat, own_stat)
    block_max = jnp.max(stat[1])
    bound = jnp.full((8, K), jnp.max(stat[0]))
    bound = jnp.maximum(bound, send_core(bound))
    bound = jnp.maximum(
        jnp.maximum(bound, send_y(bound, 2)), jnp.maximum(send_y(bound, 1), send_y(bound, -1))
    )
    y_scale = scale_for(bound[0, 0] * 8.0)

    own_part = own_half.reshape(4, 2, 8 * B, K)
    pair_part = from_pair.reshape(4, 2, 8 * B, K)
    pieces = [tuple(own_part[r, h] + pair_part[r, h] for h in range(2)) for r in range(4)]
    y_first, y_second = ring_sum(pieces, send_y, y_scale)

    mine = [((v / y_scale).astype(f16)) for v in (y_first, y_second)]
    below = [send_y(mine[0], 1), None]
    above = [None, send_y(mine[1], -1)]
    below[1] = send_y(mine[1], 1)
    above[0] = send_y(mine[0], -1)
    across = [send_y(below[0], 1), send_y(above[1], -1)]
    own_core = [mine, above, across, below]
    pair_core = [[send_core(v) for v in part] for part in own_core]
    tables = [
        (v.astype(f32) * y_scale).reshape(8, B, K)
        for side in (own_core, pair_core)
        for part in side
        for v in part
    ]

    y_share = jnp.concatenate([y_first, y_second], axis=0)
    gram = jnp.dot(y_share.T, y_share, precision=highest, preferred_element_type=f32)
    y_max = jnp.max(jnp.abs(y_share))
    limits = jnp.concatenate([jnp.full((8, K), y_max), jnp.full((8, K), block_max)], axis=0)
    for axis, perm in (
        ("col", PAIR),
        ("col", [(c, c ^ 2) for c in range(8)]),
        ("col", [(c, c ^ 4) for c in range(8)]),
        ("row", [(r, r ^ 1) for r in range(16)]),
        ("row", [(r, r ^ 2) for r in range(16)]),
        ("row", [(r, r ^ 4) for r in range(16)]),
        ("row", [(r, r ^ 8) for r in range(16)]),
    ):
        got = lax.ppermute(jnp.concatenate([gram, limits], axis=0), axis, perm)
        gram = gram + got[:K]
        limits = jnp.maximum(limits, got[K:])
    z_scale = scale_for(limits[0, 0] * limits[8, 0] * (16.0 * NBLK * B))

    info = jnp.stack([count, core, here_y, here_x, here_z])
    half_a = partial_cols(0, rows, cols, info, blocks, tables)
    half_b = partial_cols(1, rows, cols, info, blocks, tables)

    def two_stage(partial, send_one, send_two):
        parts = partial.reshape(4, 2, 2, 4 * B, K)
        firsts = ring_sum(
            [tuple(parts[r, h].reshape(2 * 4 * B, K) for h in range(2)) for r in range(4)],
            send_one,
            z_scale,
        )
        firsts = [v.reshape(2, 2, 2 * B, K) for v in firsts]
        return ring_sum(
            [tuple(firsts[r // 2][r % 2, h] for h in range(2)) for r in range(4)], send_two, z_scale
        )

    z_a = two_stage(half_a, send_x, send_z)
    z_b = two_stage(half_b, send_z, send_x)

    lower_factor = jnp.linalg.cholesky(gram)
    inverse = lax.linalg.triangular_solve(
        lower_factor, jnp.eye(K, dtype=f32), left_side=True, lower=True
    )
    q_share = jnp.dot(y_share, inverse.T, precision=highest, preferred_element_type=f32)
    z_raw = jnp.concatenate([*z_a, *z_b], axis=0)
    z_share = jnp.dot(z_raw, inverse.T, precision=highest, preferred_element_type=f32)
    row_scale = math.sqrt(BR * B * lax.axis_size("row"))
    return (q_share * row_scale, z_share[None])


def solution(mesh):
    in_specs = (
        P("row", "col", None, None, None),
        P("col", None),
        P("row", "col", None),
        P("row", "col", None),
        P("row", "col"),
    )
    out_specs = (P(("row", "col"), None), P("col", "row", None))
    return jax.shard_map(body, mesh=mesh, in_specs=in_specs, out_specs=out_specs, check_vma=False)
```

```python
import math

import jax
import jax.numpy as jnp
from jax import lax
from jax.experimental import pallas as pl
from jax.experimental.pallas import tpu as pltpu
from jax.sharding import PartitionSpec as P

B = 256
K = 128
BR = 128
BC = 128
NBLK = 96
CHUNK = 8
AHEAD = 24
GROUP = 4
VMEM_BYTES = 56 * 1024 * 1024
f32 = jnp.float32
f16 = jnp.float16


def ring(shift):
    return [(c, ((c // 2 + shift) % 4) * 2 + c % 2) for c in range(8)]


def along_x(shift):
    return [(r, ((r // 4 + shift) % 4) * 4 + r % 4) for r in range(16)]


def along_z(shift):
    return [(r, (r // 4) * 4 + (r % 4 + shift) % 4) for r in range(16)]


PAIR = [(c, c ^ 1) for c in range(8)]


def in_groups(start, stop, group, carry):
    groups = (stop - start) // GROUP
    carry = lax.fori_loop(0, groups, lambda g, c: group(start + g * GROUP, GROUP, c), carry)
    return lax.fori_loop(start + groups * GROUP, stop, lambda j, c: group(j, 1, c), carry)


def sort_slots(count, target_of, order, targets):
    order[0] = 0

    def pick(low, high):
        def one(s, n):
            target = target_of(s)
            order[n] = s
            targets[n] = target
            return n + jnp.where((target >= low) & (target < high), 1, 0)

        return one

    split = lax.fori_loop(0, count, pick(0, 4 * CHUNK), 0)
    total = lax.fori_loop(0, count, pick(4 * CHUNK, 8 * CHUNK), split)
    return split, total


def run_slots(split, total, begin, group, carry, total_sum, outs, out_sems):
    lax.fori_loop(0, jnp.minimum(total, AHEAD), begin, 0)

    def clear(t, _):
        total_sum[t] = jnp.zeros((B, K), f32)
        return 0

    lax.fori_loop(0, 8 * CHUNK, clear, 0)
    written = [
        pltpu.make_async_copy(total_sum.at[pl.ds(i * 4 * CHUNK, 4 * CHUNK)], outs[i], out_sems.at[i])
        for i in range(2)
    ]
    carry = in_groups(0, split, group, carry)
    written[0].start()
    carry = in_groups(split, total, group, carry)
    written[1].start()
    for copy in written:
        copy.wait()
    return carry


def y_kernel(
    rows, cols, info, blocks, sketch, first, second, stat, *scratch
):
    total_sum, order, targets, block_buf, sketch_buf, sems, out_sems = scratch
    count, core, here = info[0], info[1], info[2]

    def target_of(s):
        row = rows[s]
        chunk = info[8 + ((((row >> 5) - here) & 3) << 1) + ((row >> 3) & 1)]
        return jnp.where(((row >> 4) & 1) == core, chunk * CHUNK + (row & 7), -1)

    split, total = sort_slots(count, target_of, order, targets)

    def copies(j):
        s = order[j]
        return (
            pltpu.make_async_copy(blocks.at[s], block_buf.at[j], sems.at[0, j]),
            pltpu.make_async_copy(sketch.at[cols[s]], sketch_buf.at[j], sems.at[1, j]),
        )

    def begin(j, _):
        for copy in copies(j):
            copy.start()
        return 0

    def begin_later(j):
        @pl.when(j < total)
        def _():
            begin(j, 0)

    def group(at, size, carry):
        bound, largest = carry
        for u in range(size):
            begin_later(at + u + AHEAD)
        for u in range(size):
            for copy in copies(at + u):
                copy.wait()
        for u in range(size):
            tile = block_buf[at + u]
            target = targets[at + u]
            value = total_sum[target] + jnp.dot(
                tile, sketch_buf[at + u], preferred_element_type=f32
            )
            total_sum[target] = value
            bound = jnp.maximum(bound, jnp.max(jnp.abs(value).reshape(B // 8, 8, K), axis=0))
            largest = jnp.maximum(
                largest, jnp.max(jnp.abs(tile).reshape(B // 16, 16, B), axis=0)
            )
        return bound, largest

    bound, largest = run_slots(
        split,
        total,
        begin,
        group,
        (jnp.zeros((8, K), f32), jnp.zeros((16, B), jnp.bfloat16)),
        total_sum,
        (first, second),
        out_sems,
    )
    stat[0] = bound
    wide = largest.astype(f32)
    stat[1] = jnp.maximum(
        jnp.maximum(wide[:8, :K], wide[8:, :K]), jnp.maximum(wide[:8, K:], wide[8:, K:])
    )


HALF_SUMS = jax.ShapeDtypeStruct((4 * CHUNK, B, K), f32)


def scratch_for(y_type):
    return [
        pltpu.VMEM((8 * CHUNK, B, K), f32),
        pltpu.SMEM((NBLK + 1,), jnp.int32),
        pltpu.SMEM((NBLK + 1,), jnp.int32),
        pltpu.VMEM((NBLK, B, B), jnp.bfloat16),
        pltpu.VMEM((NBLK, B, K), y_type),
        pltpu.SemaphoreType.DMA((2, NBLK)),
        pltpu.SemaphoreType.DMA((2,)),
    ]


def partial_rows(rows, cols, info, blocks, sketch):
    return pl.pallas_call(
        y_kernel,
        out_shape=(HALF_SUMS, HALF_SUMS, jax.ShapeDtypeStruct((2, 8, K), f32)),
        in_specs=[pl.BlockSpec(memory_space=pltpu.SMEM)] * 3
        + [pl.BlockSpec(memory_space=pl.ANY)] * 2,
        out_specs=(
            pl.BlockSpec(memory_space=pl.ANY),
            pl.BlockSpec(memory_space=pl.ANY),
            pl.BlockSpec(memory_space=pltpu.VMEM),
        ),
        scratch_shapes=scratch_for(jnp.bfloat16),
        compiler_params=pltpu.CompilerParams(vmem_limit_bytes=VMEM_BYTES),
        cost_estimate=pl.CostEstimate(
            flops=NBLK * B * B * K, bytes_accessed=18 * 1024 * 1024, transcendentals=0
        ),
        name="partial_rows",
    )(rows, cols, info, blocks, sketch)


def z_kernel(half, rows, cols, info, blocks, *rest):
    tables, (first, second, *scratch) = rest[:10], rest[10:]
    total_sum, order, targets, block_buf, y_buf, sems, out_sems = scratch
    count, core, here_y, here_x, here_z = info[0], info[1], info[2], info[3], info[4]

    def target_of(s):
        col = cols[s]
        rel_x = ((col >> 5) - here_x) & 3
        rel_z = ((col >> 3) - here_z) & 3
        rel, other = (rel_x, rel_z) if half == 0 else (rel_z, rel_x)
        chunk = info[8 + (rel << 1) + ((col >> 1) & 1)]
        return jnp.where(((col >> 2) & 1) == half, chunk * CHUNK + (other << 1) + (col & 1), -1)

    split, total = sort_slots(count, target_of, order, targets)

    def block_copy(j):
        return pltpu.make_async_copy(blocks.at[order[j]], block_buf.at[j], sems.at[0, j])

    def y_copy(j, table, inner):
        return pltpu.make_async_copy(table.at[inner], y_buf.at[j], sems.at[1, j])

    def begin(j, _):
        block_copy(j).start()
        row = rows[order[j]]
        rel = ((row >> 5) - here_y) & 3
        same = ((row >> 4) & 1) == core

        for side, at in ((same, 0), (jnp.logical_not(same), 5)):

            @pl.when(side & (rel == 0))
            def _():
                y_copy(j, tables[at], row & 15).start()

            @pl.when(side & (rel == 1))
            def _():
                y_copy(j, tables[at + 1], row & 15).start()

            @pl.when(side & (rel == 3))
            def _():
                y_copy(j, tables[at + 2], row & 15).start()

            @pl.when(side & (rel == 2) & ((row & 8) == 0))
            def _():
                y_copy(j, tables[at + 3], row & 7).start()

            @pl.when(side & (rel == 2) & ((row & 8) != 0))
            def _():
                y_copy(j, tables[at + 4], row & 7).start()

        return 0

    def begin_later(j):
        @pl.when(j < total)
        def _():
            begin(j, 0)

    def group(at, size, _):
        for u in range(size):
            begin_later(at + u + AHEAD)
        for u in range(size):
            block_copy(at + u).wait()
            y_copy(at + u, tables[0], 0).wait()
        for u in range(size):
            value = y_buf[at + u]
            high = value.astype(jnp.bfloat16)
            low = (value - high.astype(f32)).astype(jnp.bfloat16)
            product = lax.dot_general(
                block_buf[at + u],
                jnp.concatenate([high, low], axis=1),
                (((0,), (0,)), ((), ())),
                preferred_element_type=f32,
            )
            total_sum[targets[at + u]] += product[:, :K] + product[:, K:]
        return 0

    run_slots(split, total, begin, group, 0, total_sum, (first, second), out_sems)


def partial_cols(half, rows, cols, info, blocks, tables):
    def kernel(*refs):
        z_kernel(half, *refs)

    return pl.pallas_call(
        kernel,
        out_shape=(HALF_SUMS, HALF_SUMS),
        in_specs=[pl.BlockSpec(memory_space=pltpu.SMEM)] * 3
        + [pl.BlockSpec(memory_space=pl.ANY)] * 11,
        out_specs=(pl.BlockSpec(memory_space=pl.ANY),) * 2,
        scratch_shapes=scratch_for(f32),
        compiler_params=pltpu.CompilerParams(vmem_limit_bytes=VMEM_BYTES),
        cost_estimate=pl.CostEstimate(
            flops=NBLK * B * B * K * 2, bytes_accessed=22 * 1024 * 1024, transcendentals=0
        ),
        name="partial_cols",
    )(rows, cols, info, blocks, *tables)


def scale_for(bound):
    return jnp.exp2(jnp.ceil(jnp.log2(jnp.maximum(bound, 1e-30))) - 15.0)


def pack(value, scale):
    return (value * (1.0 / scale)).astype(f16)


def unpack(value, scale):
    return value.astype(f32) * scale


PLACES = (6, 7, 4, 1, 0, 2, 3, 5)


def ring_sum(up, down, then_up, then_down, stay, send, scale, below=None, above=None, final=None):
    if final is None:
        below = above = final = scale
    from_below = send(pack(up, scale), 1)
    from_above = send(pack(down, scale), -1)
    sum_up = send(pack(then_up + unpack(from_below[0], below), final), 1)
    sum_down = send(pack(then_down + unpack(from_above[0], above), final), -1)
    from_below, from_above, sum_up, sum_down = lax.optimization_barrier(
        (from_below, from_above, sum_up, sum_down)
    )
    return (
        stay[0] + unpack(from_above[1], above) + unpack(sum_up, final),
        stay[1] + unpack(from_below[1], below) + unpack(sum_down, final),
    )


def ring_fold(value, send, op):
    across, below, above = send(value, 2), send(value, 1), send(value, -1)
    return op(op(value, across), op(below, above))


def body(blocks, sketch, block_row, block_col, counts):
    highest = lax.Precision.HIGHEST
    blocks = blocks[0, 0]
    rows, cols = block_row[0, 0], block_col[0, 0]
    count = counts[0, 0]
    row_at, col_at = lax.axis_index("row"), lax.axis_index("col")
    here_x, here_z = row_at // 4, row_at % 4
    here_y, core = col_at // 2, col_at % 2
    sketch_table = sketch.reshape(BC, B, K)

    def send_core(value):
        return lax.ppermute(value, "col", PAIR)

    def send_y(value, shift):
        return lax.ppermute(value, "col", ring(shift))

    def send_x(value, shift):
        return lax.ppermute(value, "row", along_x(shift))

    def send_z(value, shift):
        return lax.ppermute(value, "row", along_z(shift))

    def info(which):
        here = jnp.stack([count, which, here_y, here_x, here_z, 0, 0, 0])
        return jnp.concatenate([here, jnp.array(PLACES, jnp.int32)])

    other_first, other_second, other_stat = partial_rows(
        rows, cols, info(1 - core), blocks, sketch_table
    )
    pair_first, pair_second = send_core(other_first), send_core(other_second)
    own_first, own_second, own_stat = partial_rows(rows, cols, info(core), blocks, sketch_table)

    stat = jnp.maximum(other_stat, own_stat)
    block_max = jnp.max(stat[1])
    chip_bound = jnp.full((8, K), jnp.max(stat[0]))
    chip_bound = chip_bound + send_core(chip_bound)
    bounds = [chip_bound, send_y(chip_bound, 1), send_y(chip_bound, -1), send_y(chip_bound, 2)]
    y_bound = 4.0 * jnp.maximum(
        jnp.maximum(bounds[0], bounds[3]), jnp.maximum(bounds[1], bounds[2])
    )
    y_scale = scale_for(y_bound[0, 0])

    part = (4, CHUNK * B, K)
    own_first, pair_first = own_first.reshape(part), pair_first.reshape(part)
    own_second, pair_second = own_second.reshape(part), pair_second.reshape(part)
    y_first, y_second = ring_sum(
        own_first[:2] + pair_first[:2],
        own_first[2:] + pair_first[2:],
        own_second[0] + pair_second[0],
        own_second[1] + pair_second[1],
        [own_second[2] + pair_second[2], own_second[3] + pair_second[3]],
        send_y,
        *(scale_for(bound[0, 0]) for bound in bounds[:3]),
        y_scale,
    )

    y_share = jnp.concatenate([y_first, y_second], axis=0)
    mine = pack(y_share, y_scale)
    below, above = send_y(mine, 1), send_y(mine, -1)
    pair_mine = send_core(mine)
    across = [send_y(below[: CHUNK * B], 1), send_y(above[CHUNK * B :], -1)]
    own_core = [mine, above, below, *across]
    pair_core = [pair_mine] + [send_core(v) for v in own_core[1:]]
    tables = [unpack(v, y_scale).reshape(-1, B, K) for v in own_core + pair_core]

    y_gram, _ = lax.optimization_barrier((y_share, pair_mine))
    gram = jnp.dot(y_gram.T, y_gram, precision=highest, preferred_element_type=f32)
    live = jnp.arange(NBLK, dtype=jnp.int32) < count
    hits = (cols[:, None] == jnp.arange(BC, dtype=jnp.int32)[None, :]) & live[:, None]
    repeats = jnp.max(jnp.sum(hits.astype(f32), axis=0))
    both = jnp.concatenate([gram, y_bound * (repeats * block_max * float(B))], axis=0)

    def add_and_max(a, b):
        return jnp.concatenate([a[:K] + b[:K], jnp.maximum(a[K:], b[K:])], axis=0)

    both = ring_fold(ring_fold(both, send_x, add_and_max), send_z, add_and_max)
    gram = both[:K]
    z_scale = scale_for(both[K, 0] * 16.0)

    half_a = partial_cols(0, rows, cols, info(core), blocks, tables)
    gram, half_a = lax.optimization_barrier((gram, half_a))
    gram = gram + send_core(gram)
    gram = ring_fold(gram, send_y, jnp.add)
    half_b = partial_cols(1, rows, cols, info(core), blocks, tables)
    gram, half_b = lax.optimization_barrier((gram, half_b))

    def two_stage(partial, send_one, send_two):
        first, second = (v.reshape(4, CHUNK * B, K) for v in partial)
        a, b = ring_sum(
            first[:2], first[2:], second[0], second[1], second[2:], send_one, z_scale
        )
        a, b = a.reshape(4, 2 * B, K), b.reshape(4, 2 * B, K)
        return ring_sum(
            jnp.stack([a[2], b[1]]),
            jnp.stack([b[2], a[3]]),
            a[1],
            b[3],
            [a[0], b[0]],
            send_two,
            z_scale,
        )

    z_a = two_stage(half_a, send_x, send_z)
    z_b = two_stage(half_b, send_z, send_x)

    lower_factor = jnp.linalg.cholesky(gram)
    inverse = lax.linalg.triangular_solve(
        lower_factor, jnp.eye(K, dtype=f32), left_side=True, lower=True
    )
    q_share = jnp.dot(y_share, inverse.T, precision=highest, preferred_element_type=f32)
    z_raw = jnp.concatenate([*z_a, *z_b], axis=0)
    z_share = jnp.dot(z_raw, inverse.T, precision=highest, preferred_element_type=f32)
    row_scale = math.sqrt(BR * B * lax.axis_size("row"))
    return (q_share * row_scale, z_share[None])


def solution(mesh):
    in_specs = (
        P("row", "col", None, None, None),
        P("col", None),
        P("row", "col", None),
        P("row", "col", None),
        P("row", "col"),
    )
    out_specs = (P(("row", "col"), None), P("col", "row", None))
    return jax.shard_map(body, mesh=mesh, in_specs=in_specs, out_specs=out_specs, check_vma=False)
```

```python
import math

import jax
import jax.numpy as jnp
from jax import lax
from jax.experimental import pallas as pl
from jax.experimental.pallas import tpu as pltpu
from jax.sharding import PartitionSpec as P

B = 256
K = 128
BR = 128
BC = 128
NBLK = 96
CHUNK = 8
AHEAD = 24
GROUP = 4
VMEM_BYTES = 56 * 1024 * 1024
f32 = jnp.float32
f16 = jnp.float16


def ring(shift):
    return [(c, ((c // 2 + shift) % 4) * 2 + c % 2) for c in range(8)]


def along_x(shift):
    return [(r, ((r // 4 + shift) % 4) * 4 + r % 4) for r in range(16)]


def along_z(shift):
    return [(r, (r // 4) * 4 + (r % 4 + shift) % 4) for r in range(16)]


PAIR = [(c, c ^ 1) for c in range(8)]


def in_groups(start, stop, group, carry):
    groups = (stop - start) // GROUP
    carry = lax.fori_loop(0, groups, lambda g, c: group(start + g * GROUP, GROUP, c), carry)
    return lax.fori_loop(start + groups * GROUP, stop, lambda j, c: group(j, 1, c), carry)


def run_slots(count, targets, order, begin, group, carry, total_sum, outs, out_sems):
    size = 4 * CHUNK
    order[0] = 0

    def pick(part):
        def one(s, n):
            order[n] = s
            target = targets[s]
            return n + jnp.where((target >= part * size) & (target < (part + 1) * size), 1, 0)

        return one

    ends = [0]
    for part in range(len(outs)):
        ends.append(lax.fori_loop(0, count, pick(part), ends[-1]))
    total = ends[-1]

    def begin_later(j):
        @pl.when(j < total)
        def _():
            begin(j, 0)

    lax.fori_loop(0, jnp.minimum(total, AHEAD), begin, 0)

    def clear(t, _):
        total_sum[t] = jnp.zeros((B, K), f32)
        return 0

    lax.fori_loop(0, len(outs) * size, clear, 0)
    written = []
    for part, out in enumerate(outs):
        carry = in_groups(
            ends[part], ends[part + 1], lambda at, n, c: group(begin_later, at, n, c), carry
        )
        written.append(
            pltpu.make_async_copy(
                total_sum.at[pl.ds(part * size, size)], out, out_sems.at[part]
            )
        )
        written[-1].start()
    for copy in written:
        copy.wait()
    return carry


def y_kernel(count, targets, cols, blocks, sketch, first, second, stat, *scratch):
    total_sum, order, block_buf, sketch_buf, sems, out_sems = scratch

    def copies(j):
        s = order[j]
        return (
            pltpu.make_async_copy(blocks.at[s], block_buf.at[j], sems.at[0, j]),
            pltpu.make_async_copy(sketch.at[cols[s]], sketch_buf.at[j], sems.at[1, j]),
        )

    def begin(j, _):
        for copy in copies(j):
            copy.start()
        return 0

    def group(begin_later, at, size, carry):
        bound, largest = carry
        for u in range(size):
            begin_later(at + u + AHEAD)
        for u in range(size):
            for copy in copies(at + u):
                copy.wait()
        for u in range(size):
            tile = block_buf[at + u]
            target = targets[order[at + u]]
            value = total_sum[target] + jnp.dot(
                tile, sketch_buf[at + u], preferred_element_type=f32
            )
            total_sum[target] = value
            bound = jnp.maximum(bound, jnp.max(jnp.abs(value).reshape(B // 8, 8, K), axis=0))
            largest = jnp.maximum(
                largest, jnp.max(jnp.abs(tile).reshape(B // 16, 16, B), axis=0)
            )
        return bound, largest

    bound, largest = run_slots(
        count[0],
        targets,
        order,
        begin,
        group,
        (jnp.zeros((8, K), f32), jnp.zeros((16, B), jnp.bfloat16)),
        total_sum,
        (first, second),
        out_sems,
    )
    stat[0] = bound
    wide = largest.astype(f32)
    stat[1] = jnp.maximum(
        jnp.maximum(wide[:8, :K], wide[8:, :K]), jnp.maximum(wide[:8, K:], wide[8:, K:])
    )


HALF_SUMS = jax.ShapeDtypeStruct((4 * CHUNK, B, K), f32)


def scratch_for(outs, y_type):
    return [
        pltpu.VMEM((outs * 4 * CHUNK, B, K), f32),
        pltpu.SMEM((NBLK + 1,), jnp.int32),
        pltpu.VMEM((NBLK, B, B), jnp.bfloat16),
        pltpu.VMEM((NBLK, B, K), y_type),
        pltpu.SemaphoreType.DMA((2, NBLK)),
        pltpu.SemaphoreType.DMA((outs,)),
    ]


def partial_rows(count, targets, cols, blocks, sketch):
    return pl.pallas_call(
        y_kernel,
        out_shape=(HALF_SUMS, HALF_SUMS, jax.ShapeDtypeStruct((2, 8, K), f32)),
        in_specs=[pl.BlockSpec(memory_space=pltpu.SMEM)] * 3
        + [pl.BlockSpec(memory_space=pl.ANY)] * 2,
        out_specs=(
            pl.BlockSpec(memory_space=pl.ANY),
            pl.BlockSpec(memory_space=pl.ANY),
            pl.BlockSpec(memory_space=pltpu.VMEM),
        ),
        scratch_shapes=scratch_for(2, jnp.bfloat16),
        compiler_params=pltpu.CompilerParams(vmem_limit_bytes=VMEM_BYTES),
        cost_estimate=pl.CostEstimate(
            flops=NBLK * B * B * K, bytes_accessed=18 * 1024 * 1024, transcendentals=0
        ),
        name="partial_rows",
    )(count, targets, cols, blocks, sketch)


def z_kernel(count, targets, rows, blocks, table, *rest):
    outs, (total_sum, order, block_buf, y_buf, sems, out_sems) = rest[:4], rest[4:]

    def copies(j):
        s = order[j]
        return (
            pltpu.make_async_copy(blocks.at[s], block_buf.at[j], sems.at[0, j]),
            pltpu.make_async_copy(table.at[rows[s]], y_buf.at[j], sems.at[1, j]),
        )

    def begin(j, _):
        for copy in copies(j):
            copy.start()
        return 0

    def group(begin_later, at, size, _):
        for u in range(size):
            begin_later(at + u + AHEAD)
        for u in range(size):
            for copy in copies(at + u):
                copy.wait()
        for u in range(size):
            value = y_buf[at + u]
            high = value.astype(jnp.bfloat16)
            low = (value - high.astype(f32)).astype(jnp.bfloat16)
            product = lax.dot_general(
                block_buf[at + u],
                jnp.concatenate([high, low], axis=1),
                (((0,), (0,)), ((), ())),
                preferred_element_type=f32,
            )
            total_sum[targets[order[at + u]]] += product[:, :K] + product[:, K:]
        return 0

    run_slots(count[0], targets, order, begin, group, 0, total_sum, outs, out_sems)


def partial_cols(count, targets, rows, blocks, table):
    return pl.pallas_call(
        z_kernel,
        out_shape=(HALF_SUMS,) * 4,
        in_specs=[pl.BlockSpec(memory_space=pltpu.SMEM)] * 3
        + [pl.BlockSpec(memory_space=pl.ANY)] * 2,
        out_specs=(pl.BlockSpec(memory_space=pl.ANY),) * 4,
        scratch_shapes=scratch_for(4, f32),
        compiler_params=pltpu.CompilerParams(vmem_limit_bytes=VMEM_BYTES),
        cost_estimate=pl.CostEstimate(
            flops=NBLK * B * B * K * 4, bytes_accessed=42 * 1024 * 1024, transcendentals=0
        ),
        name="partial_cols",
    )(count, targets, rows, blocks, table)


def scale_for(bound):
    return jnp.exp2(jnp.ceil(jnp.log2(jnp.maximum(bound, 1e-30))) - 15.0)


def pack(value, scale):
    return (value * (1.0 / scale)).astype(f16)


def unpack(value, scale):
    return value.astype(f32) * scale


PLACES = (6, 7, 4, 1, 0, 2, 3, 5)


def ring_sum(up, down, later, send, scale, below=None, above=None, final=None):
    if final is None:
        below = above = final = scale
    from_below = send(up, 1)
    from_above = send(down, -1)
    sum_up = send(pack(later[0] + unpack(from_below[0], below), final), 1)
    sum_down = send(pack(later[1] + unpack(from_above[0], above), final), -1)
    from_below, from_above, sum_up, sum_down = lax.optimization_barrier(
        (from_below, from_above, sum_up, sum_down)
    )

    def total(half, start=0, stop=CHUNK * B):
        direct, direct_scale, summed = (
            (from_above[1], above, sum_up) if half == 0 else (from_below[1], below, sum_down)
        )
        return (
            later[2 + half][start:stop]
            + unpack(direct[start:stop], direct_scale)
            + unpack(summed[start:stop], final)
        )

    return total


def ring_exchange(parts, send, scale):
    up, down, across = (send(pack(parts[r], scale), r) for r in (1, 3, 2))
    return parts[0] + unpack(up, scale) + unpack(down, scale) + unpack(across, scale)


def ring_fold(value, send, op):
    across, below, above = send(value, 2), send(value, 1), send(value, -1)
    return op(op(value, across), op(below, above))


def body(blocks, sketch, block_row, block_col, counts):
    highest = lax.Precision.HIGHEST
    blocks = blocks[0, 0]
    rows, cols = block_row[0, 0], block_col[0, 0]
    count = counts[0, 0]
    row_at, col_at = lax.axis_index("row"), lax.axis_index("col")
    here_x, here_z = row_at // 4, row_at % 4
    here_y, core = col_at // 2, col_at % 2
    sketch_table = sketch.reshape(BC, B, K)

    def send_core(value):
        return lax.ppermute(value, "col", PAIR)

    def send_y(value, shift):
        return lax.ppermute(value, "col", ring(shift))

    def send_x(value, shift):
        return lax.ppermute(value, "row", along_x(shift))

    def send_z(value, shift):
        return lax.ppermute(value, "row", along_z(shift))

    live = jnp.arange(NBLK, dtype=jnp.int32) < count
    places = jnp.array(PLACES, jnp.int32)

    def chunk_of(rel, half):
        key = (rel & 3) * 2 + half
        return jnp.sum(jnp.where(key[:, None] == jnp.arange(8), places[None, :], 0), axis=1) * CHUNK

    y_target = chunk_of((rows >> 5) - here_y, (rows >> 3) & 1) + (rows & 7)
    row_core = (rows >> 4) & 1
    rel_x, rel_z = ((cols >> 5) - here_x) & 3, ((cols >> 3) - here_z) & 3
    col_half, col_pair = (cols >> 2) & 1, (cols >> 1) & 1
    a_target = chunk_of(rel_x, col_pair) + rel_z * 2 + (cols & 1)
    b_target = chunk_of(rel_z, col_pair) + rel_x * 2 + (cols & 1)
    other_target = jnp.where(live & (row_core != core), y_target, -1)
    own_target = jnp.where(live & (row_core == core), y_target, -1)
    z_target = jnp.where(col_half == 0, a_target, b_target + 8 * CHUNK)
    z_target = jnp.where(live, z_target, -1)
    count = count[None]

    other_first, other_second, other_stat = partial_rows(
        count, other_target, cols, blocks, sketch_table
    )
    pair_first, pair_second = send_core(other_first), send_core(other_second)
    own_first, own_second, own_stat = partial_rows(count, own_target, cols, blocks, sketch_table)

    stat = jnp.maximum(other_stat, own_stat)
    block_max = jnp.max(stat[1])
    chip_bound = jnp.full((8, K), jnp.max(stat[0]))
    chip_bound = chip_bound + send_core(chip_bound)
    bounds = [chip_bound, send_y(chip_bound, 1), send_y(chip_bound, -1), send_y(chip_bound, 2)]
    y_bound = 4.0 * jnp.maximum(
        jnp.maximum(bounds[0], bounds[3]), jnp.maximum(bounds[1], bounds[2])
    )
    y_scale = scale_for(y_bound[0, 0])
    y_scales = [scale_for(bound[0, 0]) for bound in bounds[:3]] + [y_scale]

    part = (4, CHUNK * B, K)
    first = (own_first + pair_first).reshape(part)
    up, down, y_bound, *y_scales = lax.optimization_barrier(
        (pack(first[:2], y_scales[0]), pack(first[2:], y_scales[0]), y_bound, *y_scales)
    )
    y_scale = y_scales[3]
    later = lax.optimization_barrier((own_second + pair_second).reshape(part))
    y_part = ring_sum(up, down, later, send_y, *y_scales)

    y_share = jnp.concatenate([y_part(0), y_part(1)], axis=0)
    mine = pack(y_share, y_scale)
    gram = jnp.dot(
        y_share.T, y_share, precision=lax.Precision.HIGH, preferred_element_type=f32
    )
    hits = (cols[:, None] == jnp.arange(BC, dtype=jnp.int32)[None, :]) & live[:, None]
    repeats = jnp.max(jnp.sum(hits.astype(f32), axis=0))
    both = jnp.concatenate([gram, y_bound * (repeats * block_max * float(B))], axis=0)

    def add_and_max(a, b):
        return jnp.concatenate([a[:K] + b[:K], jnp.maximum(a[K:], b[K:])], axis=0)

    mine, both = lax.optimization_barrier((mine, both))
    gathered = lax.all_gather(mine, "col", axis=0, tiled=True)
    both = ring_fold(both, send_x, add_and_max)
    both, gathered = lax.optimization_barrier((both, gathered))
    table = unpack(gathered, y_scale).reshape(BR, B, K)
    both = ring_fold(both, send_z, add_and_max)
    gram, limit = both[:K], both[K, 0]
    z_scale = scale_for(limit * 16.0)

    gram, z_scale, table = lax.optimization_barrier((gram, z_scale, table))
    def two_stage(up, down, later, send_one, send_two):
        total = ring_sum(up, down, later, send_one, z_scale)
        parts = [
            jnp.concatenate([total(h, r * 2 * B, (r + 1) * 2 * B) for h in range(2)], axis=0)
            for r in range(4)
        ]
        return ring_exchange(parts, send_two, z_scale)

    gram = gram + send_core(gram)
    partial = partial_cols(count, z_target, rows, blocks, table)
    a_first, a_second, b_first, b_second = (v.reshape(part) for v in partial)
    sends = [pack(v, z_scale) for v in (a_first[:2], a_first[2:], b_first[:2], b_first[2:])]
    gram, *sends = lax.optimization_barrier((gram, *sends))
    gram = ring_fold(gram, send_y, jnp.add)
    z_a = two_stage(*sends[:2], a_second, send_x, send_z)
    z_b = two_stage(*sends[2:], b_second, send_z, send_x)

    lower_factor = jnp.linalg.cholesky(gram)
    inverse = lax.linalg.triangular_solve(
        lower_factor, jnp.eye(K, dtype=f32), left_side=True, lower=True
    )
    q_share = jnp.dot(y_share, inverse.T, precision=highest, preferred_element_type=f32)
    z_raw = jnp.concatenate([z_a, z_b], axis=0)
    z_share = jnp.dot(z_raw, inverse.T, precision=highest, preferred_element_type=f32)
    row_scale = math.sqrt(BR * B * lax.axis_size("row"))
    return (q_share * row_scale, z_share[None])


def solution(mesh):
    in_specs = (
        P("row", "col", None, None, None),
        P("col", None),
        P("row", "col", None),
        P("row", "col", None),
        P("row", "col"),
    )
    out_specs = (P(("row", "col"), None), P("col", "row", None))
    return jax.shard_map(body, mesh=mesh, in_specs=in_specs, out_specs=out_specs, check_vma=False)
```

```python
import math

import jax
import jax.numpy as jnp
from jax import lax
from jax.experimental import pallas as pl
from jax.experimental.pallas import tpu as pltpu
from jax.sharding import PartitionSpec as P

B = 256
K = 128
BR = 128
BC = 128
NBLK = 96
CHUNK = 8
AHEAD = 24
GROUP = 4
VMEM_BYTES = 56 * 1024 * 1024
f32 = jnp.float32
f16 = jnp.float16


def ring(shift):
    return [(c, ((c // 2 + shift) % 4) * 2 + c % 2) for c in range(8)]


def along_x(shift):
    return [(r, ((r // 4 + shift) % 4) * 4 + r % 4) for r in range(16)]


def along_z(shift):
    return [(r, (r // 4) * 4 + (r % 4 + shift) % 4) for r in range(16)]


PAIR = [(c, c ^ 1) for c in range(8)]


def in_groups(start, stop, group, carry):
    groups = (stop - start) // GROUP
    carry = lax.fori_loop(0, groups, lambda g, c: group(start + g * GROUP, GROUP, c), carry)
    return lax.fori_loop(start + groups * GROUP, stop, lambda j, c: group(j, 1, c), carry)


def run_slots(chunks, count, targets, order, begin, group, carry, total_sum, outs, out_sems):
    halves = len(outs) // len(chunks)
    size = 4 * CHUNK
    order[0] = 0

    def pick(part):
        def one(s, n):
            order[n] = s
            target = targets[s]
            return n + jnp.where((target >= part * size) & (target < (part + 1) * size), 1, 0)

        return one

    ends = [0]
    for part in range(2 * halves):
        ends.append(lax.fori_loop(0, count, pick(part), ends[-1]))
    total = ends[-1]

    def begin_later(j):
        @pl.when(j < total)
        def _():
            begin(j, 0)

    lax.fori_loop(0, jnp.minimum(total, AHEAD), begin, 0)

    def clear(t, _):
        total_sum[t] = jnp.zeros((B, K), f32)
        return 0

    lax.fori_loop(0, 2 * halves * size, clear, 0)
    written = []

    for part in range(2 * halves):
        carry = in_groups(
            ends[part], ends[part + 1], lambda at, n, c: group(begin_later, at, n, c), carry
        )
        start = part // 2 * 2 * size
        for i, n in enumerate(chunks):
            if part * size <= start < (part + 1) * size:
                at = part // 2 * len(chunks) + i
                copy = pltpu.make_async_copy(
                    total_sum.at[pl.ds(start, n * CHUNK)], outs[at], out_sems.at[at]
                )
                copy.start()
                written.append(copy)
            start += n * CHUNK
    for copy in written:
        copy.wait()
    return carry


def y_kernel(count, targets, cols, blocks, sketch, *rest):
    outs, stat, scratch = rest[:3], rest[3], rest[4:]
    total_sum, order, block_buf, sketch_buf, sems, out_sems = scratch

    def copies(j):
        s = order[j]
        return (
            pltpu.make_async_copy(blocks.at[s], block_buf.at[j], sems.at[0, j]),
            pltpu.make_async_copy(sketch.at[cols[s]], sketch_buf.at[j], sems.at[1, j]),
        )

    def begin(j, _):
        for copy in copies(j):
            copy.start()
        return 0

    def group(begin_later, at, size, carry):
        largest, largest_block = carry
        for u in range(size):
            begin_later(at + u + AHEAD)
        for u in range(size):
            for copy in copies(at + u):
                copy.wait()
        for u in range(size):
            target = targets[order[at + u]]
            tile = block_buf[at + u]
            value = total_sum[target] + jnp.dot(
                tile, sketch_buf[at + u], preferred_element_type=f32
            )
            total_sum[target] = value
            largest = jnp.maximum(largest, jnp.max(jnp.abs(value).reshape(B // 8, 8, K), axis=0))
            largest_block = jnp.maximum(
                largest_block, jnp.max(jnp.abs(tile).reshape(B // 16, 16, B), axis=0)
            )
        return largest, largest_block

    carry = jnp.zeros((8, K), f32), jnp.zeros((16, B), jnp.bfloat16)
    largest, largest_block = run_slots(
        Y_CHUNKS, count[0], targets, order, begin, group, carry, total_sum, outs, out_sems
    )
    stat[:4] = jnp.full((4, K), jnp.max(largest))
    stat[4:] = jnp.full((4, K), jnp.max(largest_block.astype(f32)))


Y_CHUNKS = (4, 2, 2)
Z_CHUNKS = (2, 2, 1, 1, 1, 1)


def sums_of(chunks):
    return tuple(jax.ShapeDtypeStruct((n * CHUNK, B, K), f32) for n in chunks)


def scratch_for(halves, chunks, y_type):
    return [
        pltpu.VMEM((halves * 8 * CHUNK, B, K), f32),
        pltpu.SMEM((NBLK + 1,), jnp.int32),
        pltpu.VMEM((NBLK, B, B), jnp.bfloat16),
        pltpu.VMEM((NBLK, B, K), y_type),
        pltpu.SemaphoreType.DMA((2, NBLK)),
        pltpu.SemaphoreType.DMA((halves * len(chunks),)),
    ]


def partial_rows(count, targets, cols, blocks, sketch):
    return pl.pallas_call(
        y_kernel,
        out_shape=sums_of(Y_CHUNKS) + (jax.ShapeDtypeStruct((8, K), f32),),
        in_specs=[pl.BlockSpec(memory_space=pltpu.SMEM)] * 3
        + [pl.BlockSpec(memory_space=pl.ANY)] * 2,
        out_specs=(pl.BlockSpec(memory_space=pl.ANY),) * 3
        + (pl.BlockSpec(memory_space=pltpu.VMEM),),
        scratch_shapes=scratch_for(1, Y_CHUNKS, jnp.bfloat16),
        compiler_params=pltpu.CompilerParams(vmem_limit_bytes=VMEM_BYTES),
        cost_estimate=pl.CostEstimate(
            flops=NBLK * B * B * K, bytes_accessed=60 * 1024 * 1024, transcendentals=0
        ),
        name="partial_rows",
    )(count, targets, cols, blocks, sketch)


def z_kernel(count, targets, rows, blocks, table, *rest):
    outs, scratch = rest[:12], rest[12:]
    total_sum, order, block_buf, y_buf, sems, out_sems = scratch

    def copies(j):
        s = order[j]
        return (
            pltpu.make_async_copy(blocks.at[s], block_buf.at[j], sems.at[0, j]),
            pltpu.make_async_copy(table.at[rows[s]], y_buf.at[j], sems.at[1, j]),
        )

    def begin(j, _):
        for copy in copies(j):
            copy.start()
        return 0

    def group(begin_later, at, size, carry):
        for u in range(size):
            begin_later(at + u + AHEAD)
        for u in range(size):
            for copy in copies(at + u):
                copy.wait()
        for u in range(size):
            value = y_buf[at + u]
            high = value.astype(jnp.bfloat16)
            low = (value - high.astype(f32)).astype(jnp.bfloat16)
            product = lax.dot_general(
                block_buf[at + u],
                jnp.concatenate([high, low], axis=1),
                (((0,), (0,)), ((), ())),
                preferred_element_type=f32,
            )
            total_sum[targets[order[at + u]]] += product[:, :K] + product[:, K:]
        return carry

    run_slots(Z_CHUNKS, count[0], targets, order, begin, group, 0, total_sum, outs, out_sems)


def partial_cols(count, targets, rows, blocks, table):
    return pl.pallas_call(
        z_kernel,
        out_shape=sums_of(Z_CHUNKS * 2),
        in_specs=[pl.BlockSpec(memory_space=pltpu.SMEM)] * 3
        + [pl.BlockSpec(memory_space=pl.ANY)] * 2,
        out_specs=(pl.BlockSpec(memory_space=pl.ANY),) * 12,
        scratch_shapes=scratch_for(2, Z_CHUNKS, f32),
        compiler_params=pltpu.CompilerParams(vmem_limit_bytes=VMEM_BYTES),
        cost_estimate=pl.CostEstimate(
            flops=NBLK * B * B * K * 4, bytes_accessed=42 * 1024 * 1024, transcendentals=0
        ),
        name="partial_cols",
    )(count, targets, rows, blocks, table)


def scales_for(bound):
    exponent = jnp.ceil(jnp.log2(jnp.maximum(bound, 1e-30))) - 15.0
    return lax.optimization_barrier((jnp.exp2(exponent), jnp.exp2(-exponent)))


def pack(value, scales):
    return (value * scales[1]).astype(f16)


def unpack(message, scales):
    return message.astype(f32) * scales[0]


PLACES = (6, 7, 4, 1, 0, 2, 3, 5)


HALF = CHUNK * B


def ring_first(messages, send):
    return lax.optimization_barrier((send(messages[0], 1), send(messages[1], -1)))


def ring_second(received, passing, send, scales, below, above):
    messages = lax.optimization_barrier(
        (
            pack(passing[0] + unpack(received[0][:HALF], below), scales),
            pack(passing[1] + unpack(received[1][:HALF], above), scales),
        )
    )
    sums = send(messages[0], 1), send(messages[1], -1)
    return lax.optimization_barrier((received, sums, messages))


def ring_total(received, sums, staying, scales, below, above):
    def total(which, start=0, stop=HALF):
        direct = received[1 - which][HALF + start : HALF + stop]
        return (
            staying[which][start:stop]
            + unpack(direct, below if which else above)
            + unpack(sums[which][start:stop], scales)
        )

    return total


def ring_exchange(parts, send, scales):
    messages = lax.optimization_barrier([pack(parts[r], scales) for r in (1, 3, 2)])
    up, down, across = (unpack(send(m, r), scales) for m, r in zip(messages, (1, 3, 2)))
    return parts[0] + up + down + across, messages


def ring_fold(value, send, op):
    across, below, above = send(value, 2), send(value, 1), send(value, -1)
    return op(op(value, across), op(below, above)), below, above


def body(blocks, sketch, block_row, block_col, counts):
    highest = lax.Precision.HIGHEST
    blocks = blocks[0, 0]
    rows, cols = block_row[0, 0], block_col[0, 0]
    count = counts[0, 0]
    row_at, col_at = lax.axis_index("row"), lax.axis_index("col")
    here_x, here_z = row_at // 4, row_at % 4
    here_y, core = col_at // 2, col_at % 2
    sketch_table = sketch.reshape(BC, B, K)

    def send_core(value):
        return lax.ppermute(value, "col", PAIR)

    def send_y(value, shift):
        return lax.ppermute(value, "col", ring(shift))

    def send_x(value, shift):
        return lax.ppermute(value, "row", along_x(shift))

    def send_z(value, shift):
        return lax.ppermute(value, "row", along_z(shift))

    live = jnp.arange(NBLK, dtype=jnp.int32) < count

    def chunk_of(rel, half):
        key = (rel & 3) * 2 + half
        chunk = PLACES[7]
        for k in range(7):
            chunk = jnp.where(key == k, PLACES[k], chunk)
        return chunk * CHUNK

    y_target = chunk_of((rows >> 5) - here_y, (rows >> 3) & 1) + (rows & 7)
    row_core = (rows >> 4) & 1
    rel_x, rel_z = ((cols >> 5) - here_x) & 3, ((cols >> 3) - here_z) & 3
    col_half, col_pair = (cols >> 2) & 1, (cols >> 1) & 1
    a_target = chunk_of(rel_x, col_pair) + rel_z * 2 + (cols & 1)
    b_target = chunk_of(rel_z, col_pair) + rel_x * 2 + (cols & 1)
    other_target = jnp.where(live & (row_core != core), y_target, -1)
    own_target = jnp.where(live & (row_core == core), y_target, -1)
    z_target = jnp.where(live, jnp.where(col_half == 0, a_target, b_target + 8 * CHUNK), -1)
    count = count[None]

    def flat(values):
        return [v.reshape(-1, K) for v in values]

    *other, other_stat = partial_rows(count, other_target, cols, blocks, sketch_table)
    *from_pair, pair_stat = [send_core(v) for v in (*other, other_stat)]
    *own, own_stat = partial_rows(count, own_target, cols, blocks, sketch_table)
    own, from_pair = flat(own), flat(from_pair)

    first_bound = own_stat + pair_stat
    scales = scales_for(first_bound[:1])
    first = lax.optimization_barrier(
        tuple(
            pack(own[0][at : at + 2 * HALF] + from_pair[0][at : at + 2 * HALF], scales)
            for at in (0, 2 * HALF)
        )
    )
    received = [send_y(first[0], 1), send_y(first[1], -1)]
    in_first = lax.broadcasted_iota(jnp.int32, (8, K), 0) < 4
    entries = jnp.maximum(own_stat, other_stat) * count[0].astype(f32)
    bounds, _ = lax.optimization_barrier((jnp.where(in_first, first_bound, entries), first))
    bounds, below, above = ring_fold(bounds, send_y, jnp.maximum)
    later, _ = lax.optimization_barrier(((own[1:], from_pair[1:]), bounds))
    parts = [
        [mine[at : at + HALF] + pair[at : at + HALF] for at in (0, HALF)] for mine, pair in zip(*later)
    ]
    passing, staying = lax.optimization_barrier(parts)
    around = scales_for(below[:1]), scales_for(above[:1])
    sum_scales = scales_for(bounds[:1] * 4.0)
    received, sums, messages = ring_second(received, passing, send_y, sum_scales, *around)
    y_part = ring_total(received, sums, staying, sum_scales, *around)
    y_share = jnp.concatenate([y_part(0), y_part(1)], axis=0)

    bounds, _ = lax.optimization_barrier((bounds, messages))
    bounds = jnp.maximum(bounds, send_core(bounds))
    y_scales = scales_for(bounds[:1] * 4.0)
    bounds = ring_fold(ring_fold(bounds, send_x, jnp.maximum)[0], send_z, jnp.maximum)[0]
    z_scales = scales_for(bounds[:1] * bounds[4:5] * (4.0 * 16.0 * B))

    mine, z_scales = lax.optimization_barrier((pack(y_share, y_scales), z_scales))
    gathered = lax.all_gather(mine, "col", axis=0, tiled=True)
    table = unpack(gathered, y_scales).reshape(BR, B, K)

    gram = jnp.dot(
        y_share.T, y_share, precision=lax.Precision.HIGH, preferred_element_type=f32
    )
    gram = lax.psum(gram, "row")

    partial = flat(partial_cols(count, z_target, rows, blocks, table))
    rings = [(partial[:6], send_x, send_z), (partial[6:], send_z, send_x)]
    around = z_scales, z_scales
    messages = lax.optimization_barrier(
        [[pack(v, z_scales) for v in values[:2]] for values, _, _ in rings]
    )
    received = [[send(m[0], 1), send(m[1], -1)] for m, (_, send, _) in zip(messages, rings)]
    gram, _ = lax.optimization_barrier((gram, messages))
    gram = gram + send_core(gram)
    gram = ring_fold(gram, send_y, jnp.add)[0]
    seconds = [
        ring_second(r, values[2:4], send, z_scales, *around)
        for r, (values, send, _) in zip(received, rings)
    ]
    gram, _ = lax.optimization_barrier((gram, [messages for _, _, messages in seconds]))
    lower_factor = jnp.linalg.cholesky(gram)
    thirds = []
    for (direct, sums, _), (values, _, send) in zip(seconds, rings):
        total = ring_total(direct, sums, values[4:], z_scales, *around)
        parts = [
            jnp.concatenate([total(h, r * 2 * B, (r + 1) * 2 * B) for h in range(2)], axis=0)
            for r in range(4)
        ]
        thirds.append(ring_exchange(parts, send, z_scales))
    lower_factor, _ = lax.optimization_barrier((lower_factor, [m for _, m in thirds]))
    inverse = lax.linalg.triangular_solve(
        lower_factor, jnp.eye(K, dtype=f32), left_side=True, lower=True
    )
    q_share = jnp.dot(y_share, inverse.T, precision=highest, preferred_element_type=f32)
    z_raw = jnp.concatenate([z for z, _ in thirds], axis=0)
    z_share = jnp.dot(z_raw, inverse.T, precision=highest, preferred_element_type=f32)
    row_scale = math.sqrt(BR * B * lax.axis_size("row"))
    return (q_share * row_scale, z_share[None])


def solution(mesh):
    in_specs = (
        P("row", "col", None, None, None),
        P("col", None),
        P("row", "col", None),
        P("row", "col", None),
        P("row", "col"),
    )
    out_specs = (P(("row", "col"), None), P("col", "row", None))
    return jax.shard_map(body, mesh=mesh, in_specs=in_specs, out_specs=out_specs, check_vma=False)
```

```python
import math

import jax
import jax.numpy as jnp
from jax import lax
from jax.experimental import pallas as pl
from jax.experimental.layout import Layout, with_layout_constraint
from jax.experimental.pallas import tpu as pltpu
from jax.sharding import PartitionSpec as P

B = 256
K = 128
BR = 128
BC = 128
NBLK = 96
CHUNK = 8
AHEAD = 24
GROUP = 4
VMEM_BYTES = 56 * 1024 * 1024
f32 = jnp.float32
f16 = jnp.float16


def ring(shift):
    return [(c, ((c // 2 + shift) % 4) * 2 + c % 2) for c in range(8)]


def along_x(shift):
    return [(r, ((r // 4 + shift) % 4) * 4 + r % 4) for r in range(16)]


def along_z(shift):
    return [(r, (r // 4) * 4 + (r % 4 + shift) % 4) for r in range(16)]


PAIR = [(c, c ^ 1) for c in range(8)]


def in_groups(start, stop, group, carry):
    groups = (stop - start) // GROUP
    carry = lax.fori_loop(0, groups, lambda g, c: group(start + g * GROUP, GROUP, c), carry)
    return lax.fori_loop(start + groups * GROUP, stop, lambda j, c: group(j, 1, c), carry)


def run_slots(parts, count, targets, order, begin, group, carry, total_sum, outs, out_sems):
    halves = len(outs) // len(parts)
    size = 4 * CHUNK
    order[0] = 0

    def pick(part):
        def one(s, n):
            order[n] = s
            target = targets[s]
            return n + jnp.where((target >= part * size) & (target < (part + 1) * size), 1, 0)

        return one

    ends = [0]
    for part in range(2 * halves):
        ends.append(lax.fori_loop(0, count, pick(part), ends[-1]))
    total = ends[-1]

    def begin_later(j):
        @pl.when(j < total)
        def _():
            begin(j, 0)

    lax.fori_loop(0, jnp.minimum(total, AHEAD), begin, 0)

    def clear(t, _):
        total_sum[t] = jnp.zeros((B, K), f32)
        return 0

    lax.fori_loop(0, 2 * halves * size, clear, 0)
    written = []

    for part in range(2 * halves):
        carry = in_groups(
            ends[part], ends[part + 1], lambda at, n, c: group(begin_later, at, n, c), carry
        )
        start = part // 2 * 2 * size
        for i, n in enumerate(parts):
            if part * size <= start < (part + 1) * size:
                at = part // 2 * len(parts) + i
                copy = pltpu.make_async_copy(
                    total_sum.at[pl.ds(start, n)], outs[at], out_sems.at[at]
                )
                copy.start()
                written.append(copy)
            start += n
    for copy in written:
        copy.wait()
    return carry


def y_kernel(count, targets, cols, blocks, sketch, *rest):
    outs, stat, scratch = rest[:3], rest[3], rest[4:]
    total_sum, order, block_buf, sketch_buf, sems, out_sems = scratch

    def copies(j):
        s = order[j]
        return (
            pltpu.make_async_copy(blocks.at[s], block_buf.at[j], sems.at[0, j]),
            pltpu.make_async_copy(sketch.at[cols[s]], sketch_buf.at[j], sems.at[1, j]),
        )

    def begin(j, _):
        for copy in copies(j):
            copy.start()
        return 0

    def group(begin_later, at, size, carry):
        largest, largest_block = carry
        for u in range(size):
            begin_later(at + u + AHEAD)
        for u in range(size):
            for copy in copies(at + u):
                copy.wait()
        for u in range(size):
            target = targets[order[at + u]]
            tile = block_buf[at + u]
            value = total_sum[target] + jnp.dot(
                tile, sketch_buf[at + u], preferred_element_type=f32
            )
            total_sum[target] = value
            largest = jnp.maximum(largest, jnp.max(jnp.abs(value).reshape(B // 8, 8, K), axis=0))
            largest_block = jnp.maximum(
                largest_block, jnp.max(jnp.abs(tile).reshape(B // 16, 16, B), axis=0)
            )
        return largest, largest_block

    carry = jnp.zeros((8, K), f32), jnp.zeros((16, B), jnp.bfloat16)
    largest, largest_block = run_slots(
        Y_PARTS, count[0], targets, order, begin, group, carry, total_sum, outs, out_sems
    )
    stat[:4] = jnp.full((4, K), jnp.max(largest))
    stat[4:] = jnp.full((4, K), jnp.max(largest_block.astype(f32)))


Y_PARTS = (32, 16, 16)
Z_PARTS = (16, 16, 8, 8, 4, 4, 4, 4)


def sums_of(parts):
    return tuple(jax.ShapeDtypeStruct((n, B, K), f32) for n in parts)


def scratch_for(halves, parts, y_type):
    return [
        pltpu.VMEM((halves * 8 * CHUNK, B, K), f32),
        pltpu.SMEM((NBLK + 1,), jnp.int32),
        pltpu.VMEM((NBLK, B, B), jnp.bfloat16),
        pltpu.VMEM((NBLK, B, K), y_type),
        pltpu.SemaphoreType.DMA((2, NBLK)),
        pltpu.SemaphoreType.DMA((halves * len(parts),)),
    ]


def partial_rows(count, targets, cols, blocks, sketch):
    return pl.pallas_call(
        y_kernel,
        out_shape=sums_of(Y_PARTS) + (jax.ShapeDtypeStruct((8, K), f32),),
        in_specs=[pl.BlockSpec(memory_space=pltpu.SMEM)] * 3
        + [pl.BlockSpec(memory_space=pl.ANY)] * 2,
        out_specs=(pl.BlockSpec(memory_space=pl.ANY),) * 3
        + (pl.BlockSpec(memory_space=pltpu.VMEM),),
        scratch_shapes=scratch_for(1, Y_PARTS, jnp.bfloat16),
        compiler_params=pltpu.CompilerParams(vmem_limit_bytes=VMEM_BYTES),
        cost_estimate=pl.CostEstimate(
            flops=NBLK * B * B * K, bytes_accessed=60 * 1024 * 1024, transcendentals=0
        ),
        name="partial_rows",
    )(count, targets, cols, blocks, sketch)


def z_kernel(count, targets, rows, blocks, table, *rest):
    outs, scratch = rest[:16], rest[16:]
    total_sum, order, block_buf, y_buf, sems, out_sems = scratch

    def copies(j):
        s = order[j]
        return (
            pltpu.make_async_copy(blocks.at[s], block_buf.at[j], sems.at[0, j]),
            pltpu.make_async_copy(table.at[rows[s]], y_buf.at[j], sems.at[1, j]),
        )

    def begin(j, _):
        for copy in copies(j):
            copy.start()
        return 0

    def group(begin_later, at, size, carry):
        for u in range(size):
            begin_later(at + u + AHEAD)
        for u in range(size):
            for copy in copies(at + u):
                copy.wait()
        for u in range(size):
            value = y_buf[at + u]
            high = value.astype(jnp.bfloat16)
            low = (value - high.astype(f32)).astype(jnp.bfloat16)
            product = lax.dot_general(
                block_buf[at + u],
                jnp.concatenate([high, low], axis=1),
                (((0,), (0,)), ((), ())),
                preferred_element_type=f32,
            )
            total_sum[targets[order[at + u]]] += product[:, :K] + product[:, K:]
        return carry

    run_slots(Z_PARTS, count[0], targets, order, begin, group, 0, total_sum, outs, out_sems)


def partial_cols(count, targets, rows, blocks, table):
    return pl.pallas_call(
        z_kernel,
        out_shape=sums_of(Z_PARTS * 2),
        in_specs=[pl.BlockSpec(memory_space=pltpu.SMEM)] * 3
        + [pl.BlockSpec(memory_space=pl.ANY)] * 2,
        out_specs=(pl.BlockSpec(memory_space=pl.ANY),) * 16,
        scratch_shapes=scratch_for(2, Z_PARTS, f32),
        compiler_params=pltpu.CompilerParams(vmem_limit_bytes=VMEM_BYTES),
        cost_estimate=pl.CostEstimate(
            flops=NBLK * B * B * K * 4, bytes_accessed=42 * 1024 * 1024, transcendentals=0
        ),
        name="partial_cols",
    )(count, targets, rows, blocks, table)


def scales_for(bound):
    exponent = jnp.ceil(jnp.log2(jnp.maximum(bound, 1e-30))) - 15.0
    scale, inverse = lax.optimization_barrier((jnp.exp2(exponent), jnp.exp2(-exponent)))
    return scale[0, 0], inverse[0, 0]


def by_rows(value):
    return with_layout_constraint(value, Layout(tuple(range(value.ndim))))


def pack(value, scales):
    return by_rows((value * scales[1]).astype(f16))


def unpack(message, scales):
    return message.astype(f32) * scales[0]


PLACES = (6, 7, 4, 1, 0, 2, 3, 5)


HALF = CHUNK * B


def ring_first(messages, send):
    return lax.optimization_barrier((send(messages[0], 1), send(messages[1], -1)))


def ring_second(received, passing, send, scales, below, above):
    messages = lax.optimization_barrier(
        (
            pack(passing[0] + unpack(received[0][:HALF], below), scales),
            pack(passing[1] + unpack(received[1][:HALF], above), scales),
        )
    )
    sums = send(messages[0], 1), send(messages[1], -1)
    return lax.optimization_barrier((received, sums, messages))


def ring_total(received, sums, staying, scales, below, above):
    def total(which, start=0, stop=HALF):
        direct = received[1 - which][HALF + start : HALF + stop]
        return (
            staying[which][start // (stop - start)]
            + unpack(direct, below if which else above)
            + unpack(sums[which][start:stop], scales)
        )

    return total


def ring_exchange(parts, send, scales):
    messages = [pack(parts[r], scales) for r in (1, 3, 2)]
    up, down, across = (unpack(send(m, r), scales) for m, r in zip(messages, (1, 3, 2)))
    return parts[0] + up + down + across, messages


def after(value, others):
    for other in others:
        value = value + (0.0 * other[(0,) * other.ndim]).astype(value.dtype)
    return value


def ring_fold(value, send, op):
    across, below, above = send(value, 2), send(value, 1), send(value, -1)
    return op(op(value, across), op(below, above)), below, above


def body(blocks, sketch, block_row, block_col, counts):
    highest = lax.Precision.HIGHEST
    blocks = blocks[0, 0]
    rows, cols = block_row[0, 0], block_col[0, 0]
    count = counts[0, 0]
    row_at, col_at = lax.axis_index("row"), lax.axis_index("col")
    here_x, here_z = row_at // 4, row_at % 4
    here_y, core = col_at // 2, col_at % 2
    sketch_table = sketch.reshape(BC, B, K)

    def send_core(value):
        return lax.ppermute(value, "col", PAIR)

    def send_y(value, shift):
        return lax.ppermute(value, "col", ring(shift))

    def send_x(value, shift):
        return lax.ppermute(value, "row", along_x(shift))

    def send_z(value, shift):
        return lax.ppermute(value, "row", along_z(shift))

    live = jnp.arange(NBLK, dtype=jnp.int32) < count

    def chunk_of(rel, half):
        key = (rel & 3) * 2 + half
        chunk = PLACES[7]
        for k in range(7):
            chunk = jnp.where(key == k, PLACES[k], chunk)
        return chunk * CHUNK

    y_target = chunk_of((rows >> 5) - here_y, (rows >> 3) & 1) + (rows & 7)
    row_core = (rows >> 4) & 1
    rel_x, rel_z = ((cols >> 5) - here_x) & 3, ((cols >> 3) - here_z) & 3
    is_a = ((cols >> 2) & 1) == 0
    one, two = jnp.where(is_a, rel_x, rel_z), jnp.where(is_a, rel_z, rel_x)
    z_target = chunk_of(one, two >> 1) + (two & 1) * 4 + (cols & 3) + jnp.where(is_a, 0, 8 * CHUNK)
    other_target = jnp.where(live & (row_core != core), y_target, -1)
    own_target = jnp.where(live & (row_core == core), y_target, -1)
    z_target = jnp.where(live, z_target, -1)
    count = count[None]

    def flat(values):
        return [v.reshape(-1, K) for v in values]

    *other, other_stat = partial_rows(count, other_target, cols, blocks, sketch_table)
    *from_pair, pair_stat = [send_core(v) for v in (*other, other_stat)]
    *own, own_stat = partial_rows(count, own_target, cols, blocks, sketch_table)
    own, from_pair = flat(own), flat(from_pair)

    first_bound = own_stat + pair_stat
    scales = scales_for(first_bound[:1])
    own_first, pair_first = (v.reshape(2, 2 * HALF, K) for v in (own[0], from_pair[0]))
    first = [pack(own_first[i] + pair_first[i], scales) for i in range(2)]
    received = [send_y(first[0], 1), send_y(first[1], -1)]

    in_first = lax.broadcasted_iota(jnp.int32, (8, K), 0) < 4
    entries = jnp.maximum(own_stat, other_stat) * count[0].astype(f32)
    bounds, _ = lax.optimization_barrier((jnp.where(in_first, first_bound, entries), first))
    bounds, below, above = ring_fold(bounds, send_y, jnp.maximum)
    later, _ = lax.optimization_barrier(((own[1:], from_pair[1:]), bounds))
    parts = [
        [mine[at : at + HALF] + pair[at : at + HALF] for at in (0, HALF)] for mine, pair in zip(*later)
    ]
    passing, staying = lax.optimization_barrier(parts)
    around = scales_for(below[:1]), scales_for(above[:1])
    sum_scales = scales_for(bounds[:1] * 4.0)
    received, sums, messages = ring_second(received, passing, send_y, sum_scales, *around)
    y_part = ring_total(received, sums, [[v] for v in staying], sum_scales, *around)
    y_share = jnp.concatenate([y_part(0), y_part(1)], axis=0)

    bounds, _ = lax.optimization_barrier((bounds, messages))
    bounds = jnp.maximum(bounds, send_core(bounds))
    y_scales = scales_for(bounds[:1] * 4.0)
    bounds = ring_fold(ring_fold(bounds, send_x, jnp.maximum)[0], send_z, jnp.maximum)[0]
    z_scales = scales_for(bounds[:1] * bounds[4:5] * (4.0 * 16.0 * B))

    gram = jnp.dot(
        y_share.T, y_share, precision=lax.Precision.HIGH, preferred_element_type=f32
    )
    mine, z_scales, gram = lax.optimization_barrier((pack(y_share, y_scales), z_scales, gram))
    gathered = lax.all_gather(mine, "col", axis=0, tiled=True)
    gram = ring_fold(gram, send_x, jnp.add)[0]
    table = by_rows(after(unpack(gathered, y_scales), [gram])).reshape(BR, B, K)
    gram = ring_fold(after(gram, [gathered]), send_z, jnp.add)[0]
    z_target = after(z_target, [gram])
    partial = flat(partial_cols(count, z_target, rows, blocks, table))
    gram = after(gram, [table])
    gram = gram + send_core(gram)
    z_scales = tuple(after(v, [gram]) for v in z_scales)
    gram = ring_fold(gram, send_y, jnp.add)[0]

    rings = [(partial[:8], send_x, send_z), (partial[8:], send_z, send_x)]
    around = z_scales, z_scales
    messages = [[pack(v, z_scales) for v in values[:2]] for values, _, _ in rings]
    received = [[send(m[0], 1), send(m[1], -1)] for m, (_, send, _) in zip(messages, rings)]
    gram = after(gram, [m for pair in messages for m in pair])
    lower_factor = jnp.linalg.cholesky(gram)
    seconds = [
        ring_second(r, values[2:4], send, z_scales, *around)
        for r, (values, send, _) in zip(received, rings)
    ]
    thirds = []
    for (direct, sums, _), (values, _, send) in zip(seconds, rings):
        total = ring_total(direct, sums, [values[4:6], values[6:]], z_scales, *around)
        quarters = [total(r // 2, r % 2 * 4 * B, (r % 2 + 1) * 4 * B) for r in range(4)]
        thirds.append(ring_exchange(quarters, send, z_scales))
    inverse = lax.linalg.triangular_solve(
        lower_factor, jnp.eye(K, dtype=f32), left_side=True, lower=True
    )
    q_share = jnp.dot(y_share, inverse.T, precision=highest, preferred_element_type=f32)
    z_raw = jnp.concatenate([z for z, _ in thirds], axis=0)
    z_share = jnp.dot(z_raw, inverse.T, precision=highest, preferred_element_type=f32)
    row_scale = math.sqrt(BR * B * lax.axis_size("row"))
    return (q_share * row_scale, z_share[None])


def solution(mesh):
    in_specs = (
        P("row", "col", None, None, None),
        P("col", None),
        P("row", "col", None),
        P("row", "col", None),
        P("row", "col"),
    )
    out_specs = (P(("row", "col"), None), P("col", "row", None))
    return jax.shard_map(body, mesh=mesh, in_specs=in_specs, out_specs=out_specs, check_vma=False)
```

```python
import math

import jax
import jax.numpy as jnp
from jax import lax
from jax.experimental import pallas as pl
from jax.experimental.layout import Layout, with_layout_constraint
from jax.experimental.pallas import tpu as pltpu
from jax.sharding import PartitionSpec as P

B = 256
K = 128
BR = 128
BC = 128
NBLK = 96
CHUNK = 8
AHEAD = 28
GROUP = 4
BUFFERS = AHEAD + GROUP
MIB = 1024 * 1024
f32 = jnp.float32
f16 = jnp.float16


def ring(shift):
    return [(c, ((c // 2 + shift) % 4) * 2 + c % 2) for c in range(8)]


def along_x(shift):
    return [(r, ((r // 4 + shift) % 4) * 4 + r % 4) for r in range(16)]


def along_z(shift):
    return [(r, (r // 4) * 4 + (r % 4 + shift) % 4) for r in range(16)]


GRAM_SCALE = 2.0**-27
LOW_SCALE = 2.0**11

PAIR = [(c, c ^ 1) for c in range(8)]


def in_groups(start, stop, group, carry):
    groups = (stop - start) // GROUP
    carry = lax.fori_loop(0, groups, lambda g, c: group(start + g * GROUP, GROUP, c), carry)
    return lax.fori_loop(start + groups * GROUP, stop, lambda j, c: group(j, 1, c), carry)


def run_slots(parts, count, targets, order, begin, group, carry, total_sum, outs, out_sems):
    halves = len(outs) // len(parts)
    size = 4 * CHUNK
    order[0] = 0

    def pick(part):
        def one(s, n):
            order[n] = s
            target = targets[s]
            return n + jnp.where((target >= part * size) & (target < (part + 1) * size), 1, 0)

        return one

    ends = [0]
    for part in range(2 * halves):
        ends.append(lax.fori_loop(0, count, pick(part), ends[-1]))
    total = ends[-1]

    def begin_later(j):
        @pl.when(j < total)
        def _():
            begin(j, 0)

    lax.fori_loop(0, jnp.minimum(total, AHEAD), begin, 0)

    def clear(t, _):
        total_sum[t] = jnp.zeros((B, K), f32)
        return 0

    lax.fori_loop(0, 2 * halves * size, clear, 0)
    written = []

    for part in range(2 * halves):
        carry = in_groups(
            ends[part], ends[part + 1], lambda at, n, c: group(begin_later, at, n, c), carry
        )
        start = part // 2 * 2 * size
        for i, n in enumerate(parts):
            if part * size <= start < (part + 1) * size:
                at = part // 2 * len(parts) + i
                copy = pltpu.make_async_copy(
                    total_sum.at[pl.ds(start, n)], outs[at], out_sems.at[at]
                )
                copy.start()
                written.append(copy)
            start += n
    for copy in written:
        copy.wait()
    return carry


def y_kernel(count, targets, cols, blocks, sketch, *rest):
    outs, stat, scratch = rest[:3], rest[3], rest[4:]
    total_sum, order, block_buf, sketch_buf, sems, out_sems = scratch

    def copies(j):
        s, at = order[j], lax.rem(j, BUFFERS)
        return (
            pltpu.make_async_copy(blocks.at[s], block_buf.at[at], sems.at[0, at]),
            pltpu.make_async_copy(sketch.at[cols[s]], sketch_buf.at[at], sems.at[1, at]),
        )

    def begin(j, _):
        for copy in copies(j):
            copy.start()
        return 0

    def group(begin_later, at, size, carry):
        largest, largest_block = carry
        for u in range(size):
            begin_later(at + u + AHEAD)
        for u in range(size):
            for copy in copies(at + u):
                copy.wait()
        for u in range(size):
            target = targets[order[at + u]]
            buffer = lax.rem(at + u, BUFFERS)
            tile = block_buf[buffer]
            value = total_sum[target] + jnp.dot(
                tile, sketch_buf[buffer], preferred_element_type=f32
            )
            total_sum[target] = value
            largest = jnp.maximum(largest, jnp.max(jnp.abs(value).reshape(B // 8, 8, K), axis=0))
            largest_block = jnp.maximum(
                largest_block, jnp.max(jnp.abs(tile).reshape(B // 16, 16, B), axis=0)
            )
        return largest, largest_block

    carry = jnp.zeros((8, K), f32), jnp.zeros((16, B), jnp.bfloat16)
    largest, largest_block = run_slots(
        Y_PARTS, count[0], targets, order, begin, group, carry, total_sum, outs, out_sems
    )
    stat[:4] = jnp.full((4, K), jnp.max(largest))
    stat[4:] = jnp.full((4, K), jnp.max(largest_block.astype(f32)))


Y_PARTS = (32, 16, 16)
Z_PARTS = (16, 16, 8, 8, 4, 4, 4, 4)


def sums_of(parts):
    return tuple(jax.ShapeDtypeStruct((n, B, K), f32) for n in parts)


def scratch_for(halves, parts, y_type):
    return [
        pltpu.VMEM((halves * 8 * CHUNK, B, K), f32),
        pltpu.SMEM((NBLK + 1,), jnp.int32),
        pltpu.VMEM((BUFFERS, B, B), jnp.bfloat16),
        pltpu.VMEM((BUFFERS, B, K), y_type),
        pltpu.SemaphoreType.DMA((2, BUFFERS)),
        pltpu.SemaphoreType.DMA((halves * len(parts),)),
    ]


def partial_rows(count, targets, cols, blocks, sketch):
    return pl.pallas_call(
        y_kernel,
        out_shape=sums_of(Y_PARTS) + (jax.ShapeDtypeStruct((8, K), f32),),
        in_specs=[pl.BlockSpec(memory_space=pltpu.SMEM)] * 3
        + [pl.BlockSpec(memory_space=pl.ANY)] * 2,
        out_specs=(pl.BlockSpec(memory_space=pl.ANY),) * 3
        + (pl.BlockSpec(memory_space=pltpu.VMEM),),
        scratch_shapes=scratch_for(1, Y_PARTS, jnp.bfloat16),
        compiler_params=pltpu.CompilerParams(vmem_limit_bytes=20 * MIB),
        cost_estimate=pl.CostEstimate(
            flops=NBLK * B * B * K, bytes_accessed=60 * 1024 * 1024, transcendentals=0
        ),
        name="partial_rows",
    )(count, targets, cols, blocks, sketch)


def z_kernel(count, targets, rows, blocks, table, *rest):
    outs, scratch = rest[:16], rest[16:]
    total_sum, order, block_buf, y_buf, sems, out_sems = scratch

    def copies(j):
        s, at = order[j], lax.rem(j, BUFFERS)
        return (
            pltpu.make_async_copy(blocks.at[s], block_buf.at[at], sems.at[0, at]),
            pltpu.make_async_copy(table.at[rows[s]], y_buf.at[at], sems.at[1, at]),
        )

    def begin(j, _):
        for copy in copies(j):
            copy.start()
        return 0

    def group(begin_later, at, size, carry):
        for u in range(size):
            begin_later(at + u + AHEAD)
        for u in range(size):
            for copy in copies(at + u):
                copy.wait()
        for u in range(size):
            buffer = lax.rem(at + u, BUFFERS)
            value = y_buf[buffer]
            high = value.astype(jnp.bfloat16)
            low = (value - high.astype(f32)).astype(jnp.bfloat16)
            product = lax.dot_general(
                block_buf[buffer],
                jnp.concatenate([high, low], axis=1),
                (((0,), (0,)), ((), ())),
                preferred_element_type=f32,
            )
            total_sum[targets[order[at + u]]] += product[:, :K] + product[:, K:]
        return carry

    run_slots(Z_PARTS, count[0], targets, order, begin, group, 0, total_sum, outs, out_sems)


def partial_cols(count, targets, rows, blocks, table):
    return pl.pallas_call(
        z_kernel,
        out_shape=sums_of(Z_PARTS * 2),
        in_specs=[pl.BlockSpec(memory_space=pltpu.SMEM)] * 3
        + [pl.BlockSpec(memory_space=pl.ANY)] * 2,
        out_specs=(pl.BlockSpec(memory_space=pl.ANY),) * 16,
        scratch_shapes=scratch_for(2, Z_PARTS, f32),
        compiler_params=pltpu.CompilerParams(vmem_limit_bytes=32 * MIB),
        cost_estimate=pl.CostEstimate(
            flops=NBLK * B * B * K * 4, bytes_accessed=42 * 1024 * 1024, transcendentals=0
        ),
        name="partial_cols",
    )(count, targets, rows, blocks, table)


def scales_for(bound):
    exponent = jnp.ceil(jnp.log2(jnp.maximum(bound, 1e-30))) - 15.0
    scale, inverse = lax.optimization_barrier((jnp.exp2(exponent), jnp.exp2(-exponent)))
    return scale[0, 0], inverse[0, 0]


def by_rows(value):
    return with_layout_constraint(value, Layout(tuple(range(value.ndim))))


def pack(value, scales):
    return by_rows((value * scales[1]).astype(f16))


def unpack(message, scales):
    return message.astype(f32) * scales[0]


PLACES = (6, 7, 4, 1, 0, 2, 3, 5)


HALF = CHUNK * B


def ring_first(messages, send):
    return lax.optimization_barrier((send(messages[0], 1), send(messages[1], -1)))


def ring_second(received, passing, send, scales, below, above):
    messages = lax.optimization_barrier(
        (
            pack(passing[0] + unpack(received[0][:HALF], below), scales),
            pack(passing[1] + unpack(received[1][:HALF], above), scales),
        )
    )
    sums = send(messages[0], 1), send(messages[1], -1)
    return lax.optimization_barrier((received, sums, messages))


def ring_total(received, sums, staying, scales, below, above):
    def total(which, start=0, stop=HALF):
        direct = received[1 - which][HALF + start : HALF + stop]
        return (
            staying[which][start // (stop - start)]
            + unpack(direct, below if which else above)
            + unpack(sums[which][start:stop], scales)
        )

    return total


def ring_exchange(parts, send, scales):
    messages = [pack(parts[r], scales) for r in (1, 3, 2)]
    up, down, across = (unpack(send(m, r), scales) for m, r in zip(messages, (1, 3, 2)))
    return parts[0] + up + down + across, messages


def ring_fold(value, send, op):
    across, below, above = send(value, 2), send(value, 1), send(value, -1)
    return op(op(value, across), op(below, above)), below, above


def body(blocks, sketch, block_row, block_col, counts):
    highest = lax.Precision.HIGHEST
    blocks = blocks[0, 0]
    rows, cols = block_row[0, 0], block_col[0, 0]
    count = counts[0, 0]
    row_at, col_at = lax.axis_index("row"), lax.axis_index("col")
    here_x, here_z = row_at // 4, row_at % 4
    here_y, core = col_at // 2, col_at % 2
    sketch_table = sketch.reshape(BC, B, K)

    def send_core(value):
        return lax.ppermute(value, "col", PAIR)

    def send_y(value, shift):
        return lax.ppermute(value, "col", ring(shift))

    def send_x(value, shift):
        return lax.ppermute(value, "row", along_x(shift))

    def send_z(value, shift):
        return lax.ppermute(value, "row", along_z(shift))

    live = jnp.arange(NBLK, dtype=jnp.int32) < count

    def chunk_of(rel, half):
        key = (rel & 3) * 2 + half
        chunk = PLACES[7]
        for k in range(7):
            chunk = jnp.where(key == k, PLACES[k], chunk)
        return chunk * CHUNK

    y_target = chunk_of((rows >> 5) - here_y, (rows >> 3) & 1) + (rows & 7)
    row_core = (rows >> 4) & 1
    rel_x, rel_z = ((cols >> 5) - here_x) & 3, ((cols >> 3) - here_z) & 3
    is_a = ((cols >> 2) & 1) == 0
    one, two = jnp.where(is_a, rel_x, rel_z), jnp.where(is_a, rel_z, rel_x)
    z_target = chunk_of(one, two >> 1) + (two & 1) * 4 + (cols & 3) + jnp.where(is_a, 0, 8 * CHUNK)
    other_target = jnp.where(live & (row_core != core), y_target, -1)
    own_target = jnp.where(live & (row_core == core), y_target, -1)
    z_target = jnp.where(live, z_target, -1)
    count = count[None]

    def flat(values):
        return [v.reshape(-1, K) for v in values]

    *other, other_stat = partial_rows(count, other_target, cols, blocks, sketch_table)
    *from_pair, pair_stat = [send_core(v) for v in (*other, other_stat)]
    *own, own_stat = partial_rows(count, own_target, cols, blocks, sketch_table)
    own, from_pair = flat(own), flat(from_pair)

    first_bound = own_stat + pair_stat
    scales = scales_for(first_bound[:1])
    own_first, pair_first = (v.reshape(2, 2 * HALF, K) for v in (own[0], from_pair[0]))
    first = [pack(own_first[i] + pair_first[i], scales) for i in range(2)]
    received = [send_y(first[0], 1), send_y(first[1], -1)]

    in_first = lax.broadcasted_iota(jnp.int32, (8, K), 0) < 4
    entries = jnp.maximum(own_stat, other_stat) * count[0].astype(f32)
    bounds, _ = lax.optimization_barrier((jnp.where(in_first, first_bound, entries), first))
    bounds, below, above = ring_fold(bounds, send_y, jnp.maximum)
    later, _ = lax.optimization_barrier(((own[1:], from_pair[1:]), bounds))
    parts = [
        [mine[at : at + HALF] + pair[at : at + HALF] for at in (0, HALF)] for mine, pair in zip(*later)
    ]
    passing, staying = lax.optimization_barrier(parts)
    around = scales_for(below[:1]), scales_for(above[:1])
    sum_scales = scales_for(bounds[:1] * 4.0)
    received, sums, messages = ring_second(received, passing, send_y, sum_scales, *around)
    y_part = ring_total(received, sums, [[v] for v in staying], sum_scales, *around)
    y_share = jnp.concatenate([y_part(0), y_part(1)], axis=0)

    bounds, _ = lax.optimization_barrier((bounds, messages))
    bounds = jnp.maximum(bounds, send_core(bounds))
    y_scales = scales_for(bounds[:1] * 4.0)
    bounds = ring_fold(ring_fold(bounds, send_x, jnp.maximum)[0], send_z, jnp.maximum)[0]
    z_scales = scales_for(bounds[:1] * bounds[4:5] * (4.0 * 16.0 * B))

    scaled = y_share * y_scales[1]
    gram = jnp.dot(
        scaled.T, scaled, precision=lax.Precision.HIGH, preferred_element_type=f32
    ) * GRAM_SCALE
    high = lax.reduce_precision(gram, exponent_bits=5, mantissa_bits=10)
    low = (gram - high) * LOW_SCALE
    mine = jnp.concatenate([v.astype(f16) for v in (scaled, high, low)], axis=0)
    mine, z_scales = lax.optimization_barrier((by_rows(mine), z_scales))
    gathered = lax.all_gather(mine, "col", axis=0)
    rows_each = BR // 8 * B
    table = by_rows(unpack(gathered[:, :rows_each], y_scales)).reshape(BR, B, K)
    high, low = (
        jnp.sum(gathered[:, at : at + K].astype(f32), axis=0) for at in (rows_each, rows_each + K)
    )
    gram = (high + low * (1.0 / LOW_SCALE)) * (1.0 / GRAM_SCALE) * y_scales[0] * y_scales[0]
    gram = ring_fold(gram, send_x, jnp.add)[0]
    partial = flat(partial_cols(count, z_target, rows, blocks, table))
    gram = ring_fold(gram, send_z, jnp.add)[0]

    rings = [(partial[:8], send_x, send_z), (partial[8:], send_z, send_x)]
    around = z_scales, z_scales
    messages = [[pack(v, z_scales) for v in values[:2]] for values, _, _ in rings]
    received = [[send(m[0], 1), send(m[1], -1)] for m, (_, send, _) in zip(messages, rings)]
    lower_factor = jnp.linalg.cholesky(gram)
    seconds = [
        ring_second(r, values[2:4], send, z_scales, *around)
        for r, (values, send, _) in zip(received, rings)
    ]
    thirds = []
    for (direct, sums, _), (values, _, send) in zip(seconds, rings):
        total = ring_total(direct, sums, [values[4:6], values[6:]], z_scales, *around)
        quarters = [total(r // 2, r % 2 * 4 * B, (r % 2 + 1) * 4 * B) for r in range(4)]
        thirds.append(ring_exchange(quarters, send, z_scales))
    inverse = lax.linalg.triangular_solve(
        lower_factor, jnp.eye(K, dtype=f32), left_side=True, lower=True
    )
    q_share = jnp.dot(y_share, inverse.T, precision=highest, preferred_element_type=f32)
    z_raw = jnp.concatenate([z for z, _ in thirds], axis=0)
    z_share = jnp.dot(z_raw, inverse.T, precision=highest, preferred_element_type=f32)
    row_scale = math.sqrt(BR * B * lax.axis_size("row"))
    return (q_share * row_scale, z_share[None])


def solution(mesh):
    in_specs = (
        P("row", "col", None, None, None),
        P("col", None),
        P("row", "col", None),
        P("row", "col", None),
        P("row", "col"),
    )
    out_specs = (P(("row", "col"), None), P("col", "row", None))
    return jax.shard_map(body, mesh=mesh, in_specs=in_specs, out_specs=out_specs, check_vma=False)
```

```python
import math

import jax
import jax.numpy as jnp
from jax import lax
from jax.experimental import pallas as pl
from jax.experimental.layout import Layout, with_layout_constraint
from jax.experimental.pallas import tpu as pltpu
from jax.sharding import PartitionSpec as P

B = 256
K = 128
BR = 128
BC = 128
NBLK = 96
CHUNK = 8
AHEAD = 28
GROUP = 4
BUFFERS = AHEAD + GROUP
VMEM_BYTES = 56 * 1024 * 1024
f32 = jnp.float32
f16 = jnp.float16


def ring(shift):
    return [(c, ((c // 2 + shift) % 4) * 2 + c % 2) for c in range(8)]


def along_x(shift):
    return [(r, ((r // 4 + shift) % 4) * 4 + r % 4) for r in range(16)]


def along_z(shift):
    return [(r, (r // 4) * 4 + (r % 4 + shift) % 4) for r in range(16)]


GRAM_SCALE = 2.0**-27
LOW_SCALE = 2.0**11

PAIR = [(c, c ^ 1) for c in range(8)]


def run_slots(parts, count, targets, order, bounds, begin, group, carry, total_sum, outs, out_sems):
    chunks = total_sum.shape[0] // CHUNK

    def chunk_of(s):
        return jnp.where(targets[s] < 0, chunks, targets[s] // CHUNK)

    for c in range(chunks + 1):
        bounds[c] = 0

    def tally(s, _):
        c = chunk_of(s)
        bounds[c] = bounds[c] + 1
        return 0

    lax.fori_loop(0, count, tally, 0)
    total = 0
    for c in range(chunks):
        here = bounds[c]
        bounds[c] = total
        total = total + here
    bounds[chunks] = total

    def place(s, _):
        c = chunk_of(s)
        at = bounds[c]
        order[at] = s
        bounds[c] = at + 1
        return 0

    lax.fori_loop(0, count, place, 0)

    def begin_later(j):
        @pl.when(j < total)
        def _():
            begin(j, 0)

    lax.fori_loop(0, jnp.minimum(total, AHEAD), begin, 0)

    def clear(t, _):
        total_sum[t] = jnp.zeros((B, K), f32)
        return 0

    lax.fori_loop(0, chunks * CHUNK, clear, 0)

    writes = [[] for _ in range(chunks)]
    first = 0
    for ring_at in range(len(outs) // len(parts)):
        for i, tiles in enumerate(parts):
            at = ring_at * len(parts) + i
            for piece in range(0, tiles, CHUNK):
                size = min(CHUNK, tiles)
                sem = sum(len(w) for w in writes)
                writes[first // CHUNK].append(
                    pltpu.make_async_copy(
                        total_sum.at[pl.ds(first, size)],
                        outs[at].at[pl.ds(piece, size)],
                        out_sems.at[sem],
                    )
                )
                first += size

    def write_done(done, chunk):
        def step(c):
            for i, pieces in enumerate(writes):

                @pl.when(c == i)
                def _():
                    for copy in pieces:
                        copy.start()

            return c + 1

        return lax.while_loop(
            lambda c: (c < chunks) & (bounds[jnp.minimum(c, chunks - 1)] <= done), step, chunk
        )

    def by_group(size, first):
        def step(g, state):
            chunk, carry = state
            at = first + g * size
            carry = group(begin_later, at, size, carry)
            return write_done(at + size, chunk), carry

        return step

    groups = total // GROUP
    state = write_done(0, 0), carry
    state = lax.fori_loop(0, groups, by_group(GROUP, 0), state)
    state = lax.fori_loop(0, total - groups * GROUP, by_group(1, groups * GROUP), state)
    for pieces in writes:
        for copy in pieces:
            copy.wait()
    return state[1]


def y_kernel(count, targets, cols, blocks, sketch, *rest):
    outs, stat, scratch = rest[:3], rest[3], rest[4:]
    total_sum, order, bounds, block_buf, sketch_buf, sems, out_sems = scratch

    def copies(j):
        s, at = order[j], lax.rem(j, BUFFERS)
        return (
            pltpu.make_async_copy(blocks.at[s], block_buf.at[at], sems.at[0, at]),
            pltpu.make_async_copy(sketch.at[cols[s]], sketch_buf.at[at], sems.at[1, at]),
        )

    def begin(j, _):
        for copy in copies(j):
            copy.start()
        return 0

    def group(begin_later, at, size, carry):
        largest, largest_block = carry
        for u in range(size):
            begin_later(at + u + AHEAD)
        for u in range(size):
            for copy in copies(at + u):
                copy.wait()
        for u in range(size):
            target = targets[order[at + u]]
            buffer = lax.rem(at + u, BUFFERS)
            tile = block_buf[buffer]
            value = total_sum[target] + jnp.dot(
                tile, sketch_buf[buffer], preferred_element_type=f32
            )
            total_sum[target] = value
            largest = jnp.maximum(largest, jnp.max(jnp.abs(value).reshape(B // 8, 8, K), axis=0))
            largest_block = jnp.maximum(
                largest_block, jnp.max(jnp.abs(tile).reshape(B // 16, 16, B), axis=0)
            )
        return largest, largest_block

    carry = jnp.zeros((8, K), f32), jnp.zeros((16, B), jnp.bfloat16)
    largest, largest_block = run_slots(
        Y_PARTS, count[0], targets, order, bounds, begin, group, carry, total_sum, outs, out_sems
    )
    stat[:4] = jnp.full((4, K), jnp.max(largest))
    stat[4:] = jnp.full((4, K), jnp.max(largest_block.astype(f32)))


Y_PARTS = (32, 16, 16)
Z_PARTS = (16, 16, 8, 8, 4, 4, 4, 4)


def sums_of(parts):
    return tuple(jax.ShapeDtypeStruct((n, B, K), f32) for n in parts)


def scratch_for(halves, parts, y_type):
    return [
        pltpu.VMEM((halves * 8 * CHUNK, B, K), f32),
        pltpu.SMEM((NBLK + 1,), jnp.int32),
        pltpu.SMEM((halves * 8 + 1,), jnp.int32),
        pltpu.VMEM((BUFFERS, B, B), jnp.bfloat16),
        pltpu.VMEM((BUFFERS, B, K), y_type),
        pltpu.SemaphoreType.DMA((2, BUFFERS)),
        pltpu.SemaphoreType.DMA((halves * 10,)),
    ]


def partial_rows(count, targets, cols, blocks, sketch):
    return pl.pallas_call(
        y_kernel,
        out_shape=sums_of(Y_PARTS) + (jax.ShapeDtypeStruct((8, K), f32),),
        in_specs=[pl.BlockSpec(memory_space=pltpu.SMEM)] * 3
        + [pl.BlockSpec(memory_space=pl.ANY)] * 2,
        out_specs=(pl.BlockSpec(memory_space=pl.ANY),) * 3
        + (pl.BlockSpec(memory_space=pltpu.VMEM),),
        scratch_shapes=scratch_for(1, Y_PARTS, jnp.bfloat16),
        compiler_params=pltpu.CompilerParams(vmem_limit_bytes=VMEM_BYTES),
        cost_estimate=pl.CostEstimate(
            flops=NBLK * B * B * K, bytes_accessed=60 * 1024 * 1024, transcendentals=0
        ),
        name="partial_rows",
    )(count, targets, cols, blocks, sketch)


def z_kernel(count, targets, rows, blocks, table, *rest):
    outs, scratch = rest[:16], rest[16:]
    total_sum, order, bounds, block_buf, y_buf, sems, out_sems = scratch

    def copies(j):
        s, at = order[j], lax.rem(j, BUFFERS)
        return (
            pltpu.make_async_copy(blocks.at[s], block_buf.at[at], sems.at[0, at]),
            pltpu.make_async_copy(table.at[rows[s]], y_buf.at[at], sems.at[1, at]),
        )

    def begin(j, _):
        for copy in copies(j):
            copy.start()
        return 0

    def group(begin_later, at, size, carry):
        for u in range(size):
            begin_later(at + u + AHEAD)
        for u in range(size):
            for copy in copies(at + u):
                copy.wait()
        for u in range(size):
            buffer = lax.rem(at + u, BUFFERS)
            value = y_buf[buffer]
            high = value.astype(jnp.bfloat16)
            low = (value - high.astype(f32)).astype(jnp.bfloat16)
            product = lax.dot_general(
                block_buf[buffer],
                jnp.concatenate([high, low], axis=1),
                (((0,), (0,)), ((), ())),
                preferred_element_type=f32,
            )
            total_sum[targets[order[at + u]]] += product[:, :K] + product[:, K:]
        return carry

    run_slots(
        Z_PARTS, count[0], targets, order, bounds, begin, group, 0, total_sum, outs, out_sems
    )


def partial_cols(count, targets, rows, blocks, table):
    return pl.pallas_call(
        z_kernel,
        out_shape=sums_of(Z_PARTS * 2),
        in_specs=[pl.BlockSpec(memory_space=pltpu.SMEM)] * 3
        + [pl.BlockSpec(memory_space=pl.ANY)] * 2,
        out_specs=(pl.BlockSpec(memory_space=pl.ANY),) * 16,
        scratch_shapes=scratch_for(2, Z_PARTS, f32),
        compiler_params=pltpu.CompilerParams(vmem_limit_bytes=VMEM_BYTES),
        cost_estimate=pl.CostEstimate(
            flops=NBLK * B * B * K * 4, bytes_accessed=42 * 1024 * 1024, transcendentals=0
        ),
        name="partial_cols",
    )(count, targets, rows, blocks, table)


def scales_for(bound):
    exponent = jnp.ceil(jnp.log2(jnp.maximum(bound, 1e-30))) - 15.0
    scale, inverse = lax.optimization_barrier((jnp.exp2(exponent), jnp.exp2(-exponent)))
    return scale[0, 0], inverse[0, 0]


def by_rows(value):
    return with_layout_constraint(value, Layout(tuple(range(value.ndim))))


def pack(value, scales):
    return by_rows((value * scales[1]).astype(f16))


def unpack(message, scales):
    return message.astype(f32) * scales[0]


PLACES = (6, 7, 4, 1, 0, 2, 3, 5)


HALF = CHUNK * B


def ring_first(messages, send):
    return lax.optimization_barrier((send(messages[0], 1), send(messages[1], -1)))


def ring_second(received, passing, send, scales, below, above):
    messages = lax.optimization_barrier(
        (
            pack(passing[0] + unpack(received[0][:HALF], below), scales),
            pack(passing[1] + unpack(received[1][:HALF], above), scales),
        )
    )
    sums = send(messages[0], 1), send(messages[1], -1)
    return lax.optimization_barrier((received, sums, messages))


def ring_total(received, sums, staying, scales, below, above):
    def total(which, start=0, stop=HALF):
        direct = received[1 - which][HALF + start : HALF + stop]
        return (
            staying[which][start // (stop - start)]
            + unpack(direct, below if which else above)
            + unpack(sums[which][start:stop], scales)
        )

    return total


def ring_exchange(parts, send, scales):
    messages = [pack(parts[r], scales) for r in (1, 3, 2)]
    up, down, across = (unpack(send(m, r), scales) for m, r in zip(messages, (1, 3, 2)))
    return parts[0] + up + down + across, messages


def ring_fold(value, send, op):
    across, below, above = send(value, 2), send(value, 1), send(value, -1)
    return op(op(value, across), op(below, above)), below, above


def body(blocks, sketch, block_row, block_col, counts):
    highest = lax.Precision.HIGHEST
    blocks = blocks[0, 0]
    rows, cols = block_row[0, 0], block_col[0, 0]
    count = counts[0, 0]
    row_at, col_at = lax.axis_index("row"), lax.axis_index("col")
    here_x, here_z = row_at // 4, row_at % 4
    here_y, core = col_at // 2, col_at % 2
    sketch_table = sketch.reshape(BC, B, K)

    def send_core(value):
        return lax.ppermute(value, "col", PAIR)

    def send_y(value, shift):
        return lax.ppermute(value, "col", ring(shift))

    def send_x(value, shift):
        return lax.ppermute(value, "row", along_x(shift))

    def send_z(value, shift):
        return lax.ppermute(value, "row", along_z(shift))

    live = jnp.arange(NBLK, dtype=jnp.int32) < count

    def chunk_of(rel, half):
        key = (rel & 3) * 2 + half
        chunk = PLACES[7]
        for k in range(7):
            chunk = jnp.where(key == k, PLACES[k], chunk)
        return chunk * CHUNK

    y_target = chunk_of((rows >> 5) - here_y, (rows >> 3) & 1) + (rows & 7)
    row_core = (rows >> 4) & 1
    rel_x, rel_z = ((cols >> 5) - here_x) & 3, ((cols >> 3) - here_z) & 3
    is_a = ((cols >> 2) & 1) == 0
    one, two = jnp.where(is_a, rel_x, rel_z), jnp.where(is_a, rel_z, rel_x)
    z_target = chunk_of(one, two >> 1) + (two & 1) * 4 + (cols & 3) + jnp.where(is_a, 0, 8 * CHUNK)
    other_target = jnp.where(live & (row_core != core), y_target, -1)
    own_target = jnp.where(live & (row_core == core), y_target, -1)
    z_target = jnp.where(live, z_target, -1)
    count = count[None]

    def flat(values):
        return [v.reshape(-1, K) for v in values]

    *other, other_stat = partial_rows(count, other_target, cols, blocks, sketch_table)
    *from_pair, pair_stat = [send_core(v) for v in (*other, other_stat)]
    *own, own_stat = partial_rows(count, own_target, cols, blocks, sketch_table)
    own, from_pair = flat(own), flat(from_pair)

    first_bound = own_stat + pair_stat
    scales = scales_for(first_bound[:1])
    own_first, pair_first = (v.reshape(2, 2 * HALF, K) for v in (own[0], from_pair[0]))
    first = [pack(own_first[i] + pair_first[i], scales) for i in range(2)]
    received = [send_y(first[0], 1), send_y(first[1], -1)]

    in_first = lax.broadcasted_iota(jnp.int32, (8, K), 0) < 4
    entries = jnp.maximum(own_stat, other_stat) * count[0].astype(f32)
    bounds, _ = lax.optimization_barrier((jnp.where(in_first, first_bound, entries), first))
    bounds, below, above = ring_fold(bounds, send_y, jnp.maximum)
    later, _ = lax.optimization_barrier(((own[1:], from_pair[1:]), bounds))
    parts = [
        [mine[at : at + HALF] + pair[at : at + HALF] for at in (0, HALF)] for mine, pair in zip(*later)
    ]
    passing, staying = lax.optimization_barrier(parts)
    around = scales_for(below[:1]), scales_for(above[:1])
    sum_scales = scales_for(bounds[:1] * 4.0)
    received, sums, messages = ring_second(received, passing, send_y, sum_scales, *around)
    y_part = ring_total(received, sums, [[v] for v in staying], sum_scales, *around)
    y_share = jnp.concatenate([y_part(0), y_part(1)], axis=0)

    bounds, _ = lax.optimization_barrier((bounds, messages))
    bounds = jnp.maximum(bounds, send_core(bounds))
    y_scales = scales_for(bounds[:1] * 4.0)
    bounds = ring_fold(ring_fold(bounds, send_x, jnp.maximum)[0], send_z, jnp.maximum)[0]
    z_scales = scales_for(bounds[:1] * bounds[4:5] * (4.0 * 16.0 * B))

    scaled = y_share * y_scales[1]
    gram = jnp.dot(
        scaled.T, scaled, precision=lax.Precision.HIGH, preferred_element_type=f32
    ) * GRAM_SCALE
    high = lax.reduce_precision(gram, exponent_bits=5, mantissa_bits=10)
    low = (gram - high) * LOW_SCALE
    mine = jnp.concatenate([v.astype(f16) for v in (scaled, high, low)], axis=0)
    mine, z_scales = lax.optimization_barrier((by_rows(mine), z_scales))
    gathered = lax.all_gather(mine, "col", axis=0, tiled=True)
    table = by_rows(unpack(gathered, y_scales)).reshape(-1, B, K)
    tiles_each = BR // 8 + 1
    table_at = (rows >> 4) * tiles_each + (rows & 15)
    shares = gathered.reshape(8, tiles_each, B, K)[:, tiles_each - 1].astype(f32)
    high, low = jnp.sum(shares[:, :K], axis=0), jnp.sum(shares[:, K:], axis=0)
    gram = (high + low * (1.0 / LOW_SCALE)) * (1.0 / GRAM_SCALE) * y_scales[0] * y_scales[0]
    gram = ring_fold(gram, send_x, jnp.add)[0]
    partial = flat(partial_cols(count, z_target, table_at, blocks, table))
    gram = ring_fold(gram, send_z, jnp.add)[0]

    rings = [(partial[:8], send_x, send_z), (partial[8:], send_z, send_x)]
    around = z_scales, z_scales
    messages = [[pack(v, z_scales) for v in values[:2]] for values, _, _ in rings]
    received = [[send(m[0], 1), send(m[1], -1)] for m, (_, send, _) in zip(messages, rings)]
    lower_factor = jnp.linalg.cholesky(gram)
    seconds = [
        ring_second(r, values[2:4], send, z_scales, *around)
        for r, (values, send, _) in zip(received, rings)
    ]
    thirds = []
    for (direct, sums, _), (values, _, send) in zip(seconds, rings):
        total = ring_total(direct, sums, [values[4:6], values[6:]], z_scales, *around)
        quarters = [total(r // 2, r % 2 * 4 * B, (r % 2 + 1) * 4 * B) for r in range(4)]
        thirds.append(ring_exchange(quarters, send, z_scales))
    inverse = lax.linalg.triangular_solve(
        lower_factor, jnp.eye(K, dtype=f32), left_side=True, lower=True
    )
    q_share = jnp.dot(y_share, inverse.T, precision=highest, preferred_element_type=f32)
    z_raw = jnp.concatenate([z for z, _ in thirds], axis=0)
    z_share = jnp.dot(z_raw, inverse.T, precision=highest, preferred_element_type=f32)
    row_scale = math.sqrt(BR * B * lax.axis_size("row"))
    return (q_share * row_scale, z_share[None])


def solution(mesh):
    in_specs = (
        P("row", "col", None, None, None),
        P("col", None),
        P("row", "col", None),
        P("row", "col", None),
        P("row", "col"),
    )
    out_specs = (P(("row", "col"), None), P("col", "row", None))
    return jax.shard_map(body, mesh=mesh, in_specs=in_specs, out_specs=out_specs, check_vma=False)
```

```python
import math

import jax
import jax.numpy as jnp
from jax import lax
from jax.experimental import pallas as pl
from jax.experimental.layout import Layout, with_layout_constraint
from jax.experimental.pallas import tpu as pltpu
from jax.sharding import PartitionSpec as P

B = 256
K = 128
BR = 128
BC = 128
NBLK = 96
CHUNK = 8
AHEAD = 28
GROUP = 4
BUFFERS = AHEAD + GROUP
VMEM_BYTES = 56 * 1024 * 1024
f32 = jnp.float32
f16 = jnp.float16


def ring(shift):
    return [(c, ((c // 2 + shift) % 4) * 2 + c % 2) for c in range(8)]


def along_x(shift):
    return [(r, ((r // 4 + shift) % 4) * 4 + r % 4) for r in range(16)]


def along_z(shift):
    return [(r, (r // 4) * 4 + (r % 4 + shift) % 4) for r in range(16)]


SHARE_ROWS = BR // 8 * B + 2 * K + BR // 8
LOW_SCALE = 2.0**15

PAIR = [(c, c ^ 1) for c in range(8)]


def run_slots(parts, count, targets, order, bounds, begin, group, carry, total_sum, outs, out_sems):
    chunks = total_sum.shape[0] // CHUNK

    def chunk_of(s):
        return jnp.where(targets[s] < 0, chunks, targets[s] // CHUNK)

    for c in range(chunks + 1):
        bounds[c] = 0

    def tally(s, _):
        c = chunk_of(s)
        bounds[c] = bounds[c] + 1
        return 0

    lax.fori_loop(0, count, tally, 0)
    total = 0
    for c in range(chunks):
        here = bounds[c]
        bounds[c] = total
        total = total + here
    bounds[chunks] = total

    def place(s, _):
        c = chunk_of(s)
        at = bounds[c]
        order[at] = s
        bounds[c] = at + 1
        return 0

    lax.fori_loop(0, count, place, 0)

    def begin_later(j):
        @pl.when(j < total)
        def _():
            begin(j, 0)

    lax.fori_loop(0, jnp.minimum(total, AHEAD), begin, 0)

    def clear(t, _):
        total_sum[t] = jnp.zeros((B, K), f32)
        return 0

    lax.fori_loop(0, chunks * CHUNK, clear, 0)

    writes = [[] for _ in range(chunks)]
    first = 0
    for ring_at in range(len(outs) // len(parts)):
        for i, tiles in enumerate(parts):
            at = ring_at * len(parts) + i
            for piece in range(0, tiles, CHUNK):
                size = min(CHUNK, tiles)
                sem = sum(len(w) for w in writes)
                writes[first // CHUNK].append(
                    pltpu.make_async_copy(
                        total_sum.at[pl.ds(first, size)],
                        outs[at].at[pl.ds(piece, size)],
                        out_sems.at[sem],
                    )
                )
                first += size

    def write_done(done, chunk):
        def step(c):
            for i, pieces in enumerate(writes):

                @pl.when(c == i)
                def _():
                    for copy in pieces:
                        copy.start()

            return c + 1

        return lax.while_loop(
            lambda c: (c < chunks) & (bounds[jnp.minimum(c, chunks - 1)] <= done), step, chunk
        )

    def by_group(size, first):
        def step(g, state):
            chunk, carry = state
            at = first + g * size
            carry = group(begin_later, at, size, carry)
            return write_done(at + size, chunk), carry

        return step

    groups = total // GROUP
    state = write_done(0, 0), carry
    state = lax.fori_loop(0, groups, by_group(GROUP, 0), state)
    state = lax.fori_loop(0, total - groups * GROUP, by_group(1, groups * GROUP), state)
    for pieces in writes:
        for copy in pieces:
            copy.wait()
    return state[1]


def y_kernel(count, targets, cols, blocks, sketch, *rest):
    outs, stat, scratch = rest[:3], rest[3], rest[4:]
    total_sum, order, bounds, block_buf, sketch_buf, sems, out_sems = scratch

    def copies(j):
        s, at = order[j], lax.rem(j, BUFFERS)
        return (
            pltpu.make_async_copy(blocks.at[s], block_buf.at[at], sems.at[0, at]),
            pltpu.make_async_copy(sketch.at[cols[s]], sketch_buf.at[at], sems.at[1, at]),
        )

    def begin(j, _):
        for copy in copies(j):
            copy.start()
        return 0

    def group(begin_later, at, size, carry):
        largest, largest_block = carry
        for u in range(size):
            begin_later(at + u + AHEAD)
        for u in range(size):
            for copy in copies(at + u):
                copy.wait()
        for u in range(size):
            target = targets[order[at + u]]
            buffer = lax.rem(at + u, BUFFERS)
            tile = block_buf[buffer]
            value = total_sum[target] + jnp.dot(
                tile, sketch_buf[buffer], preferred_element_type=f32
            )
            total_sum[target] = value
            largest = jnp.maximum(largest, jnp.max(jnp.abs(value).reshape(B // 8, 8, K), axis=0))
            largest_block = jnp.maximum(
                largest_block, jnp.max(jnp.abs(tile).reshape(B // 16, 16, B), axis=0)
            )
        return largest, largest_block

    carry = jnp.zeros((8, K), f32), jnp.zeros((16, B), jnp.bfloat16)
    largest, largest_block = run_slots(
        Y_PARTS, count[0], targets, order, bounds, begin, group, carry, total_sum, outs, out_sems
    )
    stat[:4] = jnp.full((4, K), jnp.max(largest))
    stat[4:] = jnp.full((4, K), jnp.max(largest_block.astype(f32)))


Y_PARTS = (32, 16, 16)
Z_PARTS = (16, 16, 8, 8, 4, 4, 4, 4)


def sums_of(parts):
    return tuple(jax.ShapeDtypeStruct((n, B, K), f32) for n in parts)


def scratch_for(halves, parts, y_type):
    return [
        pltpu.VMEM((halves * 8 * CHUNK, B, K), f32),
        pltpu.SMEM((NBLK + 1,), jnp.int32),
        pltpu.SMEM((halves * 8 + 1,), jnp.int32),
        pltpu.VMEM((BUFFERS, B, B), jnp.bfloat16),
        pltpu.VMEM((BUFFERS, B, K), y_type),
        pltpu.SemaphoreType.DMA((2, BUFFERS)),
        pltpu.SemaphoreType.DMA((halves * 10,)),
    ]


def partial_rows(count, targets, cols, blocks, sketch):
    return pl.pallas_call(
        y_kernel,
        out_shape=sums_of(Y_PARTS) + (jax.ShapeDtypeStruct((8, K), f32),),
        in_specs=[pl.BlockSpec(memory_space=pltpu.SMEM)] * 3
        + [pl.BlockSpec(memory_space=pl.ANY)] * 2,
        out_specs=(pl.BlockSpec(memory_space=pl.ANY),) * 3
        + (pl.BlockSpec(memory_space=pltpu.VMEM),),
        scratch_shapes=scratch_for(1, Y_PARTS, jnp.bfloat16),
        compiler_params=pltpu.CompilerParams(vmem_limit_bytes=VMEM_BYTES),
        cost_estimate=pl.CostEstimate(
            flops=NBLK * B * B * K, bytes_accessed=60 * 1024 * 1024, transcendentals=0
        ),
        name="partial_rows",
    )(count, targets, cols, blocks, sketch)


def table_row(row):
    return pl.multiple_of((row >> 4) * SHARE_ROWS + (row & 15) * B, 16)


def z_kernel(count, targets, rows, tile_scales, blocks, table, *rest):
    outs, scratch = rest[:16], rest[16:]
    total_sum, order, bounds, block_buf, y_buf, sems, out_sems = scratch

    def copies(j):
        s, at = order[j], lax.rem(j, BUFFERS)
        return (
            pltpu.make_async_copy(blocks.at[s], block_buf.at[at], sems.at[0, at]),
            pltpu.make_async_copy(
                table.at[pl.ds(table_row(rows[s]), B)], y_buf.at[at], sems.at[1, at]
            ),
        )

    def begin(j, _):
        for copy in copies(j):
            copy.start()
        return 0

    def group(begin_later, at, size, carry):
        for u in range(size):
            begin_later(at + u + AHEAD)
        for u in range(size):
            for copy in copies(at + u):
                copy.wait()
        for u in range(size):
            buffer = lax.rem(at + u, BUFFERS)
            value = y_buf[buffer].astype(f32)
            high = value.astype(jnp.bfloat16)
            low = (value - high.astype(f32)).astype(jnp.bfloat16)
            product = lax.dot_general(
                block_buf[buffer],
                jnp.concatenate([high, low], axis=1),
                (((0,), (0,)), ((), ())),
                preferred_element_type=f32,
            )
            slot = order[at + u]
            product = (product[:, :K] + product[:, K:]) * tile_scales[rows[slot]]
            total_sum[targets[slot]] += product
        return carry

    run_slots(
        Z_PARTS, count[0], targets, order, bounds, begin, group, 0, total_sum, outs, out_sems
    )


def partial_cols(count, targets, rows, tile_scales, blocks, table):
    return pl.pallas_call(
        z_kernel,
        out_shape=sums_of(Z_PARTS * 2),
        in_specs=[pl.BlockSpec(memory_space=pltpu.SMEM)] * 4
        + [pl.BlockSpec(memory_space=pl.ANY)] * 2,
        out_specs=(pl.BlockSpec(memory_space=pl.ANY),) * 16,
        scratch_shapes=scratch_for(2, Z_PARTS, jnp.int16),
        compiler_params=pltpu.CompilerParams(vmem_limit_bytes=VMEM_BYTES),
        cost_estimate=pl.CostEstimate(
            flops=NBLK * B * B * K * 4, bytes_accessed=42 * 1024 * 1024, transcendentals=0
        ),
        name="partial_cols",
    )(count, targets, rows, tile_scales, blocks, table)


def scales_for(bound):
    exponent = jnp.ceil(jnp.log2(jnp.maximum(bound, 1e-30))) - 15.0
    scale, inverse = lax.optimization_barrier((jnp.exp2(exponent), jnp.exp2(-exponent)))
    return scale[0, 0], inverse[0, 0]


def by_rows(value):
    return with_layout_constraint(value, Layout(tuple(range(value.ndim))))


def pack(value, scales):
    return by_rows((value * scales[1]).astype(f16))


def unpack(message, scales):
    return message.astype(f32) * scales[0]


PLACES = (6, 7, 4, 1, 0, 2, 3, 5)


HALF = CHUNK * B


def ring_first(messages, send):
    return lax.optimization_barrier((send(messages[0], 1), send(messages[1], -1)))


def ring_second(received, passing, send, scales, below, above):
    messages = lax.optimization_barrier(
        (
            pack(passing[0] + unpack(received[0][:HALF], below), scales),
            pack(passing[1] + unpack(received[1][:HALF], above), scales),
        )
    )
    sums = send(messages[0], 1), send(messages[1], -1)
    return lax.optimization_barrier((received, sums, messages))


def ring_total(received, sums, staying, scales, below, above):
    def total(which, start=0, stop=HALF):
        direct = received[1 - which][HALF + start : HALF + stop]
        return (
            staying[which][start // (stop - start)]
            + unpack(direct, below if which else above)
            + unpack(sums[which][start:stop], scales)
        )

    return total


def ring_exchange(parts, send, scales):
    messages = [pack(parts[r], scales) for r in (1, 3, 2)]
    up, down, across = (unpack(send(m, r), scales) for m, r in zip(messages, (1, 3, 2)))
    return parts[0] + up + down + across, messages


def exponent_of(largest):
    return jnp.floor(jnp.log2(jnp.maximum(largest, 1e-30))) - 14.0


def whole(value):
    return jnp.clip(jnp.round(value), -32767.0, 32767.0)


def after(value, other):
    return value + (0.0 * other[(0,) * other.ndim]).astype(value.dtype)


def ring_fold(value, send, op):
    across, below, above = send(value, 2), send(value, 1), send(value, -1)
    return op(op(value, across), op(below, above)), below, above


def body(blocks, sketch, block_row, block_col, counts):
    highest = lax.Precision.HIGHEST
    blocks = blocks[0, 0]
    rows, cols = block_row[0, 0], block_col[0, 0]
    count = counts[0, 0]
    row_at, col_at = lax.axis_index("row"), lax.axis_index("col")
    here_x, here_z = row_at // 4, row_at % 4
    here_y, core = col_at // 2, col_at % 2
    sketch_table = sketch.reshape(BC, B, K)

    def send_core(value):
        return lax.ppermute(value, "col", PAIR)

    def send_y(value, shift):
        return lax.ppermute(value, "col", ring(shift))

    def send_x(value, shift):
        return lax.ppermute(value, "row", along_x(shift))

    def send_z(value, shift):
        return lax.ppermute(value, "row", along_z(shift))

    live = jnp.arange(NBLK, dtype=jnp.int32) < count

    def chunk_of(rel, half):
        key = (rel & 3) * 2 + half
        chunk = PLACES[7]
        for k in range(7):
            chunk = jnp.where(key == k, PLACES[k], chunk)
        return chunk * CHUNK

    y_target = chunk_of((rows >> 5) - here_y, (rows >> 3) & 1) + (rows & 7)
    row_core = (rows >> 4) & 1
    rel_x, rel_z = ((cols >> 5) - here_x) & 3, ((cols >> 3) - here_z) & 3
    is_a = ((cols >> 2) & 1) == 0
    one, two = jnp.where(is_a, rel_x, rel_z), jnp.where(is_a, rel_z, rel_x)
    z_target = chunk_of(one, two >> 1) + (two & 1) * 4 + (cols & 3) + jnp.where(is_a, 0, 8 * CHUNK)
    other_target = jnp.where(live & (row_core != core), y_target, -1)
    own_target = jnp.where(live & (row_core == core), y_target, -1)
    z_target = jnp.where(live, z_target, -1)
    count = count[None]

    def flat(values):
        return [v.reshape(-1, K) for v in values]

    *other, other_stat = partial_rows(count, other_target, cols, blocks, sketch_table)
    *from_pair, pair_stat = [send_core(v) for v in (*other, other_stat)]
    *own, own_stat = partial_rows(count, own_target, cols, blocks, sketch_table)
    own, from_pair = flat(own), flat(from_pair)

    first_bound = own_stat + pair_stat
    scales = scales_for(first_bound[:1])
    own_first, pair_first = (v.reshape(2, 2 * HALF, K) for v in (own[0], from_pair[0]))
    first = [pack(own_first[i] + pair_first[i], scales) for i in range(2)]
    received = [send_y(first[0], 1), send_y(first[1], -1)]

    in_first = lax.broadcasted_iota(jnp.int32, (8, K), 0) < 4
    entries = jnp.maximum(own_stat, other_stat) * count[0].astype(f32)
    bounds, _ = lax.optimization_barrier((jnp.where(in_first, first_bound, entries), first))
    bounds, below, above = ring_fold(bounds, send_y, jnp.maximum)
    later, _ = lax.optimization_barrier(((own[1:], from_pair[1:]), bounds))
    parts = [
        [mine[at : at + HALF] + pair[at : at + HALF] for at in (0, HALF)] for mine, pair in zip(*later)
    ]
    passing, staying = lax.optimization_barrier(parts)
    around = scales_for(below[:1]), scales_for(above[:1])
    sum_scales = scales_for(bounds[:1] * 4.0)
    received, sums, messages = ring_second(received, passing, send_y, sum_scales, *around)
    y_part = ring_total(received, sums, [[v] for v in staying], sum_scales, *around)
    y_share = jnp.concatenate([y_part(0), y_part(1)], axis=0)

    bounds, _ = lax.optimization_barrier((bounds, messages))
    bounds = jnp.maximum(bounds, send_core(bounds))
    y_scales = scales_for(bounds[:1] * 4.0)
    bounds = ring_fold(ring_fold(bounds, send_x, jnp.maximum)[0], send_z, jnp.maximum)[0]
    z_scales = scales_for(bounds[:1] * bounds[4:5] * (4.0 * 16.0 * B))

    gram = jnp.dot(
        y_share.T, y_share, precision=lax.Precision.HIGH, preferred_element_type=f32
    )
    tiles = y_share.reshape(BR // 8, B, K)
    exponents = exponent_of(jnp.max(jnp.abs(tiles), axis=(1, 2)))
    gram_exponent = exponent_of(jnp.max(jnp.abs(gram)))
    codes = whole(tiles * jnp.exp2(-exponents)[:, None, None]).reshape(-1, K)
    gram = gram * jnp.exp2(-gram_exponent)
    high = whole(gram)
    low = whole((gram - high) * LOW_SCALE)
    in_first = lax.broadcasted_iota(jnp.int32, (BR // 8, K), 1) < K // 2
    scale_rows = jnp.where(in_first, exponents[:, None], gram_exponent)
    mine = jnp.concatenate([v.astype(jnp.int16) for v in (codes, high, low, scale_rows)], axis=0)
    mine, z_scales = lax.optimization_barrier((by_rows(mine), z_scales))
    gathered = lax.all_gather(mine, "col", axis=0, tiled=True)
    last = gathered.reshape(8, SHARE_ROWS, K)[:, BR // 8 * B :].astype(f32)
    tile_scales = jnp.exp2(last[:, 2 * K :, 0]).reshape(BR)
    gram_scales = jnp.exp2(last[:, 2 * K, K - 1])[:, None, None]
    gram = jnp.sum((last[:, :K] + last[:, K : 2 * K] * (1.0 / LOW_SCALE)) * gram_scales, axis=0)
    gram = ring_fold(gram, send_x, jnp.add)[0]
    partial = flat(partial_cols(count, z_target, rows, tile_scales, blocks, gathered))
    gram = ring_fold(gram, send_z, jnp.add)[0]

    rings = [(partial[:8], send_x, send_z), (partial[8:], send_z, send_x)]
    around = z_scales, z_scales
    messages = [[pack(v, z_scales) for v in values[:2]] for values, _, _ in rings]
    received = [[send(m[0], 1), send(m[1], -1)] for m, (_, send, _) in zip(messages, rings)]
    lower_factor = jnp.linalg.cholesky(gram)
    seconds = [
        ring_second(r, values[2:4], send, z_scales, *around)
        for r, (values, send, _) in zip(received, rings)
    ]
    thirds = []
    for (direct, sums, _), (values, _, send) in zip(seconds, rings):
        total = ring_total(direct, sums, [values[4:6], values[6:]], z_scales, *around)
        quarters = [total(r // 2, r % 2 * 4 * B, (r % 2 + 1) * 4 * B) for r in range(4)]
        thirds.append(ring_exchange(quarters, send, z_scales))
    inverse = lax.linalg.triangular_solve(
        lower_factor, jnp.eye(K, dtype=f32), left_side=True, lower=True
    )
    basis_factor = after(inverse, thirds[1][1][0])
    q_share = jnp.dot(y_share, basis_factor.T, precision=highest, preferred_element_type=f32)
    z_raw = jnp.concatenate([z for z, _ in thirds], axis=0)
    z_share = jnp.dot(z_raw, inverse.T, precision=highest, preferred_element_type=f32)
    row_scale = math.sqrt(BR * B * lax.axis_size("row"))
    return (q_share * row_scale, z_share[None])


def solution(mesh):
    in_specs = (
        P("row", "col", None, None, None),
        P("col", None),
        P("row", "col", None),
        P("row", "col", None),
        P("row", "col"),
    )
    out_specs = (P(("row", "col"), None), P("col", "row", None))
    return jax.shard_map(body, mesh=mesh, in_specs=in_specs, out_specs=out_specs, check_vma=False)
```

```python
import math

import jax
import jax.numpy as jnp
from jax import lax
from jax.experimental import pallas as pl
from jax.experimental.layout import Layout, with_layout_constraint
from jax.experimental.pallas import tpu as pltpu
from jax.sharding import PartitionSpec as P

B = 256
K = 128
BR = 128
BC = 128
NBLK = 96
CHUNK = 8
AHEAD = 28
GROUP = 4
BUFFERS = AHEAD + GROUP
VMEM_BYTES = 56 * 1024 * 1024
f32 = jnp.float32
f16 = jnp.float16


def ring(shift):
    return [(c, ((c // 2 + shift) % 4) * 2 + c % 2) for c in range(8)]


def along_x(shift):
    return [(r, ((r // 4 + shift) % 4) * 4 + r % 4) for r in range(16)]


def along_z(shift):
    return [(r, (r // 4) * 4 + (r % 4 + shift) % 4) for r in range(16)]


SHARE_ROWS = BR // 8 * B + 2 * K + 32
LOW_SCALE = 2.0**15

PAIR = [(c, c ^ 1) for c in range(8)]


def run_slots(parts, count, targets, order, bounds, begin, group, carry, total_sum, outs, out_sems):
    chunks = total_sum.shape[0] // CHUNK

    def chunk_of(s):
        return jnp.where(targets[s] < 0, chunks, targets[s] // CHUNK)

    for c in range(chunks + 1):
        bounds[c] = 0

    def tally(s, _):
        c = chunk_of(s)
        bounds[c] = bounds[c] + 1
        return 0

    lax.fori_loop(0, count, tally, 0)
    total = 0
    for c in range(chunks):
        here = bounds[c]
        bounds[c] = total
        total = total + here
    bounds[chunks] = total

    def place(s, _):
        c = chunk_of(s)
        at = bounds[c]
        order[at] = s
        bounds[c] = at + 1
        return 0

    lax.fori_loop(0, count, place, 0)

    def begin_later(j):
        @pl.when(j < total)
        def _():
            begin(j, 0)

    lax.fori_loop(0, jnp.minimum(total, AHEAD), begin, 0)

    def clear(t, _):
        total_sum[t] = jnp.zeros((B, K), f32)
        return 0

    lax.fori_loop(0, chunks * CHUNK, clear, 0)

    writes = [[] for _ in range(chunks)]
    first = 0
    for ring_at in range(len(outs) // len(parts)):
        for i, tiles in enumerate(parts):
            at = ring_at * len(parts) + i
            for piece in range(0, tiles, CHUNK):
                size = min(CHUNK, tiles)
                sem = sum(len(w) for w in writes)
                writes[first // CHUNK].append(
                    pltpu.make_async_copy(
                        total_sum.at[pl.ds(first, size)],
                        outs[at].at[pl.ds(piece, size)],
                        out_sems.at[sem],
                    )
                )
                first += size

    def write_done(done, chunk):
        def step(c):
            for i, pieces in enumerate(writes):

                @pl.when(c == i)
                def _():
                    for copy in pieces:
                        copy.start()

            return c + 1

        return lax.while_loop(
            lambda c: (c < chunks) & (bounds[jnp.minimum(c, chunks - 1)] <= done), step, chunk
        )

    def by_group(size, first):
        def step(g, state):
            chunk, carry = state
            at = first + g * size
            carry = group(begin_later, at, size, carry)
            return write_done(at + size, chunk), carry

        return step

    groups = total // GROUP
    state = write_done(0, 0), carry
    state = lax.fori_loop(0, groups, by_group(GROUP, 0), state)
    state = lax.fori_loop(0, total - groups * GROUP, by_group(1, groups * GROUP), state)
    for pieces in writes:
        for copy in pieces:
            copy.wait()
    return state[1]


def y_kernel(count, targets, cols, blocks, sketch, *rest):
    outs, stat, scratch = rest[:3], rest[3], rest[4:]
    total_sum, order, bounds, block_buf, sketch_buf, sems, out_sems = scratch

    def copies(j):
        s, at = order[j], lax.rem(j, BUFFERS)
        return (
            pltpu.make_async_copy(blocks.at[s], block_buf.at[at], sems.at[0, at]),
            pltpu.make_async_copy(sketch.at[cols[s]], sketch_buf.at[at], sems.at[1, at]),
        )

    def begin(j, _):
        for copy in copies(j):
            copy.start()
        return 0

    def group(begin_later, at, size, carry):
        largest, largest_block = carry
        for u in range(size):
            begin_later(at + u + AHEAD)
        for u in range(size):
            for copy in copies(at + u):
                copy.wait()
        for u in range(size):
            target = targets[order[at + u]]
            buffer = lax.rem(at + u, BUFFERS)
            tile = block_buf[buffer]
            value = total_sum[target] + jnp.dot(
                tile, sketch_buf[buffer], preferred_element_type=f32
            )
            total_sum[target] = value
            largest = jnp.maximum(largest, jnp.max(jnp.abs(value).reshape(B // 8, 8, K), axis=0))
            largest_block = jnp.maximum(
                largest_block, jnp.max(jnp.abs(tile).reshape(B // 16, 16, B), axis=0)
            )
        return largest, largest_block

    carry = jnp.zeros((8, K), f32), jnp.zeros((16, B), jnp.bfloat16)
    largest, largest_block = run_slots(
        Y_PARTS, count[0], targets, order, bounds, begin, group, carry, total_sum, outs, out_sems
    )
    stat[:4] = jnp.full((4, K), jnp.max(largest))
    stat[4:] = jnp.full((4, K), jnp.max(largest_block.astype(f32)))


Y_PARTS = (32, 16, 16)
Z_PARTS = (16, 16, 8, 8, 4, 4, 4, 4)


def sums_of(parts):
    return tuple(jax.ShapeDtypeStruct((n, B, K), f32) for n in parts)


def scratch_for(halves, parts, y_type):
    return [
        pltpu.VMEM((halves * 8 * CHUNK, B, K), f32),
        pltpu.SMEM((NBLK + 1,), jnp.int32),
        pltpu.SMEM((halves * 8 + 1,), jnp.int32),
        pltpu.VMEM((BUFFERS, B, B), jnp.bfloat16),
        pltpu.VMEM((BUFFERS, B, K), y_type),
        pltpu.SemaphoreType.DMA((2, BUFFERS)),
        pltpu.SemaphoreType.DMA((halves * 10,)),
    ]


def partial_rows(count, targets, cols, blocks, sketch):
    return pl.pallas_call(
        y_kernel,
        out_shape=sums_of(Y_PARTS) + (jax.ShapeDtypeStruct((8, K), f32),),
        in_specs=[pl.BlockSpec(memory_space=pltpu.SMEM)] * 3
        + [pl.BlockSpec(memory_space=pl.ANY)] * 2,
        out_specs=(pl.BlockSpec(memory_space=pl.ANY),) * 3
        + (pl.BlockSpec(memory_space=pltpu.VMEM),),
        scratch_shapes=scratch_for(1, Y_PARTS, jnp.bfloat16),
        compiler_params=pltpu.CompilerParams(vmem_limit_bytes=VMEM_BYTES),
        cost_estimate=pl.CostEstimate(
            flops=NBLK * B * B * K, bytes_accessed=60 * 1024 * 1024, transcendentals=0
        ),
        name="partial_rows",
    )(count, targets, cols, blocks, sketch)


def table_row(row):
    return pl.multiple_of((row >> 4) * SHARE_ROWS + (row & 15) * B, 16)


def share_kernel(gathered, gram, scales, buffer, sems):
    copies = [
        pltpu.make_async_copy(
            gathered.at[pl.ds(c * SHARE_ROWS + BR // 8 * B, 2 * K + 32)], buffer.at[c], sems.at[c]
        )
        for c in range(8)
    ]
    for copy in copies:
        copy.start()
    total = jnp.zeros((K, K), f32)
    for c, copy in enumerate(copies):
        copy.wait()
        scale = jnp.exp2(buffer[c, 2 * K : 2 * K + 32].astype(f32))
        scales[c * 16 : (c + 1) * 16] = scale[:16]
        high, low = buffer[c, :K].astype(f32), buffer[c, K : 2 * K].astype(f32)
        total += (high + low * (1.0 / LOW_SCALE)) * scale[16:17]
    gram[...] = total


def read_shares(gathered):
    return pl.pallas_call(
        share_kernel,
        out_shape=(jax.ShapeDtypeStruct((K, K), f32), jax.ShapeDtypeStruct((BR, K), f32)),
        in_specs=[pl.BlockSpec(memory_space=pl.ANY)],
        out_specs=(pl.BlockSpec(memory_space=pltpu.VMEM),) * 2,
        scratch_shapes=[
            pltpu.VMEM((8, 2 * K + 32, K), jnp.int16),
            pltpu.SemaphoreType.DMA((8,)),
        ],
        compiler_params=pltpu.CompilerParams(vmem_limit_bytes=VMEM_BYTES),
        name="read_shares",
    )(gathered)


def z_kernel(count, targets, rows, blocks, table, tile_scales, *rest):
    outs, scratch = rest[:16], rest[16:]
    total_sum, order, bounds, block_buf, y_buf, sems, out_sems = scratch

    def copies(j):
        s, at = order[j], lax.rem(j, BUFFERS)
        return (
            pltpu.make_async_copy(blocks.at[s], block_buf.at[at], sems.at[0, at]),
            pltpu.make_async_copy(
                table.at[pl.ds(table_row(rows[s]), B)], y_buf.at[at], sems.at[1, at]
            ),
        )

    def begin(j, _):
        for copy in copies(j):
            copy.start()
        return 0

    def group(begin_later, at, size, carry):
        for u in range(size):
            begin_later(at + u + AHEAD)
        for u in range(size):
            for copy in copies(at + u):
                copy.wait()
        for u in range(size):
            buffer = lax.rem(at + u, BUFFERS)
            value = y_buf[buffer].astype(f32)
            high = value.astype(jnp.bfloat16)
            low = (value - high.astype(f32)).astype(jnp.bfloat16)
            product = lax.dot_general(
                block_buf[buffer],
                jnp.concatenate([high, low], axis=1),
                (((0,), (0,)), ((), ())),
                preferred_element_type=f32,
            )
            slot = order[at + u]
            product = (product[:, :K] + product[:, K:]) * tile_scales[pl.ds(rows[slot], 1)]
            total_sum[targets[slot]] += product
        return carry

    run_slots(
        Z_PARTS, count[0], targets, order, bounds, begin, group, 0, total_sum, outs, out_sems
    )


def partial_cols(count, targets, rows, blocks, table, tile_scales):
    return pl.pallas_call(
        z_kernel,
        out_shape=sums_of(Z_PARTS * 2),
        in_specs=[pl.BlockSpec(memory_space=pltpu.SMEM)] * 3
        + [pl.BlockSpec(memory_space=pl.ANY)] * 2
        + [pl.BlockSpec(memory_space=pltpu.VMEM)],
        out_specs=(pl.BlockSpec(memory_space=pl.ANY),) * 16,
        scratch_shapes=scratch_for(2, Z_PARTS, jnp.int16),
        compiler_params=pltpu.CompilerParams(vmem_limit_bytes=VMEM_BYTES),
        cost_estimate=pl.CostEstimate(
            flops=NBLK * B * B * K * 4, bytes_accessed=42 * 1024 * 1024, transcendentals=0
        ),
        name="partial_cols",
    )(count, targets, rows, blocks, table, tile_scales)


def scales_for(bound):
    exponent = jnp.ceil(jnp.log2(jnp.maximum(bound, 1e-30))) - 15.0
    scale, inverse = lax.optimization_barrier((jnp.exp2(exponent), jnp.exp2(-exponent)))
    return scale[0, 0], inverse[0, 0]


def by_rows(value):
    return with_layout_constraint(value, Layout(tuple(range(value.ndim))))


def pack(value, scales):
    return by_rows((value * scales[1]).astype(f16))


def unpack(message, scales):
    return message.astype(f32) * scales[0]


PLACES = (6, 7, 4, 1, 0, 2, 3, 5)


HALF = CHUNK * B


def ring_first(messages, send):
    return lax.optimization_barrier((send(messages[0], 1), send(messages[1], -1)))


def ring_second(received, passing, send, scales, below, above):
    messages = lax.optimization_barrier(
        (
            pack(passing[0] + unpack(received[0][:HALF], below), scales),
            pack(passing[1] + unpack(received[1][:HALF], above), scales),
        )
    )
    sums = send(messages[0], 1), send(messages[1], -1)
    return lax.optimization_barrier((received, sums, messages))


def ring_total(received, sums, staying, scales, below, above):
    def total(which, start=0, stop=HALF):
        direct = received[1 - which][HALF + start : HALF + stop]
        return (
            staying[which][start // (stop - start)]
            + unpack(direct, below if which else above)
            + unpack(sums[which][start:stop], scales)
        )

    return total


def ring_exchange(parts, send, scales):
    messages = [pack(parts[r], scales) for r in (1, 3, 2)]
    up, down, across = (unpack(send(m, r), scales) for m, r in zip(messages, (1, 3, 2)))
    return parts[0] + up + down + across, messages


def exponent_of(largest):
    return jnp.floor(jnp.log2(jnp.maximum(largest, 1e-30))) - 14.0


def whole(value):
    return jnp.clip(jnp.round(value), -32767.0, 32767.0)


def after(value, other):
    return value + (0.0 * other[(0,) * other.ndim]).astype(value.dtype)


def ring_fold(value, send, op):
    across, below, above = send(value, 2), send(value, 1), send(value, -1)
    return op(op(value, across), op(below, above)), below, above


def body(blocks, sketch, block_row, block_col, counts):
    highest = lax.Precision.HIGHEST
    blocks = blocks[0, 0]
    rows, cols = block_row[0, 0], block_col[0, 0]
    count = counts[0, 0]
    row_at, col_at = lax.axis_index("row"), lax.axis_index("col")
    here_x, here_z = row_at // 4, row_at % 4
    here_y, core = col_at // 2, col_at % 2
    sketch_table = sketch.reshape(BC, B, K)

    def send_core(value):
        return lax.ppermute(value, "col", PAIR)

    def send_y(value, shift):
        return lax.ppermute(value, "col", ring(shift))

    def send_x(value, shift):
        return lax.ppermute(value, "row", along_x(shift))

    def send_z(value, shift):
        return lax.ppermute(value, "row", along_z(shift))

    live = jnp.arange(NBLK, dtype=jnp.int32) < count

    def chunk_of(rel, half):
        key = (rel & 3) * 2 + half
        chunk = PLACES[7]
        for k in range(7):
            chunk = jnp.where(key == k, PLACES[k], chunk)
        return chunk * CHUNK

    y_target = chunk_of((rows >> 5) - here_y, (rows >> 3) & 1) + (rows & 7)
    row_core = (rows >> 4) & 1
    rel_x, rel_z = ((cols >> 5) - here_x) & 3, ((cols >> 3) - here_z) & 3
    is_a = ((cols >> 2) & 1) == 0
    one, two = jnp.where(is_a, rel_x, rel_z), jnp.where(is_a, rel_z, rel_x)
    z_target = chunk_of(one, two >> 1) + (two & 1) * 4 + (cols & 3) + jnp.where(is_a, 0, 8 * CHUNK)
    other_target = jnp.where(live & (row_core != core), y_target, -1)
    own_target = jnp.where(live & (row_core == core), y_target, -1)
    z_target = jnp.where(live, z_target, -1)
    count = count[None]

    def flat(values):
        return [v.reshape(-1, K) for v in values]

    *other, other_stat = partial_rows(count, other_target, cols, blocks, sketch_table)
    *from_pair, pair_stat = [send_core(v) for v in (*other, other_stat)]
    *own, own_stat = partial_rows(count, own_target, cols, blocks, sketch_table)
    own, from_pair = flat(own), flat(from_pair)

    first_bound = own_stat + pair_stat
    scales = scales_for(first_bound[:1])
    own_first, pair_first = (v.reshape(2, 2 * HALF, K) for v in (own[0], from_pair[0]))
    first = [pack(own_first[i] + pair_first[i], scales) for i in range(2)]
    received = [send_y(first[0], 1), send_y(first[1], -1)]

    in_first = lax.broadcasted_iota(jnp.int32, (8, K), 0) < 4
    entries = jnp.maximum(own_stat, other_stat) * count[0].astype(f32)
    bounds, _ = lax.optimization_barrier((jnp.where(in_first, first_bound, entries), first))
    bounds, below, above = ring_fold(bounds, send_y, jnp.maximum)
    later, _ = lax.optimization_barrier(((own[1:], from_pair[1:]), bounds))
    parts = [
        [mine[at : at + HALF] + pair[at : at + HALF] for at in (0, HALF)] for mine, pair in zip(*later)
    ]
    passing, staying = lax.optimization_barrier(parts)
    around = scales_for(below[:1]), scales_for(above[:1])
    sum_scales = scales_for(bounds[:1] * 4.0)
    received, sums, messages = ring_second(received, passing, send_y, sum_scales, *around)
    y_part = ring_total(received, sums, [[v] for v in staying], sum_scales, *around)
    y_share = jnp.concatenate([y_part(0), y_part(1)], axis=0)

    bounds, _ = lax.optimization_barrier((bounds, messages))
    bounds = jnp.maximum(bounds, send_core(bounds))
    y_scales = scales_for(bounds[:1] * 4.0)
    bounds = ring_fold(ring_fold(bounds, send_x, jnp.maximum)[0], send_z, jnp.maximum)[0]
    z_scales = scales_for(bounds[:1] * bounds[4:5] * (4.0 * 16.0 * B))

    gram = jnp.dot(
        y_share.T, y_share, precision=lax.Precision.HIGH, preferred_element_type=f32
    )
    tiles = y_share.reshape(BR // 8, B, K)
    exponents = exponent_of(jnp.max(jnp.abs(tiles), axis=(1, 2)))
    gram_exponent = exponent_of(jnp.max(jnp.abs(gram)))
    codes = whole(tiles * jnp.exp2(-exponents)[:, None, None]).reshape(-1, K)
    gram = gram * jnp.exp2(-gram_exponent)
    high = whole(gram)
    low = whole((gram - high) * LOW_SCALE)
    scale_rows = jnp.concatenate([exponents, jnp.full((16,), gram_exponent)])
    scale_rows = jnp.broadcast_to(scale_rows[:, None], (32, K))
    mine = jnp.concatenate([v.astype(jnp.int16) for v in (codes, high, low, scale_rows)], axis=0)
    mine, z_scales = lax.optimization_barrier((by_rows(mine), z_scales))
    gathered = lax.all_gather(mine, "col", axis=0, tiled=True)
    gram, tile_scales = read_shares(gathered)
    gram = ring_fold(gram, send_x, jnp.add)[0]
    partial = flat(partial_cols(count, z_target, rows, blocks, gathered, tile_scales))
    gram = ring_fold(gram, send_z, jnp.add)[0]

    rings = [(partial[:8], send_x, send_z), (partial[8:], send_z, send_x)]
    around = z_scales, z_scales
    scales_each = [z_scales, (z_scales[0], after(z_scales[1], gram))]
    messages = [
        [pack(v, scales) for v in values[:2]] for (values, _, _), scales in zip(rings, scales_each)
    ]
    received = [[send(m[0], 1), send(m[1], -1)] for m, (_, send, _) in zip(messages, rings)]
    lower_factor = jnp.linalg.cholesky(gram)
    seconds = [
        ring_second(r, values[2:4], send, z_scales, *around)
        for r, (values, send, _) in zip(received, rings)
    ]
    thirds = []
    for (direct, sums, _), (values, _, send) in zip(seconds, rings):
        total = ring_total(direct, sums, [values[4:6], values[6:]], z_scales, *around)
        quarters = [total(r // 2, r % 2 * 4 * B, (r % 2 + 1) * 4 * B) for r in range(4)]
        thirds.append(ring_exchange(quarters, send, z_scales))
    inverse = lax.linalg.triangular_solve(
        lower_factor, jnp.eye(K, dtype=f32), left_side=True, lower=True
    )
    q_share = jnp.dot(y_share, inverse.T, precision=highest, preferred_element_type=f32)
    z_raw = jnp.concatenate([z for z, _ in thirds], axis=0)
    z_share = jnp.dot(z_raw, inverse.T, precision=highest, preferred_element_type=f32)
    row_scale = math.sqrt(BR * B * lax.axis_size("row"))
    return (q_share * row_scale, z_share[None])


def solution(mesh):
    in_specs = (
        P("row", "col", None, None, None),
        P("col", None),
        P("row", "col", None),
        P("row", "col", None),
        P("row", "col"),
    )
    out_specs = (P(("row", "col"), None), P("col", "row", None))
    return jax.shard_map(body, mesh=mesh, in_specs=in_specs, out_specs=out_specs, check_vma=False)
```

```python
import math

import jax
import jax.numpy as jnp
from jax import lax
from jax.experimental import pallas as pl
from jax.experimental.layout import Layout, with_layout_constraint
from jax.experimental.pallas import tpu as pltpu
from jax.sharding import PartitionSpec as P

B = 256
K = 128
BR = 128
BC = 128
NBLK = 96
CHUNK = 8
AHEAD = 28
GROUP = 4
BUFFERS = AHEAD + GROUP
VMEM_BYTES = 56 * 1024 * 1024
f32 = jnp.float32
f16 = jnp.float16


def ring(shift):
    return [(c, ((c // 2 + shift) % 4) * 2 + c % 2) for c in range(8)]


def along_x(shift):
    return [(r, ((r // 4 + shift) % 4) * 4 + r % 4) for r in range(16)]


def along_z(shift):
    return [(r, (r // 4) * 4 + (r % 4 + shift) % 4) for r in range(16)]


SHARE_ROWS = BR // 8 * B + 2 * K + 32
LOW_SCALE = 2.0**15

PAIR = [(c, c ^ 1) for c in range(8)]


def run_slots(parts, count, targets, order, bounds, begin, group, carry, total_sum, outs, out_sems):
    chunks = total_sum.shape[0] // CHUNK

    def chunk_of(s):
        return jnp.where(targets[s] < 0, chunks, targets[s] // CHUNK)

    for c in range(chunks + 1):
        bounds[c] = 0

    def tally(s, _):
        c = chunk_of(s)
        bounds[c] = bounds[c] + 1
        return 0

    lax.fori_loop(0, count, tally, 0)
    total = 0
    for c in range(chunks):
        here = bounds[c]
        bounds[c] = total
        total = total + here
    bounds[chunks] = total

    def place(s, _):
        c = chunk_of(s)
        at = bounds[c]
        order[at] = s
        bounds[c] = at + 1
        return 0

    lax.fori_loop(0, count, place, 0)

    def begin_later(j):
        @pl.when(j < total)
        def _():
            begin(j, 0)

    lax.fori_loop(0, jnp.minimum(total, AHEAD), begin, 0)

    def clear(t, _):
        total_sum[t] = jnp.zeros((B, K), f32)
        return 0

    lax.fori_loop(0, chunks * CHUNK, clear, 0)

    writes = [[] for _ in range(chunks)]
    first = 0
    for ring_at in range(len(outs) // len(parts)):
        for i, tiles in enumerate(parts):
            at = ring_at * len(parts) + i
            for piece in range(0, tiles, CHUNK):
                size = min(CHUNK, tiles)
                sem = sum(len(w) for w in writes)
                writes[first // CHUNK].append(
                    pltpu.make_async_copy(
                        total_sum.at[pl.ds(first, size)],
                        outs[at].at[pl.ds(piece, size)],
                        out_sems.at[sem],
                    )
                )
                first += size

    def write_done(done, chunk):
        def step(c):
            for i, pieces in enumerate(writes):

                @pl.when(c == i)
                def _():
                    for copy in pieces:
                        copy.start()

            return c + 1

        return lax.while_loop(
            lambda c: (c < chunks) & (bounds[jnp.minimum(c, chunks - 1)] <= done), step, chunk
        )

    def by_group(size, first):
        def step(g, state):
            chunk, carry = state
            at = first + g * size
            carry = group(begin_later, at, size, carry)
            return write_done(at + size, chunk), carry

        return step

    groups = total // GROUP
    state = write_done(0, 0), carry
    state = lax.fori_loop(0, groups, by_group(GROUP, 0), state)
    state = lax.fori_loop(0, total - groups * GROUP, by_group(1, groups * GROUP), state)
    for pieces in writes:
        for copy in pieces:
            copy.wait()
    return state[1]


def y_kernel(count, targets, cols, blocks, sketch, *rest):
    outs, stat, scratch = rest[:3], rest[3], rest[4:]
    total_sum, order, bounds, block_buf, sketch_buf, sems, out_sems = scratch

    def copies(j):
        s, at = order[j], lax.rem(j, BUFFERS)
        return (
            pltpu.make_async_copy(blocks.at[s], block_buf.at[at], sems.at[0, at]),
            pltpu.make_async_copy(sketch.at[cols[s]], sketch_buf.at[at], sems.at[1, at]),
        )

    def begin(j, _):
        for copy in copies(j):
            copy.start()
        return 0

    def group(begin_later, at, size, carry):
        largest, largest_block = carry
        for u in range(size):
            begin_later(at + u + AHEAD)
        for u in range(size):
            for copy in copies(at + u):
                copy.wait()
        for u in range(size):
            target = targets[order[at + u]]
            buffer = lax.rem(at + u, BUFFERS)
            tile = block_buf[buffer]
            value = total_sum[target] + jnp.dot(
                tile, sketch_buf[buffer], preferred_element_type=f32
            )
            total_sum[target] = value
            largest = jnp.maximum(largest, jnp.max(jnp.abs(value).reshape(B // 8, 8, K), axis=0))
            largest_block = jnp.maximum(
                largest_block, jnp.max(jnp.abs(tile).reshape(B // 16, 16, B), axis=0)
            )
        return largest, largest_block

    carry = jnp.zeros((8, K), f32), jnp.zeros((16, B), jnp.bfloat16)
    largest, largest_block = run_slots(
        Y_PARTS, count[0], targets, order, bounds, begin, group, carry, total_sum, outs, out_sems
    )
    stat[:4] = jnp.full((4, K), jnp.max(largest))
    stat[4:] = jnp.full((4, K), jnp.max(largest_block.astype(f32)))


Y_PARTS = (32, 16, 16)
Z_PARTS = (16, 16, 8, 8, 4, 4, 4, 4)


def sums_of(parts):
    return tuple(jax.ShapeDtypeStruct((n, B, K), f32) for n in parts)


def scratch_for(halves, parts, y_type):
    return [
        pltpu.VMEM((halves * 8 * CHUNK, B, K), f32),
        pltpu.SMEM((NBLK + 1,), jnp.int32),
        pltpu.SMEM((halves * 8 + 1,), jnp.int32),
        pltpu.VMEM((BUFFERS, B, B), jnp.bfloat16),
        pltpu.VMEM((BUFFERS, B, K), y_type),
        pltpu.SemaphoreType.DMA((2, BUFFERS)),
        pltpu.SemaphoreType.DMA((halves * 10,)),
    ]


def partial_rows(count, targets, cols, blocks, sketch):
    return pl.pallas_call(
        y_kernel,
        out_shape=sums_of(Y_PARTS) + (jax.ShapeDtypeStruct((8, K), f32),),
        in_specs=[pl.BlockSpec(memory_space=pltpu.SMEM)] * 3
        + [pl.BlockSpec(memory_space=pl.ANY)] * 2,
        out_specs=(pl.BlockSpec(memory_space=pl.ANY),) * 3
        + (pl.BlockSpec(memory_space=pltpu.VMEM),),
        scratch_shapes=scratch_for(1, Y_PARTS, jnp.bfloat16),
        compiler_params=pltpu.CompilerParams(vmem_limit_bytes=VMEM_BYTES),
        cost_estimate=pl.CostEstimate(
            flops=NBLK * B * B * K, bytes_accessed=60 * 1024 * 1024, transcendentals=0
        ),
        name="partial_rows",
    )(count, targets, cols, blocks, sketch)


def table_row(row):
    return pl.multiple_of((row >> 4) * SHARE_ROWS + (row & 15) * B, 16)


def share_kernel(gathered, gram, scales, buffer, sems):
    copies = [
        pltpu.make_async_copy(
            gathered.at[pl.ds(c * SHARE_ROWS + BR // 8 * B, 2 * K + 32)], buffer.at[c], sems.at[c]
        )
        for c in range(8)
    ]
    for copy in copies:
        copy.start()
    total = jnp.zeros((K, K), f32)
    for c, copy in enumerate(copies):
        copy.wait()
        scale = jnp.exp2(buffer[c, 2 * K : 2 * K + 32].astype(f32))
        scales[c * 16 : (c + 1) * 16] = scale[:16]
        high, low = buffer[c, :K].astype(f32), buffer[c, K : 2 * K].astype(f32)
        total += (high + low * (1.0 / LOW_SCALE)) * scale[16:17]
    gram[...] = total


def read_shares(gathered):
    return pl.pallas_call(
        share_kernel,
        out_shape=(jax.ShapeDtypeStruct((K, K), f32), jax.ShapeDtypeStruct((BR, K), f32)),
        in_specs=[pl.BlockSpec(memory_space=pl.ANY)],
        out_specs=(pl.BlockSpec(memory_space=pltpu.VMEM),) * 2,
        scratch_shapes=[
            pltpu.VMEM((8, 2 * K + 32, K), jnp.int16),
            pltpu.SemaphoreType.DMA((8,)),
        ],
        compiler_params=pltpu.CompilerParams(vmem_limit_bytes=VMEM_BYTES),
        name="read_shares",
    )(gathered)


def z_kernel(count, targets, rows, blocks, table, tile_scales, *rest):
    outs, scratch = rest[:16], rest[16:]
    total_sum, order, bounds, block_buf, y_buf, sems, out_sems = scratch

    def copies(j):
        s, at = order[j], lax.rem(j, BUFFERS)
        return (
            pltpu.make_async_copy(blocks.at[s], block_buf.at[at], sems.at[0, at]),
            pltpu.make_async_copy(
                table.at[pl.ds(table_row(rows[s]), B)], y_buf.at[at], sems.at[1, at]
            ),
        )

    def begin(j, _):
        for copy in copies(j):
            copy.start()
        return 0

    def group(begin_later, at, size, carry):
        for u in range(size):
            begin_later(at + u + AHEAD)
        for u in range(size):
            for copy in copies(at + u):
                copy.wait()
        for u in range(size):
            buffer = lax.rem(at + u, BUFFERS)
            value = y_buf[buffer].astype(f32)
            high = value.astype(jnp.bfloat16)
            low = (value - high.astype(f32)).astype(jnp.bfloat16)
            product = lax.dot_general(
                block_buf[buffer],
                jnp.concatenate([high, low], axis=1),
                (((0,), (0,)), ((), ())),
                preferred_element_type=f32,
            )
            slot = order[at + u]
            product = (product[:, :K] + product[:, K:]) * tile_scales[pl.ds(rows[slot], 1)]
            total_sum[targets[slot]] += product
        return carry

    run_slots(
        Z_PARTS, count[0], targets, order, bounds, begin, group, 0, total_sum, outs, out_sems
    )


def partial_cols(count, targets, rows, blocks, table, tile_scales):
    return pl.pallas_call(
        z_kernel,
        out_shape=sums_of(Z_PARTS * 2),
        in_specs=[pl.BlockSpec(memory_space=pltpu.SMEM)] * 3
        + [pl.BlockSpec(memory_space=pl.ANY)] * 2
        + [pl.BlockSpec(memory_space=pltpu.VMEM)],
        out_specs=(pl.BlockSpec(memory_space=pl.ANY),) * 16,
        scratch_shapes=scratch_for(2, Z_PARTS, jnp.int16),
        compiler_params=pltpu.CompilerParams(vmem_limit_bytes=VMEM_BYTES),
        cost_estimate=pl.CostEstimate(
            flops=NBLK * B * B * K * 4, bytes_accessed=42 * 1024 * 1024, transcendentals=0
        ),
        name="partial_cols",
    )(count, targets, rows, blocks, table, tile_scales)


def scales_for(bound):
    exponent = jnp.ceil(jnp.log2(jnp.maximum(bound, 1e-30))) - 15.0
    scale, inverse = lax.optimization_barrier((jnp.exp2(exponent), jnp.exp2(-exponent)))
    return scale[0, 0], inverse[0, 0]


def by_rows(value):
    return with_layout_constraint(value, Layout(tuple(range(value.ndim))))


def pack(value, scales):
    return by_rows((value * scales[1]).astype(f16))


def unpack(message, scales):
    return message.astype(f32) * scales[0]


PLACES = (6, 7, 4, 1, 0, 2, 3, 5)


HALF = CHUNK * B


def ring_first(messages, send):
    return lax.optimization_barrier((send(messages[0], 1), send(messages[1], -1)))


def ring_second(received, passing, send, scales, below, above):
    messages = lax.optimization_barrier(
        (
            pack(passing[0] + unpack(received[0][:HALF], below), scales),
            pack(passing[1] + unpack(received[1][:HALF], above), scales),
        )
    )
    sums = send(messages[0], 1), send(messages[1], -1)
    return lax.optimization_barrier((received, sums, messages))


def ring_total(received, sums, staying, scales, below, above):
    def total(which, start=0, stop=HALF):
        direct = received[1 - which][HALF + start : HALF + stop]
        return (
            staying[which][start // (stop - start)]
            + unpack(direct, below if which else above)
            + unpack(sums[which][start:stop], scales)
        )

    return total


def ring_exchange(parts, send, scales):
    messages = [pack(parts[r], scales) for r in (1, 3, 2)]
    up, down, across = (unpack(send(m, r), scales) for m, r in zip(messages, (1, 3, 2)))
    return parts[0] + up + down + across, messages


def exponent_of(largest):
    return jnp.floor(jnp.log2(jnp.maximum(largest, 1e-30))) - 14.0


def whole(value):
    return jnp.clip(jnp.round(value), -32767.0, 32767.0)


def after(value, other):
    return value + (0.0 * other[(0,) * other.ndim]).astype(value.dtype)


def ring_fold(value, send, op):
    across, below, above = send(value, 2), send(value, 1), send(value, -1)
    return op(op(value, across), op(below, above)), below, above


def body(blocks, sketch, block_row, block_col, counts):
    highest = lax.Precision.HIGHEST
    blocks = blocks[0, 0]
    rows, cols = block_row[0, 0], block_col[0, 0]
    count = counts[0, 0]
    row_at, col_at = lax.axis_index("row"), lax.axis_index("col")
    here_x, here_z = row_at // 4, row_at % 4
    here_y, core = col_at // 2, col_at % 2
    sketch_table = sketch.reshape(BC, B, K)

    def send_core(value):
        return lax.ppermute(value, "col", PAIR)

    def send_y(value, shift):
        return lax.ppermute(value, "col", ring(shift))

    def send_x(value, shift):
        return lax.ppermute(value, "row", along_x(shift))

    def send_z(value, shift):
        return lax.ppermute(value, "row", along_z(shift))

    live = jnp.arange(NBLK, dtype=jnp.int32) < count

    def chunk_of(rel, half):
        key = (rel & 3) * 2 + half
        chunk = PLACES[7]
        for k in range(7):
            chunk = jnp.where(key == k, PLACES[k], chunk)
        return chunk * CHUNK

    y_target = chunk_of((rows >> 5) - here_y, (rows >> 3) & 1) + (rows & 7)
    row_core = (rows >> 4) & 1
    rel_x, rel_z = ((cols >> 5) - here_x) & 3, ((cols >> 3) - here_z) & 3
    is_a = ((cols >> 2) & 1) == 0
    one, two = jnp.where(is_a, rel_x, rel_z), jnp.where(is_a, rel_z, rel_x)
    z_target = chunk_of(one, two >> 1) + (two & 1) * 4 + (cols & 3) + jnp.where(is_a, 0, 8 * CHUNK)
    other_target = jnp.where(live & (row_core != core), y_target, -1)
    own_target = jnp.where(live & (row_core == core), y_target, -1)
    z_target = jnp.where(live, z_target, -1)
    count = count[None]

    def flat(values):
        return [v.reshape(-1, K) for v in values]

    *other, other_stat = partial_rows(count, other_target, cols, blocks, sketch_table)
    *from_pair, pair_stat = [send_core(v) for v in (*other, other_stat)]
    *own, own_stat = partial_rows(count, own_target, cols, blocks, sketch_table)
    own, from_pair = flat(own), flat(from_pair)

    first_bound = own_stat + pair_stat
    scales = scales_for(first_bound[:1])
    own_first, pair_first = (v.reshape(2, 2 * HALF, K) for v in (own[0], from_pair[0]))
    first = [pack(own_first[i] + pair_first[i], scales) for i in range(2)]
    received = [send_y(first[0], 1), send_y(first[1], -1)]

    in_first = lax.broadcasted_iota(jnp.int32, (8, K), 0) < 4
    entries = jnp.maximum(own_stat, other_stat) * count[0].astype(f32)
    bounds, _ = lax.optimization_barrier((jnp.where(in_first, first_bound, entries), first))
    bounds, below, above = ring_fold(bounds, send_y, jnp.maximum)
    later, _ = lax.optimization_barrier(((own[1:], from_pair[1:]), bounds))
    parts = [
        [mine[at : at + HALF] + pair[at : at + HALF] for at in (0, HALF)] for mine, pair in zip(*later)
    ]
    passing, staying = lax.optimization_barrier(parts)
    around = scales_for(below[:1]), scales_for(above[:1])
    sum_scales = scales_for(bounds[:1] * 4.0)
    received, sums, messages = ring_second(received, passing, send_y, sum_scales, *around)
    y_part = ring_total(received, sums, [[v] for v in staying], sum_scales, *around)
    y_share = jnp.concatenate([y_part(0), y_part(1)], axis=0)

    bounds, _ = lax.optimization_barrier((bounds, messages))
    bounds = jnp.maximum(bounds, send_core(bounds))
    y_scales = scales_for(bounds[:1] * 4.0)
    bounds = ring_fold(ring_fold(bounds, send_x, jnp.maximum)[0], send_z, jnp.maximum)[0]
    z_scales = scales_for(bounds[:1] * bounds[4:5] * (4.0 * 16.0 * B))

    gram = jnp.dot(
        y_share.T, y_share, precision=lax.Precision.HIGH, preferred_element_type=f32
    )
    tiles = y_share.reshape(BR // 8, B, K)
    exponents = exponent_of(jnp.max(jnp.abs(tiles), axis=(1, 2)))
    gram_exponent = exponent_of(jnp.max(jnp.abs(gram)))
    codes = whole(tiles * jnp.exp2(-exponents)[:, None, None]).reshape(-1, K)
    gram = gram * jnp.exp2(-gram_exponent)
    high = whole(gram)
    low = whole((gram - high) * LOW_SCALE)
    scale_rows = jnp.concatenate([exponents, jnp.full((16,), gram_exponent)])
    scale_rows = jnp.broadcast_to(scale_rows[:, None], (32, K)).astype(jnp.int16)
    scale_rows = by_rows(lax.optimization_barrier(scale_rows))
    mine = [v.astype(jnp.int16) for v in (codes, high, low)]
    mine = jnp.concatenate([*mine, scale_rows], axis=0)
    mine, z_scales = lax.optimization_barrier((by_rows(mine), z_scales))
    gathered = lax.all_gather(mine, "col", axis=0, tiled=True)
    gram, tile_scales = read_shares(gathered)
    gram = ring_fold(gram, send_x, jnp.add)[0]
    partial = flat(partial_cols(count, z_target, rows, blocks, gathered, tile_scales))
    gram = ring_fold(gram, send_z, jnp.add)[0]

    rings = [(partial[:8], send_x, send_z), (partial[8:], send_z, send_x)]
    around = z_scales, z_scales
    scales_each = [z_scales, (z_scales[0], after(z_scales[1], gram))]
    messages = [
        [pack(v, scales) for v in values[:2]] for (values, _, _), scales in zip(rings, scales_each)
    ]
    received = [[send(m[0], 1), send(m[1], -1)] for m, (_, send, _) in zip(messages, rings)]
    lower_factor = jnp.linalg.cholesky(gram)
    seconds = [
        ring_second(r, values[2:4], send, z_scales, *around)
        for r, (values, send, _) in zip(received, rings)
    ]
    thirds = []
    for (direct, sums, _), (values, _, send) in zip(seconds, rings):
        total = ring_total(direct, sums, [values[4:6], values[6:]], z_scales, *around)
        quarters = [total(r // 2, r % 2 * 4 * B, (r % 2 + 1) * 4 * B) for r in range(4)]
        thirds.append(ring_exchange(quarters, send, z_scales))
    inverse = lax.linalg.triangular_solve(
        lower_factor, jnp.eye(K, dtype=f32), left_side=True, lower=True
    )
    basis_factor = after(inverse, seconds[1][2][1])
    q_share = jnp.dot(y_share, basis_factor.T, precision=highest, preferred_element_type=f32)
    z_raw = jnp.concatenate([z for z, _ in thirds], axis=0)
    z_share = jnp.dot(z_raw, inverse.T, precision=highest, preferred_element_type=f32)
    row_scale = math.sqrt(BR * B * lax.axis_size("row"))
    return (q_share * row_scale, z_share[None])


def solution(mesh):
    in_specs = (
        P("row", "col", None, None, None),
        P("col", None),
        P("row", "col", None),
        P("row", "col", None),
        P("row", "col"),
    )
    out_specs = (P(("row", "col"), None), P("col", "row", None))
    return jax.shard_map(body, mesh=mesh, in_specs=in_specs, out_specs=out_specs, check_vma=False)
```

```python
import math

import jax
import jax.numpy as jnp
from jax import lax
from jax.experimental import pallas as pl
from jax.experimental.layout import Layout, with_layout_constraint
from jax.experimental.pallas import tpu as pltpu
from jax.sharding import PartitionSpec as P

B = 256
K = 128
BR = 128
BC = 128
NBLK = 96
CHUNK = 8
AHEAD = 28
GROUP = 4
BUFFERS = AHEAD + GROUP
VMEM_BYTES = 56 * 1024 * 1024
f32 = jnp.float32
f16 = jnp.float16


def ring(shift):
    return [(c, ((c // 2 + shift) % 4) * 2 + c % 2) for c in range(8)]


def along_x(shift):
    return [(r, ((r // 4 + shift) % 4) * 4 + r % 4) for r in range(16)]


def along_z(shift):
    return [(r, (r // 4) * 4 + (r % 4 + shift) % 4) for r in range(16)]


SHARE_ROWS = BR // 8 * B + 2 * K + 32
LOW_SCALE = 2.0**15

PAIR = [(c, c ^ 1) for c in range(8)]


def run_slots(parts, count, targets, order, bounds, begin, group, carry, total_sum, outs, out_sems):
    chunks = total_sum.shape[0] // CHUNK

    def chunk_of(s):
        return jnp.where(targets[s] < 0, chunks, targets[s] // CHUNK)

    for c in range(chunks + 1):
        bounds[c] = 0

    def tally(s, _):
        c = chunk_of(s)
        bounds[c] = bounds[c] + 1
        return 0

    lax.fori_loop(0, count, tally, 0)
    total = 0
    for c in range(chunks):
        here = bounds[c]
        bounds[c] = total
        total = total + here
    bounds[chunks] = total

    def place(s, _):
        c = chunk_of(s)
        at = bounds[c]
        order[at] = s
        bounds[c] = at + 1
        return 0

    lax.fori_loop(0, count, place, 0)

    def begin_later(j):
        @pl.when(j < total)
        def _():
            begin(j, 0)

    lax.fori_loop(0, jnp.minimum(total, AHEAD), begin, 0)

    def clear(t, _):
        total_sum[t] = jnp.zeros((B, K), f32)
        return 0

    lax.fori_loop(0, chunks * CHUNK, clear, 0)

    writes = [[] for _ in range(chunks)]
    first = 0
    for ring_at in range(len(outs) // len(parts)):
        for i, tiles in enumerate(parts):
            at = ring_at * len(parts) + i
            for piece in range(0, tiles, CHUNK):
                size = min(CHUNK, tiles)
                sem = sum(len(w) for w in writes)
                writes[first // CHUNK].append(
                    pltpu.make_async_copy(
                        total_sum.at[pl.ds(first, size)],
                        outs[at].at[pl.ds(piece, size)],
                        out_sems.at[sem],
                    )
                )
                first += size

    def write_done(done, chunk):
        def step(c):
            for i, pieces in enumerate(writes):

                @pl.when(c == i)
                def _():
                    for copy in pieces:
                        copy.start()

            return c + 1

        return lax.while_loop(
            lambda c: (c < chunks) & (bounds[jnp.minimum(c, chunks - 1)] <= done), step, chunk
        )

    def by_group(size, first):
        def step(g, state):
            chunk, carry = state
            at = first + g * size
            carry = group(begin_later, at, size, carry)
            return write_done(at + size, chunk), carry

        return step

    groups = total // GROUP
    state = write_done(0, 0), carry
    state = lax.fori_loop(0, groups, by_group(GROUP, 0), state)
    state = lax.fori_loop(0, total - groups * GROUP, by_group(1, groups * GROUP), state)
    for pieces in writes:
        for copy in pieces:
            copy.wait()
    return state[1]


def y_kernel(count, targets, cols, blocks, sketch, *rest):
    outs, stat, scratch = rest[:3], rest[3], rest[4:]
    total_sum, order, bounds, block_buf, sketch_buf, sems, out_sems = scratch

    def copies(j):
        s, at = order[j], lax.rem(j, BUFFERS)
        return (
            pltpu.make_async_copy(blocks.at[s], block_buf.at[at], sems.at[0, at]),
            pltpu.make_async_copy(sketch.at[cols[s]], sketch_buf.at[at], sems.at[1, at]),
        )

    def begin(j, _):
        for copy in copies(j):
            copy.start()
        return 0

    def group(begin_later, at, size, carry):
        largest, largest_block = carry
        for u in range(size):
            begin_later(at + u + AHEAD)
        for u in range(size):
            for copy in copies(at + u):
                copy.wait()
        for u in range(size):
            target = targets[order[at + u]]
            buffer = lax.rem(at + u, BUFFERS)
            tile = block_buf[buffer]
            value = total_sum[target] + jnp.dot(
                tile, sketch_buf[buffer], preferred_element_type=f32
            )
            total_sum[target] = value
            largest = jnp.maximum(largest, jnp.max(jnp.abs(value).reshape(B // 8, 8, K), axis=0))
            largest_block = jnp.maximum(
                largest_block, jnp.max(jnp.abs(tile).reshape(B // 16, 16, B), axis=0)
            )
        return largest, largest_block

    carry = jnp.zeros((8, K), f32), jnp.zeros((16, B), jnp.bfloat16)
    largest, largest_block = run_slots(
        Y_PARTS, count[0], targets, order, bounds, begin, group, carry, total_sum, outs, out_sems
    )
    stat[:4] = jnp.full((4, K), jnp.max(largest))
    stat[4:] = jnp.full((4, K), jnp.max(largest_block.astype(f32)))


Y_PARTS = (32, 16, 16)
Z_PARTS = (16, 16, 8, 8, 4, 4, 4, 4)


def sums_of(parts):
    return tuple(jax.ShapeDtypeStruct((n, B, K), f32) for n in parts)


def scratch_for(halves, parts, y_type):
    return [
        pltpu.VMEM((halves * 8 * CHUNK, B, K), f32),
        pltpu.SMEM((NBLK + 1,), jnp.int32),
        pltpu.SMEM((halves * 8 + 1,), jnp.int32),
        pltpu.VMEM((BUFFERS, B, B), jnp.bfloat16),
        pltpu.VMEM((BUFFERS, B, K), y_type),
        pltpu.SemaphoreType.DMA((2, BUFFERS)),
        pltpu.SemaphoreType.DMA((halves * 10,)),
    ]


def partial_rows(count, targets, cols, blocks, sketch):
    return pl.pallas_call(
        y_kernel,
        out_shape=sums_of(Y_PARTS) + (jax.ShapeDtypeStruct((8, K), f32),),
        in_specs=[pl.BlockSpec(memory_space=pltpu.SMEM)] * 3
        + [pl.BlockSpec(memory_space=pl.ANY)] * 2,
        out_specs=(pl.BlockSpec(memory_space=pl.ANY),) * 3
        + (pl.BlockSpec(memory_space=pltpu.VMEM),),
        scratch_shapes=scratch_for(1, Y_PARTS, jnp.bfloat16),
        compiler_params=pltpu.CompilerParams(vmem_limit_bytes=VMEM_BYTES),
        cost_estimate=pl.CostEstimate(
            flops=NBLK * B * B * K, bytes_accessed=60 * 1024 * 1024, transcendentals=0
        ),
        name="partial_rows",
    )(count, targets, cols, blocks, sketch)


def table_row(row):
    return pl.multiple_of((row >> 4) * SHARE_ROWS + (row & 15) * B, 16)


def share_kernel(gathered, gram, scales, buffer, sems):
    copies = [
        pltpu.make_async_copy(
            gathered.at[pl.ds(c * SHARE_ROWS + BR // 8 * B, 2 * K + 32)], buffer.at[c], sems.at[c]
        )
        for c in range(8)
    ]
    for copy in copies:
        copy.start()
    total = jnp.zeros((K, K), f32)
    for c, copy in enumerate(copies):
        copy.wait()
        scale = jnp.exp2(buffer[c, 2 * K : 2 * K + 32].astype(f32))
        scales[c * 16 : (c + 1) * 16] = scale[:16]
        high, low = buffer[c, :K].astype(f32), buffer[c, K : 2 * K].astype(f32)
        total += (high + low * (1.0 / LOW_SCALE)) * scale[16:17]
    gram[...] = total


def read_shares(gathered):
    return pl.pallas_call(
        share_kernel,
        out_shape=(jax.ShapeDtypeStruct((K, K), f32), jax.ShapeDtypeStruct((BR, K), f32)),
        in_specs=[pl.BlockSpec(memory_space=pl.ANY)],
        out_specs=(pl.BlockSpec(memory_space=pltpu.VMEM),) * 2,
        scratch_shapes=[
            pltpu.VMEM((8, 2 * K + 32, K), jnp.int16),
            pltpu.SemaphoreType.DMA((8,)),
        ],
        compiler_params=pltpu.CompilerParams(vmem_limit_bytes=VMEM_BYTES),
        name="read_shares",
    )(gathered)


def z_kernel(count, targets, rows, blocks, table, tile_scales, *rest):
    outs, scratch = rest[:16], rest[16:]
    total_sum, order, bounds, block_buf, y_buf, sems, out_sems = scratch

    def copies(j):
        s, at = order[j], lax.rem(j, BUFFERS)
        return (
            pltpu.make_async_copy(blocks.at[s], block_buf.at[at], sems.at[0, at]),
            pltpu.make_async_copy(
                table.at[pl.ds(table_row(rows[s]), B)], y_buf.at[at], sems.at[1, at]
            ),
        )

    def begin(j, _):
        for copy in copies(j):
            copy.start()
        return 0

    def group(begin_later, at, size, carry):
        for u in range(size):
            begin_later(at + u + AHEAD)
        for u in range(size):
            for copy in copies(at + u):
                copy.wait()
        for u in range(size):
            buffer = lax.rem(at + u, BUFFERS)
            value = y_buf[buffer].astype(f32)
            high = value.astype(jnp.bfloat16)
            low = (value - high.astype(f32)).astype(jnp.bfloat16)
            product = lax.dot_general(
                block_buf[buffer],
                jnp.concatenate([high, low], axis=1),
                (((0,), (0,)), ((), ())),
                preferred_element_type=f32,
            )
            slot = order[at + u]
            product = (product[:, :K] + product[:, K:]) * tile_scales[pl.ds(rows[slot], 1)]
            total_sum[targets[slot]] += product
        return carry

    run_slots(
        Z_PARTS, count[0], targets, order, bounds, begin, group, 0, total_sum, outs, out_sems
    )


def partial_cols(count, targets, rows, blocks, table, tile_scales):
    return pl.pallas_call(
        z_kernel,
        out_shape=sums_of(Z_PARTS * 2),
        in_specs=[pl.BlockSpec(memory_space=pltpu.SMEM)] * 3
        + [pl.BlockSpec(memory_space=pl.ANY)] * 2
        + [pl.BlockSpec(memory_space=pltpu.VMEM)],
        out_specs=(pl.BlockSpec(memory_space=pl.ANY),) * 16,
        scratch_shapes=scratch_for(2, Z_PARTS, jnp.int16),
        compiler_params=pltpu.CompilerParams(vmem_limit_bytes=VMEM_BYTES),
        cost_estimate=pl.CostEstimate(
            flops=NBLK * B * B * K * 4, bytes_accessed=42 * 1024 * 1024, transcendentals=0
        ),
        name="partial_cols",
    )(count, targets, rows, blocks, table, tile_scales)


def scales_for(bound):
    exponent = jnp.ceil(jnp.log2(jnp.maximum(bound, 1e-30))) - 15.0
    scale, inverse = lax.optimization_barrier((jnp.exp2(exponent), jnp.exp2(-exponent)))
    return scale[0, 0], inverse[0, 0]


def by_rows(value):
    return with_layout_constraint(value, Layout(tuple(range(value.ndim))))


def pack(value, scales):
    return by_rows((value * scales[1]).astype(f16))


def unpack(message, scales):
    return message.astype(f32) * scales[0]


PLACES = (6, 7, 4, 1, 0, 2, 3, 5)


HALF = CHUNK * B


def ring_first(messages, send):
    return lax.optimization_barrier((send(messages[0], 1), send(messages[1], -1)))


def ring_second(received, passing, send, scales, below, above):
    messages = lax.optimization_barrier(
        (
            pack(passing[0] + unpack(received[0][:HALF], below), scales),
            pack(passing[1] + unpack(received[1][:HALF], above), scales),
        )
    )
    sums = send(messages[0], 1), send(messages[1], -1)
    return lax.optimization_barrier((received, sums, messages))


def ring_total(received, sums, staying, scales, below, above):
    def total(which, start=0, stop=HALF):
        direct = received[1 - which][HALF + start : HALF + stop]
        return (
            staying[which][start // (stop - start)]
            + unpack(direct, below if which else above)
            + unpack(sums[which][start:stop], scales)
        )

    return total


def ring_exchange(parts, send, scales):
    received = [send(pack(parts[r], scales), r) for r in (1, 3, 2)]
    up, down, across = (unpack(message, scales) for message in received)
    return parts[0] + up + down + across, received


def exponent_of(largest):
    return jnp.floor(jnp.log2(jnp.maximum(largest, 1e-30))) - 14.0


def whole(value):
    return jnp.clip(jnp.round(value), -32767.0, 32767.0)


def after(value, other):
    return value + (0.0 * other[(0,) * other.ndim]).astype(value.dtype)


def ring_fold(value, send, op):
    across, below, above = send(value, 2), send(value, 1), send(value, -1)
    return op(op(value, across), op(below, above)), below, above


def body(blocks, sketch, block_row, block_col, counts):
    blocks = blocks[0, 0]
    rows, cols = block_row[0, 0], block_col[0, 0]
    count = counts[0, 0]
    row_at, col_at = lax.axis_index("row"), lax.axis_index("col")
    here_x, here_z = row_at // 4, row_at % 4
    here_y, core = col_at // 2, col_at % 2
    sketch_table = sketch.reshape(BC, B, K)

    def send_core(value):
        return lax.ppermute(value, "col", PAIR)

    def send_y(value, shift):
        return lax.ppermute(value, "col", ring(shift))

    def send_x(value, shift):
        return lax.ppermute(value, "row", along_x(shift))

    def send_z(value, shift):
        return lax.ppermute(value, "row", along_z(shift))

    live = jnp.arange(NBLK, dtype=jnp.int32) < count

    def chunk_of(rel, half):
        key = (rel & 3) * 2 + half
        chunk = PLACES[7]
        for k in range(7):
            chunk = jnp.where(key == k, PLACES[k], chunk)
        return chunk * CHUNK

    y_target = chunk_of((rows >> 5) - here_y, (rows >> 3) & 1) + (rows & 7)
    row_core = (rows >> 4) & 1
    rel_x, rel_z = ((cols >> 5) - here_x) & 3, ((cols >> 3) - here_z) & 3
    is_a = ((cols >> 2) & 1) == 0
    one, two = jnp.where(is_a, rel_x, rel_z), jnp.where(is_a, rel_z, rel_x)
    z_target = chunk_of(one, two >> 1) + (two & 1) * 4 + (cols & 3) + jnp.where(is_a, 0, 8 * CHUNK)
    other_target = jnp.where(live & (row_core != core), y_target, -1)
    own_target = jnp.where(live & (row_core == core), y_target, -1)
    z_target = jnp.where(live, z_target, -1)
    count = count[None]

    def flat(values):
        return [v.reshape(-1, K) for v in values]

    *other, other_stat = partial_rows(count, other_target, cols, blocks, sketch_table)
    *from_pair, pair_stat = [send_core(v) for v in (*other, other_stat)]
    *own, own_stat = partial_rows(count, own_target, cols, blocks, sketch_table)
    own, from_pair = flat(own), flat(from_pair)

    first_bound = own_stat + pair_stat
    scales = scales_for(first_bound[:1])
    own_first, pair_first = (v.reshape(2, 2 * HALF, K) for v in (own[0], from_pair[0]))
    first = [pack(own_first[i] + pair_first[i], scales) for i in range(2)]
    received = [send_y(first[0], 1), send_y(first[1], -1)]

    in_first = lax.broadcasted_iota(jnp.int32, (8, K), 0) < 4
    entries = jnp.maximum(own_stat, other_stat) * count[0].astype(f32)
    bounds, _ = lax.optimization_barrier((jnp.where(in_first, first_bound, entries), first))
    bounds, below, above = ring_fold(bounds, send_y, jnp.maximum)
    later, _ = lax.optimization_barrier(((own[1:], from_pair[1:]), bounds))
    parts = [
        [mine[at : at + HALF] + pair[at : at + HALF] for at in (0, HALF)] for mine, pair in zip(*later)
    ]
    passing, staying = lax.optimization_barrier(parts)
    around = scales_for(below[:1]), scales_for(above[:1])
    sum_scales = scales_for(bounds[:1] * 4.0)
    received, sums, messages = ring_second(received, passing, send_y, sum_scales, *around)
    y_part = ring_total(received, sums, [[v] for v in staying], sum_scales, *around)
    y_share = jnp.concatenate([y_part(0), y_part(1)], axis=0)

    bounds, _ = lax.optimization_barrier((bounds, messages))
    bounds = jnp.maximum(bounds, send_core(bounds))
    y_scales = scales_for(bounds[:1] * 4.0)
    bounds = ring_fold(ring_fold(bounds, send_x, jnp.maximum)[0], send_z, jnp.maximum)[0]
    z_scales = scales_for(bounds[:1] * bounds[4:5] * (4.0 * 16.0 * B))

    gram = jnp.dot(
        y_share.T, y_share, precision=lax.Precision.HIGH, preferred_element_type=f32
    )
    tiles = y_share.reshape(BR // 8, B, K)
    exponents = exponent_of(jnp.max(jnp.abs(tiles), axis=(1, 2)))
    gram_exponent = exponent_of(jnp.max(jnp.abs(gram)))
    codes = whole(tiles * jnp.exp2(-exponents)[:, None, None]).reshape(-1, K)
    gram = gram * jnp.exp2(-gram_exponent)
    high = whole(gram)
    low = whole((gram - high) * LOW_SCALE)
    scale_rows = jnp.concatenate([exponents, jnp.full((16,), gram_exponent)])
    scale_rows = jnp.broadcast_to(scale_rows[:, None], (32, K)).astype(jnp.int16)
    scale_rows = by_rows(lax.optimization_barrier(scale_rows))
    mine = [v.astype(jnp.int16) for v in (codes, high, low)]
    mine = jnp.concatenate([*mine, scale_rows], axis=0)
    mine, z_scales = lax.optimization_barrier((by_rows(mine), z_scales))
    gathered = lax.all_gather(mine, "col", axis=0, tiled=True)
    gram, tile_scales = read_shares(gathered)
    gram = ring_fold(by_rows(gram), send_x, jnp.add)[0]
    partial = flat(partial_cols(count, z_target, rows, blocks, gathered, tile_scales))
    gram = by_rows(ring_fold(gram, send_z, jnp.add)[0])

    rings = [(partial[:8], send_x, send_z), (partial[8:], send_z, send_x)]
    around = z_scales, z_scales
    scales_each = [z_scales, (z_scales[0], after(z_scales[1], gram))]
    messages = [
        [pack(v, scales) for v in values[:2]] for (values, _, _), scales in zip(rings, scales_each)
    ]
    received = [[send(m[0], 1), send(m[1], -1)] for m, (_, send, _) in zip(messages, rings)]
    lower_factor = jnp.linalg.cholesky(gram)
    seconds = [
        ring_second(r, values[2:4], send, z_scales, *around)
        for r, (values, send, _) in zip(received, rings)
    ]
    inverse = lax.linalg.triangular_solve(
        lower_factor, jnp.eye(K, dtype=f32), left_side=True, lower=True
    )
    thirds = []
    for (direct, sums, _), (values, _, send) in zip(seconds, rings):
        total = ring_total(direct, sums, [values[4:6], values[6:]], z_scales, *around)
        quarters = [total(r // 2, r % 2 * 4 * B, (r % 2 + 1) * 4 * B) for r in range(4)]
        thirds.append(ring_exchange(quarters, send, z_scales))
    basis_factor = after(inverse, thirds[0][1][0])
    q_share = jnp.dot(
        y_share, basis_factor.T, precision=lax.Precision.HIGH, preferred_element_type=f32
    )
    z_raw = jnp.concatenate([z for z, _ in thirds], axis=0)
    z_share = jnp.dot(
        z_raw, inverse.T, precision=lax.Precision.HIGH, preferred_element_type=f32
    )
    row_scale = math.sqrt(BR * B * lax.axis_size("row"))
    return (q_share * row_scale, z_share[None])


def solution(mesh):
    in_specs = (
        P("row", "col", None, None, None),
        P("col", None),
        P("row", "col", None),
        P("row", "col", None),
        P("row", "col"),
    )
    out_specs = (P(("row", "col"), None), P("col", "row", None))
    return jax.shard_map(body, mesh=mesh, in_specs=in_specs, out_specs=out_specs, check_vma=False)
```

```python
import math

import jax
import jax.numpy as jnp
from jax import lax
from jax.experimental import pallas as pl
from jax.experimental.layout import Layout, with_layout_constraint
from jax.experimental.pallas import tpu as pltpu
from jax.sharding import PartitionSpec as P

B = 256
K = 128
BR = 128
BC = 128
NBLK = 96
CHUNK = 8
AHEAD = 28
GROUP = 4
BUFFERS = AHEAD + GROUP
VMEM_BYTES = 56 * 1024 * 1024
f32 = jnp.float32
f16 = jnp.float16


def ring(shift):
    return [(c, ((c // 2 + shift) % 4) * 2 + c % 2) for c in range(8)]


def along_x(shift):
    return [(r, ((r // 4 + shift) % 4) * 4 + r % 4) for r in range(16)]


def along_z(shift):
    return [(r, (r // 4) * 4 + (r % 4 + shift) % 4) for r in range(16)]


SHARE_ROWS = BR // 8 * B + 2 * K + 32
LOW_SCALE = 2.0**15

PAIR = [(c, c ^ 1) for c in range(8)]


def run_slots(parts, count, targets, order, bounds, begin, group, carry, total_sum, outs, out_sems):
    chunks = total_sum.shape[0] // CHUNK

    def chunk_of(s):
        return jnp.where(targets[s] < 0, chunks, targets[s] // CHUNK)

    for c in range(chunks + 1):
        bounds[c] = 0

    def tally(s, _):
        c = chunk_of(s)
        bounds[c] = bounds[c] + 1
        return 0

    lax.fori_loop(0, count, tally, 0)
    total = 0
    for c in range(chunks):
        here = bounds[c]
        bounds[c] = total
        total = total + here
    bounds[chunks] = total

    def place(s, _):
        c = chunk_of(s)
        at = bounds[c]
        order[at] = s
        bounds[c] = at + 1
        return 0

    lax.fori_loop(0, count, place, 0)

    def begin_later(j):
        @pl.when(j < total)
        def _():
            begin(j, 0)

    lax.fori_loop(0, jnp.minimum(total, AHEAD), begin, 0)

    def clear(t, _):
        total_sum[t] = jnp.zeros((B, K), f32)
        return 0

    lax.fori_loop(0, chunks * CHUNK, clear, 0)

    writes = [[] for _ in range(chunks)]
    first = 0
    for ring_at in range(len(outs) // len(parts)):
        for i, tiles in enumerate(parts):
            at = ring_at * len(parts) + i
            for piece in range(0, tiles, CHUNK):
                size = min(CHUNK, tiles)
                sem = sum(len(w) for w in writes)
                writes[first // CHUNK].append(
                    pltpu.make_async_copy(
                        total_sum.at[pl.ds(first, size)],
                        outs[at].at[pl.ds(piece, size)],
                        out_sems.at[sem],
                    )
                )
                first += size

    def write_done(done, chunk):
        def step(c):
            for i, pieces in enumerate(writes):

                @pl.when(c == i)
                def _():
                    for copy in pieces:
                        copy.start()

            return c + 1

        return lax.while_loop(
            lambda c: (c < chunks) & (bounds[jnp.minimum(c, chunks - 1)] <= done), step, chunk
        )

    def by_group(size, first):
        def step(g, state):
            chunk, carry = state
            at = first + g * size
            carry = group(begin_later, at, size, carry)
            return write_done(at + size, chunk), carry

        return step

    groups = total // GROUP
    state = write_done(0, 0), carry
    state = lax.fori_loop(0, groups, by_group(GROUP, 0), state)
    state = lax.fori_loop(0, total - groups * GROUP, by_group(1, groups * GROUP), state)
    for pieces in writes:
        for copy in pieces:
            copy.wait()
    return state[1]


def y_kernel(count, targets, cols, blocks, sketch, *rest):
    outs, stat, scratch = rest[:2], rest[2], rest[3:]
    total_sum, order, bounds, block_buf, sketch_buf, sems, out_sems = scratch

    def copies(j):
        s, at = order[j], lax.rem(j, BUFFERS)
        return (
            pltpu.make_async_copy(blocks.at[s], block_buf.at[at], sems.at[0, at]),
            pltpu.make_async_copy(sketch.at[cols[s]], sketch_buf.at[at], sems.at[1, at]),
        )

    def begin(j, _):
        for copy in copies(j):
            copy.start()
        return 0

    def group(begin_later, at, size, carry):
        largest, largest_block = carry
        for u in range(size):
            begin_later(at + u + AHEAD)
        for u in range(size):
            for copy in copies(at + u):
                copy.wait()
        for u in range(size):
            target = targets[order[at + u]]
            buffer = lax.rem(at + u, BUFFERS)
            tile = block_buf[buffer]
            value = total_sum[target] + jnp.dot(
                tile, sketch_buf[buffer], preferred_element_type=f32
            )
            total_sum[target] = value
            largest = jnp.maximum(largest, jnp.max(jnp.abs(value).reshape(B // 8, 8, K), axis=0))
            largest_block = jnp.maximum(
                largest_block, jnp.max(jnp.abs(tile).reshape(B // 16, 16, B), axis=0)
            )
        return largest, largest_block

    carry = jnp.zeros((8, K), f32), jnp.zeros((16, B), jnp.bfloat16)
    largest, largest_block = run_slots(
        Y_PARTS, count[0], targets, order, bounds, begin, group, carry, total_sum, outs, out_sems
    )
    stat[:4] = jnp.full((4, K), jnp.max(largest))
    stat[4:] = jnp.full((4, K), jnp.max(largest_block.astype(f32)))


Y_PARTS = (32, 32)
Z_PARTS = (16, 16, 8, 8, 4, 4, 4, 4)


def sums_of(parts):
    return tuple(jax.ShapeDtypeStruct((n, B, K), f32) for n in parts)


def scratch_for(halves, parts, y_type):
    return [
        pltpu.VMEM((halves * 8 * CHUNK, B, K), f32),
        pltpu.SMEM((NBLK + 1,), jnp.int32),
        pltpu.SMEM((halves * 8 + 1,), jnp.int32),
        pltpu.VMEM((BUFFERS, B, B), jnp.bfloat16),
        pltpu.VMEM((BUFFERS, B, K), y_type),
        pltpu.SemaphoreType.DMA((2, BUFFERS)),
        pltpu.SemaphoreType.DMA((halves * 10,)),
    ]


def partial_rows(count, targets, cols, blocks, sketch):
    return pl.pallas_call(
        y_kernel,
        out_shape=sums_of(Y_PARTS) + (jax.ShapeDtypeStruct((8, K), f32),),
        in_specs=[pl.BlockSpec(memory_space=pltpu.SMEM)] * 3
        + [pl.BlockSpec(memory_space=pl.ANY)] * 2,
        out_specs=(pl.BlockSpec(memory_space=pl.ANY),) * 2
        + (pl.BlockSpec(memory_space=pltpu.VMEM),),
        scratch_shapes=scratch_for(1, Y_PARTS, jnp.bfloat16),
        compiler_params=pltpu.CompilerParams(vmem_limit_bytes=VMEM_BYTES),
        cost_estimate=pl.CostEstimate(
            flops=NBLK * B * B * K, bytes_accessed=60 * 1024 * 1024, transcendentals=0
        ),
        name="partial_rows",
    )(count, targets, cols, blocks, sketch)


def table_row(row):
    return pl.multiple_of((row >> 4) * SHARE_ROWS + (row & 15) * B, 16)


def share_kernel(gathered, gram, scales, buffer, sems):
    copies = [
        pltpu.make_async_copy(
            gathered.at[pl.ds(c * SHARE_ROWS + BR // 8 * B, 2 * K + 32)], buffer.at[c], sems.at[c]
        )
        for c in range(8)
    ]
    for copy in copies:
        copy.start()
    total = jnp.zeros((K, K), f32)
    for c, copy in enumerate(copies):
        copy.wait()
        scale = jnp.exp2(buffer[c, 2 * K : 2 * K + 32].astype(f32))
        scales[c * 16 : (c + 1) * 16] = scale[:16]
        high, low = buffer[c, :K].astype(f32), buffer[c, K : 2 * K].astype(f32)
        total += (high + low * (1.0 / LOW_SCALE)) * scale[16:17]
    gram[...] = total


def read_shares(gathered):
    return pl.pallas_call(
        share_kernel,
        out_shape=(jax.ShapeDtypeStruct((K, K), f32), jax.ShapeDtypeStruct((BR, K), f32)),
        in_specs=[pl.BlockSpec(memory_space=pl.ANY)],
        out_specs=(pl.BlockSpec(memory_space=pltpu.VMEM),) * 2,
        scratch_shapes=[
            pltpu.VMEM((8, 2 * K + 32, K), jnp.int16),
            pltpu.SemaphoreType.DMA((8,)),
        ],
        compiler_params=pltpu.CompilerParams(vmem_limit_bytes=VMEM_BYTES),
        name="read_shares",
    )(gathered)


def z_kernel(count, targets, rows, blocks, table, tile_scales, *rest):
    outs, scratch = rest[:16], rest[16:]
    total_sum, order, bounds, block_buf, y_buf, sems, out_sems = scratch

    def copies(j):
        s, at = order[j], lax.rem(j, BUFFERS)
        return (
            pltpu.make_async_copy(blocks.at[s], block_buf.at[at], sems.at[0, at]),
            pltpu.make_async_copy(
                table.at[pl.ds(table_row(rows[s]), B)], y_buf.at[at], sems.at[1, at]
            ),
        )

    def begin(j, _):
        for copy in copies(j):
            copy.start()
        return 0

    def group(begin_later, at, size, carry):
        for u in range(size):
            begin_later(at + u + AHEAD)
        for u in range(size):
            for copy in copies(at + u):
                copy.wait()
        for u in range(size):
            buffer = lax.rem(at + u, BUFFERS)
            value = y_buf[buffer].astype(f32)
            high = value.astype(jnp.bfloat16)
            low = (value - high.astype(f32)).astype(jnp.bfloat16)
            product = lax.dot_general(
                block_buf[buffer],
                jnp.concatenate([high, low], axis=1),
                (((0,), (0,)), ((), ())),
                preferred_element_type=f32,
            )
            slot = order[at + u]
            product = (product[:, :K] + product[:, K:]) * tile_scales[pl.ds(rows[slot], 1)]
            total_sum[targets[slot]] += product
        return carry

    run_slots(
        Z_PARTS, count[0], targets, order, bounds, begin, group, 0, total_sum, outs, out_sems
    )


def partial_cols(count, targets, rows, blocks, table, tile_scales):
    return pl.pallas_call(
        z_kernel,
        out_shape=sums_of(Z_PARTS * 2),
        in_specs=[pl.BlockSpec(memory_space=pltpu.SMEM)] * 3
        + [pl.BlockSpec(memory_space=pl.ANY)] * 2
        + [pl.BlockSpec(memory_space=pltpu.VMEM)],
        out_specs=(pl.BlockSpec(memory_space=pl.ANY),) * 16,
        scratch_shapes=scratch_for(2, Z_PARTS, jnp.int16),
        compiler_params=pltpu.CompilerParams(vmem_limit_bytes=VMEM_BYTES),
        cost_estimate=pl.CostEstimate(
            flops=NBLK * B * B * K * 4, bytes_accessed=42 * 1024 * 1024, transcendentals=0
        ),
        name="partial_cols",
    )(count, targets, rows, blocks, table, tile_scales)


def scales_for(bound):
    exponent = jnp.ceil(jnp.log2(jnp.maximum(bound, 1e-30))) - 15.0
    scale, inverse = lax.optimization_barrier((jnp.exp2(exponent), jnp.exp2(-exponent)))
    return scale[0, 0], inverse[0, 0]


def by_rows(value):
    return with_layout_constraint(value, Layout(tuple(range(value.ndim))))


def pack(value, scales):
    return by_rows((value * scales[1]).astype(f16))


def unpack(message, scales):
    return message.astype(f32) * scales[0]


PLACES = (6, 7, 4, 1, 0, 2, 3, 5)


HALF = CHUNK * B


def ring_first(messages, send):
    return lax.optimization_barrier((send(messages[0], 1), send(messages[1], -1)))


def ring_second(received, passing, send, scales, below, above):
    messages = lax.optimization_barrier(
        (
            pack(passing[0] + unpack(received[0][:HALF], below), scales),
            pack(passing[1] + unpack(received[1][:HALF], above), scales),
        )
    )
    sums = send(messages[0], 1), send(messages[1], -1)
    return lax.optimization_barrier((received, sums, messages))


def ring_total(received, sums, staying, scales, below, above):
    def total(which, start=0, stop=HALF):
        direct = received[1 - which][HALF + start : HALF + stop]
        return (
            staying[which][start // (stop - start)]
            + unpack(direct, below if which else above)
            + unpack(sums[which][start:stop], scales)
        )

    return total


def ring_exchange(parts, send, scales):
    received = [send(pack(parts[r], scales), r) for r in (1, 3, 2)]
    up, down, across = (unpack(message, scales) for message in received)
    return parts[0] + up + down + across, received


def exponent_of(largest):
    return jnp.floor(jnp.log2(jnp.maximum(largest, 1e-30))) - 14.0


def whole(value):
    return jnp.clip(jnp.round(value), -32767.0, 32767.0)


def after(value, other):
    return value + (0.0 * other[(0,) * other.ndim]).astype(value.dtype)


def ring_fold(value, send, op):
    across, below, above = send(value, 2), send(value, 1), send(value, -1)
    return op(op(value, across), op(below, above)), below, above


def body(blocks, sketch, block_row, block_col, counts):
    blocks = blocks[0, 0]
    rows, cols = block_row[0, 0], block_col[0, 0]
    count = counts[0, 0]
    row_at, col_at = lax.axis_index("row"), lax.axis_index("col")
    here_x, here_z = row_at // 4, row_at % 4
    here_y, core = col_at // 2, col_at % 2
    sketch_table = sketch.reshape(BC, B, K)

    def send_core(value):
        return lax.ppermute(value, "col", PAIR)

    def send_y(value, shift):
        return lax.ppermute(value, "col", ring(shift))

    def send_x(value, shift):
        return lax.ppermute(value, "row", along_x(shift))

    def send_z(value, shift):
        return lax.ppermute(value, "row", along_z(shift))

    live = jnp.arange(NBLK, dtype=jnp.int32) < count

    def chunk_of(rel, half):
        key = (rel & 3) * 2 + half
        chunk = PLACES[7]
        for k in range(7):
            chunk = jnp.where(key == k, PLACES[k], chunk)
        return chunk * CHUNK

    y_target = chunk_of((rows >> 5) - here_y, (rows >> 3) & 1) + (rows & 7)
    row_core = (rows >> 4) & 1
    rel_x, rel_z = ((cols >> 5) - here_x) & 3, ((cols >> 3) - here_z) & 3
    is_a = ((cols >> 2) & 1) == 0
    one, two = jnp.where(is_a, rel_x, rel_z), jnp.where(is_a, rel_z, rel_x)
    z_target = chunk_of(one, two >> 1) + (two & 1) * 4 + (cols & 3) + jnp.where(is_a, 0, 8 * CHUNK)
    other_target = jnp.where(live & (row_core != core), y_target, -1)
    own_target = jnp.where(live & (row_core == core), y_target, -1)
    z_target = jnp.where(live, z_target, -1)
    count = count[None]

    def flat(values):
        return [v.reshape(-1, K) for v in values]

    *other, other_stat = partial_rows(count, other_target, cols, blocks, sketch_table)
    *from_pair, pair_stat = [send_core(v) for v in (*other, other_stat)]
    *own, own_stat = partial_rows(count, own_target, cols, blocks, sketch_table)
    own, from_pair = flat(own), flat(from_pair)

    first_bound = own_stat + pair_stat
    scales = scales_for(first_bound[:1])
    own_first, pair_first = (v.reshape(2, 2 * HALF, K) for v in (own[0], from_pair[0]))
    first = [pack(own_first[i] + pair_first[i], scales) for i in range(2)]
    received = [send_y(first[0], 1), send_y(first[1], -1)]

    in_first = lax.broadcasted_iota(jnp.int32, (8, K), 0) < 4
    entries = jnp.maximum(own_stat, other_stat) * count[0].astype(f32)
    bounds, _ = lax.optimization_barrier((jnp.where(in_first, first_bound, entries), first))
    bounds, below, above = ring_fold(bounds, send_y, jnp.maximum)
    later, _ = lax.optimization_barrier(((own[1], from_pair[1]), bounds))
    parts = [
        [later[0][at : at + HALF] + later[1][at : at + HALF] for at in (start, start + HALF)]
        for start in (0, 2 * HALF)
    ]
    passing, staying = lax.optimization_barrier(parts)
    around = scales_for(below[:1]), scales_for(above[:1])
    sum_scales = scales_for(bounds[:1] * 4.0)
    received, sums, messages = ring_second(received, passing, send_y, sum_scales, *around)
    y_part = ring_total(received, sums, [[v] for v in staying], sum_scales, *around)
    y_share = jnp.concatenate([y_part(0), y_part(1)], axis=0)

    bounds, _ = lax.optimization_barrier((bounds, messages))
    bounds = jnp.maximum(bounds, send_core(bounds))
    y_scales = scales_for(bounds[:1] * 4.0)
    bounds = ring_fold(ring_fold(bounds, send_x, jnp.maximum)[0], send_z, jnp.maximum)[0]
    z_scales = scales_for(bounds[:1] * bounds[4:5] * (4.0 * 16.0 * B))

    gram = jnp.dot(
        y_share.T, y_share, precision=lax.Precision.HIGH, preferred_element_type=f32
    )
    tiles = y_share.reshape(BR // 8, B, K)
    exponents = exponent_of(jnp.max(jnp.abs(tiles), axis=(1, 2)))
    gram_exponent = exponent_of(jnp.max(jnp.abs(gram)))
    codes = whole(tiles * jnp.exp2(-exponents)[:, None, None]).reshape(-1, K)
    gram = gram * jnp.exp2(-gram_exponent)
    high = whole(gram)
    low = whole((gram - high) * LOW_SCALE)
    scale_rows = jnp.concatenate([exponents, jnp.full((16,), gram_exponent)])
    scale_rows = jnp.broadcast_to(scale_rows[:, None], (32, K)).astype(jnp.int16)
    scale_rows = by_rows(lax.optimization_barrier(scale_rows))
    mine = [v.astype(jnp.int16) for v in (codes, high, low)]
    mine = jnp.concatenate([*mine, scale_rows], axis=0)
    mine, z_scales = lax.optimization_barrier((by_rows(mine), z_scales))
    gathered = lax.all_gather(mine, "col", axis=0, tiled=True)
    gram, tile_scales = read_shares(gathered)
    gram = ring_fold(by_rows(gram), send_x, jnp.add)[0]
    partial = flat(partial_cols(count, z_target, rows, blocks, gathered, tile_scales))
    gram = by_rows(ring_fold(gram, send_z, jnp.add)[0])

    rings = [(partial[:8], send_x, send_z), (partial[8:], send_z, send_x)]
    around = z_scales, z_scales
    scales_each = [z_scales, (z_scales[0], after(z_scales[1], gram))]
    messages = [
        [pack(v, scales) for v in values[:2]] for (values, _, _), scales in zip(rings, scales_each)
    ]
    received = [[send(m[0], 1), send(m[1], -1)] for m, (_, send, _) in zip(messages, rings)]
    lower_factor = jnp.linalg.cholesky(gram)
    seconds = [
        ring_second(r, values[2:4], send, z_scales, *around)
        for r, (values, send, _) in zip(received, rings)
    ]
    lower_factor = after(lower_factor, seconds[0][2][1])
    inverse = lax.linalg.triangular_solve(
        lower_factor, jnp.eye(K, dtype=f32), left_side=True, lower=True
    )
    thirds = []
    for (direct, sums, _), (values, _, send) in zip(seconds, rings):
        total = ring_total(direct, sums, [values[4:6], values[6:]], z_scales, *around)
        quarters = [total(r // 2, r % 2 * 4 * B, (r % 2 + 1) * 4 * B) for r in range(4)]
        thirds.append(ring_exchange(quarters, send, z_scales))
    basis_factor = after(inverse, thirds[0][1][0])
    q_share = jnp.dot(
        y_share, basis_factor.T, precision=lax.Precision.HIGH, preferred_element_type=f32
    )
    z_raw = jnp.concatenate([z for z, _ in thirds], axis=0)
    z_share = jnp.dot(
        z_raw, inverse.T, precision=lax.Precision.HIGH, preferred_element_type=f32
    )
    row_scale = math.sqrt(BR * B * lax.axis_size("row"))
    return (q_share * row_scale, z_share[None])


def solution(mesh):
    in_specs = (
        P("row", "col", None, None, None),
        P("col", None),
        P("row", "col", None),
        P("row", "col", None),
        P("row", "col"),
    )
    out_specs = (P(("row", "col"), None), P("col", "row", None))
    return jax.shard_map(body, mesh=mesh, in_specs=in_specs, out_specs=out_specs, check_vma=False)
```

```python
import math

import jax
import jax.numpy as jnp
from jax import lax
from jax.experimental import pallas as pl
from jax.experimental.layout import Layout, with_layout_constraint
from jax.experimental.pallas import tpu as pltpu
from jax.sharding import PartitionSpec as P

B = 256
K = 128
BR = 128
BC = 128
NBLK = 96
CHUNK = 8
AHEAD = 28
GROUP = 4
BUFFERS = AHEAD + GROUP
VMEM_BYTES = 56 * 1024 * 1024
f32 = jnp.float32
f16 = jnp.float16


def ring(shift):
    return [(c, ((c // 2 + shift) % 4) * 2 + c % 2) for c in range(8)]


def along_x(shift):
    return [(r, ((r // 4 + shift) % 4) * 4 + r % 4) for r in range(16)]


def along_z(shift):
    return [(r, (r // 4) * 4 + (r % 4 + shift) % 4) for r in range(16)]


SHARE_ROWS = BR // 8 * B + 2 * K + 32
LOW_SCALE = 2.0**15

PAIR = [(c, c ^ 1) for c in range(8)]


def run_slots(parts, count, targets, order, bounds, begin, group, carry, total_sum, outs, out_sems):
    chunks = total_sum.shape[0] // CHUNK

    def chunk_of(s):
        return jnp.where(targets[s] < 0, chunks, targets[s] // CHUNK)

    for c in range(chunks + 1):
        bounds[c] = 0

    def tally(s, _):
        c = chunk_of(s)
        bounds[c] = bounds[c] + 1
        return 0

    lax.fori_loop(0, count, tally, 0)
    total = 0
    for c in range(chunks):
        here = bounds[c]
        bounds[c] = total
        total = total + here
    bounds[chunks] = total

    def place(s, _):
        c = chunk_of(s)
        at = bounds[c]
        order[at] = s
        bounds[c] = at + 1
        return 0

    lax.fori_loop(0, count, place, 0)

    def begin_later(j):
        @pl.when(j < total)
        def _():
            begin(j, 0)

    lax.fori_loop(0, jnp.minimum(total, AHEAD), begin, 0)

    def clear(t, _):
        total_sum[t] = jnp.zeros((B, K), f32)
        return 0

    lax.fori_loop(0, chunks * CHUNK, clear, 0)

    writes = [[] for _ in range(chunks)]
    first = 0
    for ring_at in range(len(outs) // len(parts)):
        for i, tiles in enumerate(parts):
            at = ring_at * len(parts) + i
            for piece in range(0, tiles, CHUNK):
                size = min(CHUNK, tiles)
                sem = sum(len(w) for w in writes)
                writes[first // CHUNK].append(
                    pltpu.make_async_copy(
                        total_sum.at[pl.ds(first, size)],
                        outs[at].at[pl.ds(piece, size)],
                        out_sems.at[sem],
                    )
                )
                first += size

    def write_done(done, chunk):
        def step(c):
            for i, pieces in enumerate(writes):

                @pl.when(c == i)
                def _():
                    for copy in pieces:
                        copy.start()

            return c + 1

        return lax.while_loop(
            lambda c: (c < chunks) & (bounds[jnp.minimum(c, chunks - 1)] <= done), step, chunk
        )

    def by_group(size, first):
        def step(g, state):
            chunk, carry = state
            at = first + g * size
            carry = group(begin_later, at, size, carry)
            return write_done(at + size, chunk), carry

        return step

    groups = total // GROUP
    state = write_done(0, 0), carry
    state = lax.fori_loop(0, groups, by_group(GROUP, 0), state)
    state = lax.fori_loop(0, total - groups * GROUP, by_group(1, groups * GROUP), state)
    for pieces in writes:
        for copy in pieces:
            copy.wait()
    return state[1]


def y_kernel(count, targets, cols, blocks, sketch, *rest):
    outs, stat, scratch = rest[:2], rest[2], rest[3:]
    total_sum, order, bounds, block_buf, sketch_buf, sems, out_sems = scratch

    def copies(j):
        s, at = order[j], lax.rem(j, BUFFERS)
        return (
            pltpu.make_async_copy(blocks.at[s], block_buf.at[at], sems.at[0, at]),
            pltpu.make_async_copy(sketch.at[cols[s]], sketch_buf.at[at], sems.at[1, at]),
        )

    def begin(j, _):
        for copy in copies(j):
            copy.start()
        return 0

    def group(begin_later, at, size, carry):
        largest, largest_block = carry
        for u in range(size):
            begin_later(at + u + AHEAD)
        for u in range(size):
            for copy in copies(at + u):
                copy.wait()
        for u in range(size):
            target = targets[order[at + u]]
            buffer = lax.rem(at + u, BUFFERS)
            tile = block_buf[buffer]
            value = total_sum[target] + jnp.dot(
                tile, sketch_buf[buffer], preferred_element_type=f32
            )
            total_sum[target] = value
            largest = jnp.maximum(largest, jnp.max(jnp.abs(value).reshape(B // 8, 8, K), axis=0))
            largest_block = jnp.maximum(
                largest_block, jnp.max(jnp.abs(tile).reshape(B // 16, 16, B), axis=0)
            )
        return largest, largest_block

    carry = jnp.zeros((8, K), f32), jnp.zeros((16, B), jnp.bfloat16)
    largest, largest_block = run_slots(
        Y_PARTS, count[0], targets, order, bounds, begin, group, carry, total_sum, outs, out_sems
    )
    stat[:4] = jnp.full((4, K), jnp.max(largest))
    stat[4:] = jnp.full((4, K), jnp.max(largest_block.astype(f32)))


Y_PARTS = (32, 32)
Z_PARTS = (16, 16, 8, 8, 4, 4, 4, 4)


def sums_of(parts):
    return tuple(jax.ShapeDtypeStruct((n, B, K), f32) for n in parts)


def scratch_for(halves, parts, y_type):
    return [
        pltpu.VMEM((halves * 8 * CHUNK, B, K), f32),
        pltpu.SMEM((NBLK + 1,), jnp.int32),
        pltpu.SMEM((halves * 8 + 1,), jnp.int32),
        pltpu.VMEM((BUFFERS, B, B), jnp.bfloat16),
        pltpu.VMEM((BUFFERS, B, K), y_type),
        pltpu.SemaphoreType.DMA((2, BUFFERS)),
        pltpu.SemaphoreType.DMA((halves * 10,)),
    ]


def partial_rows(count, targets, cols, blocks, sketch):
    return pl.pallas_call(
        y_kernel,
        out_shape=sums_of(Y_PARTS) + (jax.ShapeDtypeStruct((8, K), f32),),
        in_specs=[pl.BlockSpec(memory_space=pltpu.SMEM)] * 3
        + [pl.BlockSpec(memory_space=pl.ANY)] * 2,
        out_specs=(pl.BlockSpec(memory_space=pl.ANY),) * 2
        + (pl.BlockSpec(memory_space=pltpu.VMEM),),
        scratch_shapes=scratch_for(1, Y_PARTS, jnp.bfloat16),
        compiler_params=pltpu.CompilerParams(vmem_limit_bytes=VMEM_BYTES),
        cost_estimate=pl.CostEstimate(
            flops=NBLK * B * B * K, bytes_accessed=60 * 1024 * 1024, transcendentals=0
        ),
        name="partial_rows",
    )(count, targets, cols, blocks, sketch)


def table_row(row):
    return pl.multiple_of((row >> 4) * SHARE_ROWS + (row & 15) * B, 16)


def share_kernel(gathered, gram, scales, buffer, sems):
    copies = [
        pltpu.make_async_copy(
            gathered.at[pl.ds(c * SHARE_ROWS + BR // 8 * B, 2 * K + 32)], buffer.at[c], sems.at[c]
        )
        for c in range(8)
    ]
    for copy in copies:
        copy.start()
    total = jnp.zeros((K, K), f32)
    for c, copy in enumerate(copies):
        copy.wait()
        scale = jnp.exp2(buffer[c, 2 * K : 2 * K + 32].astype(f32))
        scales[c * 16 : (c + 1) * 16] = scale[:16]
        high, low = buffer[c, :K].astype(f32), buffer[c, K : 2 * K].astype(f32)
        total += (high + low * (1.0 / LOW_SCALE)) * scale[16:17]
    gram[...] = total


def read_shares(gathered):
    return pl.pallas_call(
        share_kernel,
        out_shape=(jax.ShapeDtypeStruct((K, K), f32), jax.ShapeDtypeStruct((BR, K), f32)),
        in_specs=[pl.BlockSpec(memory_space=pl.ANY)],
        out_specs=(pl.BlockSpec(memory_space=pltpu.VMEM),) * 2,
        scratch_shapes=[
            pltpu.VMEM((8, 2 * K + 32, K), jnp.int16),
            pltpu.SemaphoreType.DMA((8,)),
        ],
        compiler_params=pltpu.CompilerParams(vmem_limit_bytes=VMEM_BYTES),
        name="read_shares",
    )(gathered)


def z_kernel(count, targets, rows, blocks, table, tile_scales, *rest):
    outs, scratch = rest[:16], rest[16:]
    total_sum, order, bounds, block_buf, y_buf, sems, out_sems = scratch

    def copies(j):
        s, at = order[j], lax.rem(j, BUFFERS)
        return (
            pltpu.make_async_copy(blocks.at[s], block_buf.at[at], sems.at[0, at]),
            pltpu.make_async_copy(
                table.at[pl.ds(table_row(rows[s]), B)], y_buf.at[at], sems.at[1, at]
            ),
        )

    def begin(j, _):
        for copy in copies(j):
            copy.start()
        return 0

    def group(begin_later, at, size, carry):
        for u in range(size):
            begin_later(at + u + AHEAD)
        for u in range(size):
            for copy in copies(at + u):
                copy.wait()
        for u in range(size):
            buffer = lax.rem(at + u, BUFFERS)
            value = y_buf[buffer].astype(f32)
            high = value.astype(jnp.bfloat16)
            low = (value - high.astype(f32)).astype(jnp.bfloat16)
            product = lax.dot_general(
                block_buf[buffer],
                jnp.concatenate([high, low], axis=1),
                (((0,), (0,)), ((), ())),
                preferred_element_type=f32,
            )
            slot = order[at + u]
            product = (product[:, :K] + product[:, K:]) * tile_scales[pl.ds(rows[slot], 1)]
            total_sum[targets[slot]] += product
        return carry

    run_slots(
        Z_PARTS, count[0], targets, order, bounds, begin, group, 0, total_sum, outs, out_sems
    )


def partial_cols(count, targets, rows, blocks, table, tile_scales):
    return pl.pallas_call(
        z_kernel,
        out_shape=sums_of(Z_PARTS * 2),
        in_specs=[pl.BlockSpec(memory_space=pltpu.SMEM)] * 3
        + [pl.BlockSpec(memory_space=pl.ANY)] * 2
        + [pl.BlockSpec(memory_space=pltpu.VMEM)],
        out_specs=(pl.BlockSpec(memory_space=pl.ANY),) * 16,
        scratch_shapes=scratch_for(2, Z_PARTS, jnp.int16),
        compiler_params=pltpu.CompilerParams(vmem_limit_bytes=VMEM_BYTES),
        cost_estimate=pl.CostEstimate(
            flops=NBLK * B * B * K * 4, bytes_accessed=42 * 1024 * 1024, transcendentals=0
        ),
        name="partial_cols",
    )(count, targets, rows, blocks, table, tile_scales)


def scales_for(bound):
    exponent = jnp.ceil(jnp.log2(jnp.maximum(bound, 1e-30))) - 15.0
    scale, inverse = lax.optimization_barrier((jnp.exp2(exponent), jnp.exp2(-exponent)))
    return scale[0, 0], inverse[0, 0]


def by_rows(value):
    return with_layout_constraint(value, Layout(tuple(range(value.ndim))))


def pack(value, scales):
    return by_rows((value * scales[1]).astype(f16))


def unpack(message, scales):
    return message.astype(f32) * scales[0]


PLACES = (6, 7, 4, 1, 0, 2, 3, 5)


HALF = CHUNK * B


def ring_first(messages, send):
    return lax.optimization_barrier((send(messages[0], 1), send(messages[1], -1)))


def ring_second(received, passing, send, scales, below, above):
    messages = lax.optimization_barrier(
        (
            pack(passing[0] + unpack(received[0][:HALF], below), scales),
            pack(passing[1] + unpack(received[1][:HALF], above), scales),
        )
    )
    sums = send(messages[0], 1), send(messages[1], -1)
    return lax.optimization_barrier((received, sums, messages))


def ring_total(received, sums, staying, scales, below, above):
    def total(which, start=0, stop=HALF):
        direct = received[1 - which][HALF + start : HALF + stop]
        return (
            staying[which][start // (stop - start)]
            + unpack(direct, below if which else above)
            + unpack(sums[which][start:stop], scales)
        )

    return total


def ring_exchange(parts, send, scales):
    sent = [pack(parts[r], scales) for r in (1, 3, 2)]
    received = [send(message, r) for message, r in zip(sent, (1, 3, 2))]
    up, down, across = (unpack(message, scales) for message in received)
    return parts[0] + up + down + across, received


def exponent_of(largest):
    return jnp.floor(jnp.log2(jnp.maximum(largest, 1e-30))) - 14.0


def whole(value):
    return jnp.clip(jnp.round(value), -32767.0, 32767.0)


def after(value, other):
    return value + (0.0 * other[(0,) * other.ndim]).astype(value.dtype)


def ring_fold(value, send, op):
    across, below, above = send(value, 2), send(value, 1), send(value, -1)
    return op(op(value, across), op(below, above)), below, above


def body(blocks, sketch, block_row, block_col, counts):
    blocks = blocks[0, 0]
    rows, cols = block_row[0, 0], block_col[0, 0]
    count = counts[0, 0]
    row_at, col_at = lax.axis_index("row"), lax.axis_index("col")
    here_x, here_z = row_at // 4, row_at % 4
    here_y, core = col_at // 2, col_at % 2
    sketch_table = sketch.reshape(BC, B, K)

    def send_core(value):
        return lax.ppermute(value, "col", PAIR)

    def send_y(value, shift):
        return lax.ppermute(value, "col", ring(shift))

    def send_x(value, shift):
        return lax.ppermute(value, "row", along_x(shift))

    def send_z(value, shift):
        return lax.ppermute(value, "row", along_z(shift))

    live = jnp.arange(NBLK, dtype=jnp.int32) < count

    def chunk_of(rel, half):
        key = (rel & 3) * 2 + half
        chunk = PLACES[7]
        for k in range(7):
            chunk = jnp.where(key == k, PLACES[k], chunk)
        return chunk * CHUNK

    y_target = chunk_of((rows >> 5) - here_y, (rows >> 3) & 1) + (rows & 7)
    row_core = (rows >> 4) & 1
    rel_x, rel_z = ((cols >> 5) - here_x) & 3, ((cols >> 3) - here_z) & 3
    is_a = ((cols >> 2) & 1) == 0
    one, two = jnp.where(is_a, rel_x, rel_z), jnp.where(is_a, rel_z, rel_x)
    z_target = chunk_of(one, two >> 1) + (two & 1) * 4 + (cols & 3) + jnp.where(is_a, 0, 8 * CHUNK)
    other_target = jnp.where(live & (row_core != core), y_target, -1)
    own_target = jnp.where(live & (row_core == core), y_target, -1)
    z_target = jnp.where(live, z_target, -1)
    count = count[None]

    def flat(values):
        return [v.reshape(-1, K) for v in values]

    *other, other_stat = partial_rows(count, other_target, cols, blocks, sketch_table)
    *from_pair, pair_stat = [send_core(v) for v in (*other, other_stat)]
    *own, own_stat = partial_rows(count, own_target, cols, blocks, sketch_table)
    own, from_pair = flat(own), flat(from_pair)

    first_bound = own_stat + pair_stat
    scales = scales_for(first_bound[:1])
    own_first, pair_first = (v.reshape(2, 2 * HALF, K) for v in (own[0], from_pair[0]))
    first = [pack(own_first[i] + pair_first[i], scales) for i in range(2)]
    received = [send_y(first[0], 1), send_y(first[1], -1)]

    in_first = lax.broadcasted_iota(jnp.int32, (8, K), 0) < 4
    entries = jnp.maximum(own_stat, other_stat) * count[0].astype(f32)
    bounds, _ = lax.optimization_barrier((jnp.where(in_first, first_bound, entries), first))
    bounds, below, above = ring_fold(bounds, send_y, jnp.maximum)
    later, _ = lax.optimization_barrier(((own[1], from_pair[1]), bounds))
    parts = [
        [later[0][at : at + HALF] + later[1][at : at + HALF] for at in (start, start + HALF)]
        for start in (0, 2 * HALF)
    ]
    passing, staying = lax.optimization_barrier(parts)
    around = scales_for(below[:1]), scales_for(above[:1])
    sum_scales = scales_for(bounds[:1] * 4.0)
    received, sums, messages = ring_second(received, passing, send_y, sum_scales, *around)
    y_part = ring_total(received, sums, [[v] for v in staying], sum_scales, *around)
    y_share = jnp.concatenate([y_part(0), y_part(1)], axis=0)

    bounds, _ = lax.optimization_barrier((bounds, messages))
    bounds = jnp.maximum(bounds, send_core(bounds))
    y_scales = scales_for(bounds[:1] * 4.0)
    bounds = ring_fold(ring_fold(bounds, send_x, jnp.maximum)[0], send_z, jnp.maximum)[0]
    z_scales = scales_for(bounds[:1] * bounds[4:5] * (4.0 * 16.0 * B))

    gram = jnp.dot(
        y_share.T, y_share, precision=lax.Precision.HIGH, preferred_element_type=f32
    )
    tiles = y_share.reshape(BR // 8, B, K)
    exponents = exponent_of(jnp.max(jnp.abs(tiles), axis=(1, 2)))
    gram_exponent = exponent_of(jnp.max(jnp.abs(gram)))
    codes = whole(tiles * jnp.exp2(-exponents)[:, None, None]).reshape(-1, K)
    gram = gram * jnp.exp2(-gram_exponent)
    high = whole(gram)
    low = whole((gram - high) * LOW_SCALE)
    scale_rows = jnp.concatenate([exponents, jnp.full((16,), gram_exponent)])
    scale_rows = jnp.broadcast_to(scale_rows[:, None], (32, K)).astype(jnp.int16)
    scale_rows = by_rows(lax.optimization_barrier(scale_rows))
    mine = [v.astype(jnp.int16) for v in (codes, high, low)]
    mine = jnp.concatenate([*mine, scale_rows], axis=0)
    mine, z_scales = lax.optimization_barrier((by_rows(mine), z_scales))
    gathered = lax.all_gather(mine, "col", axis=0, tiled=True)
    gram, tile_scales = read_shares(gathered)
    gram = ring_fold(by_rows(gram), send_x, jnp.add)[0]
    partial = flat(partial_cols(count, z_target, rows, blocks, gathered, tile_scales))
    gram = by_rows(ring_fold(gram, send_z, jnp.add)[0])

    rings = [(partial[:8], send_x, send_z), (partial[8:], send_z, send_x)]
    around = z_scales, z_scales
    scales_each = [z_scales, (z_scales[0], after(z_scales[1], gram))]
    messages = [
        [pack(v, scales) for v in values[:2]] for (values, _, _), scales in zip(rings, scales_each)
    ]
    received = [[send(m[0], 1), send(m[1], -1)] for m, (_, send, _) in zip(messages, rings)]
    lower_factor = jnp.linalg.cholesky(gram)
    seconds = [
        ring_second(r, values[2:4], send, z_scales, *around)
        for r, (values, send, _) in zip(received, rings)
    ]
    thirds = []
    for (direct, sums, _), (values, _, send) in zip(seconds, rings):
        total = ring_total(direct, sums, [values[4:6], values[6:]], z_scales, *around)
        quarters = [total(r // 2, r % 2 * 4 * B, (r % 2 + 1) * 4 * B) for r in range(4)]
        thirds.append(ring_exchange(quarters, send, z_scales))
    lower_factor = after(lower_factor, thirds[0][1][0])
    inverse = lax.linalg.triangular_solve(
        lower_factor, jnp.eye(K, dtype=f32), left_side=True, lower=True
    )
    q_share = jnp.dot(
        y_share, inverse.T, precision=lax.Precision.HIGH, preferred_element_type=f32
    )
    z_raw = jnp.concatenate([z for z, _ in thirds], axis=0)
    z_share = jnp.dot(
        z_raw, inverse.T, precision=lax.Precision.HIGH, preferred_element_type=f32
    )
    row_scale = math.sqrt(BR * B * lax.axis_size("row"))
    return (q_share * row_scale, z_share[None])


def solution(mesh):
    in_specs = (
        P("row", "col", None, None, None),
        P("col", None),
        P("row", "col", None),
        P("row", "col", None),
        P("row", "col"),
    )
    out_specs = (P(("row", "col"), None), P("col", "row", None))
    return jax.shard_map(body, mesh=mesh, in_specs=in_specs, out_specs=out_specs, check_vma=False)
```

```python
import math

import jax
import jax.numpy as jnp
from jax import lax
from jax.experimental import pallas as pl
from jax.experimental.layout import Layout, with_layout_constraint
from jax.experimental.pallas import tpu as pltpu
from jax.sharding import PartitionSpec as P

B = 256
K = 128
BR = 128
BC = 128
NBLK = 96
CHUNK = 8
AHEAD = 28
GROUP = 4
BUFFERS = AHEAD + GROUP
VMEM_BYTES = 56 * 1024 * 1024
f32 = jnp.float32
f16 = jnp.float16


def ring(shift):
    return [(c, ((c // 2 + shift) % 4) * 2 + c % 2) for c in range(8)]


def along_x(shift):
    return [(r, ((r // 4 + shift) % 4) * 4 + r % 4) for r in range(16)]


def along_z(shift):
    return [(r, (r // 4) * 4 + (r % 4 + shift) % 4) for r in range(16)]


SHARE_ROWS = BR // 8 * B + 2 * K + 32
LOW_SCALE = 2.0**15

PAIR = [(c, c ^ 1) for c in range(8)]


def run_slots(parts, count, targets, order, bounds, begin, group, carry, total_sum, outs, out_sems):
    chunks = total_sum.shape[0] // CHUNK

    def chunk_of(s):
        return jnp.where(targets[s] < 0, chunks, targets[s] // CHUNK)

    for c in range(chunks + 1):
        bounds[c] = 0

    def tally(s, _):
        c = chunk_of(s)
        bounds[c] = bounds[c] + 1
        return 0

    lax.fori_loop(0, count, tally, 0)
    total = 0
    for c in range(chunks):
        here = bounds[c]
        bounds[c] = total
        total = total + here
    bounds[chunks] = total

    def place(s, _):
        c = chunk_of(s)
        at = bounds[c]
        order[at] = s
        bounds[c] = at + 1
        return 0

    lax.fori_loop(0, count, place, 0)

    def begin_later(j):
        @pl.when(j < total)
        def _():
            begin(j, 0)

    lax.fori_loop(0, jnp.minimum(total, AHEAD), begin, 0)

    def clear(t, _):
        total_sum[t] = jnp.zeros((B, K), f32)
        return 0

    lax.fori_loop(0, chunks * CHUNK, clear, 0)

    writes = [[] for _ in range(chunks)]
    first = 0
    for ring_at in range(len(outs) // len(parts)):
        for i, tiles in enumerate(parts):
            at = ring_at * len(parts) + i
            for piece in range(0, tiles, CHUNK):
                size = min(CHUNK, tiles)
                sem = sum(len(w) for w in writes)
                writes[first // CHUNK].append(
                    pltpu.make_async_copy(
                        total_sum.at[pl.ds(first, size)],
                        outs[at].at[pl.ds(piece, size)],
                        out_sems.at[sem],
                    )
                )
                first += size

    def write_done(done, chunk):
        def step(c):
            for i, pieces in enumerate(writes):

                @pl.when(c == i)
                def _():
                    for copy in pieces:
                        copy.start()

            return c + 1

        return lax.while_loop(
            lambda c: (c < chunks) & (bounds[jnp.minimum(c, chunks - 1)] <= done), step, chunk
        )

    def by_group(size, first):
        def step(g, state):
            chunk, carry = state
            at = first + g * size
            carry = group(begin_later, at, size, carry)
            return write_done(at + size, chunk), carry

        return step

    groups = total // GROUP
    state = write_done(0, 0), carry
    state = lax.fori_loop(0, groups, by_group(GROUP, 0), state)
    state = lax.fori_loop(0, total - groups * GROUP, by_group(1, groups * GROUP), state)
    for pieces in writes:
        for copy in pieces:
            copy.wait()
    return state[1]


def y_kernel(count, targets, cols, blocks, sketch, *rest):
    outs, stat, scratch = rest[:2], rest[2], rest[3:]
    total_sum, order, bounds, block_buf, sketch_buf, sems, out_sems = scratch

    def copies(j):
        s, at = order[j], lax.rem(j, BUFFERS)
        return (
            pltpu.make_async_copy(blocks.at[s], block_buf.at[at], sems.at[0, at]),
            pltpu.make_async_copy(sketch.at[cols[s]], sketch_buf.at[at], sems.at[1, at]),
        )

    def begin(j, _):
        for copy in copies(j):
            copy.start()
        return 0

    def group(begin_later, at, size, carry):
        largest, largest_block = carry
        for u in range(size):
            begin_later(at + u + AHEAD)
        for u in range(size):
            for copy in copies(at + u):
                copy.wait()
        for u in range(size):
            target = targets[order[at + u]]
            buffer = lax.rem(at + u, BUFFERS)
            tile = block_buf[buffer]
            value = total_sum[target] + jnp.dot(
                tile, sketch_buf[buffer], preferred_element_type=f32
            )
            total_sum[target] = value
            largest = jnp.maximum(largest, jnp.max(jnp.abs(value).reshape(B // 8, 8, K), axis=0))
            largest_block = jnp.maximum(
                largest_block, jnp.max(jnp.abs(tile).reshape(B // 16, 16, B), axis=0)
            )
        return largest, largest_block

    carry = jnp.zeros((8, K), f32), jnp.zeros((16, B), jnp.bfloat16)
    largest, largest_block = run_slots(
        Y_PARTS, count[0], targets, order, bounds, begin, group, carry, total_sum, outs, out_sems
    )
    stat[:4] = jnp.full((4, K), jnp.max(largest))
    stat[4:] = jnp.full((4, K), jnp.max(largest_block.astype(f32)))


Y_PARTS = (32, 32)
Z_PARTS = (16, 16, 16, 4, 4, 4, 4)


def sums_of(parts):
    return tuple(jax.ShapeDtypeStruct((n, B, K), f32) for n in parts)


def scratch_for(halves, parts, y_type):
    return [
        pltpu.VMEM((halves * 8 * CHUNK, B, K), f32),
        pltpu.SMEM((NBLK + 1,), jnp.int32),
        pltpu.SMEM((halves * 8 + 1,), jnp.int32),
        pltpu.VMEM((BUFFERS, B, B), jnp.bfloat16),
        pltpu.VMEM((BUFFERS, B, K), y_type),
        pltpu.SemaphoreType.DMA((2, BUFFERS)),
        pltpu.SemaphoreType.DMA((halves * 10,)),
    ]


def partial_rows(count, targets, cols, blocks, sketch):
    return pl.pallas_call(
        y_kernel,
        out_shape=sums_of(Y_PARTS) + (jax.ShapeDtypeStruct((8, K), f32),),
        in_specs=[pl.BlockSpec(memory_space=pltpu.SMEM)] * 3
        + [pl.BlockSpec(memory_space=pl.ANY)] * 2,
        out_specs=(pl.BlockSpec(memory_space=pl.ANY),) * 2
        + (pl.BlockSpec(memory_space=pltpu.VMEM),),
        scratch_shapes=scratch_for(1, Y_PARTS, jnp.bfloat16),
        compiler_params=pltpu.CompilerParams(vmem_limit_bytes=VMEM_BYTES),
        cost_estimate=pl.CostEstimate(
            flops=NBLK * B * B * K, bytes_accessed=60 * 1024 * 1024, transcendentals=0
        ),
        name="partial_rows",
    )(count, targets, cols, blocks, sketch)


def table_row(row):
    return pl.multiple_of((row >> 4) * SHARE_ROWS + (row & 15) * B, 16)


def share_kernel(gathered, gram, scales, buffer, sems):
    copies = [
        pltpu.make_async_copy(
            gathered.at[pl.ds(c * SHARE_ROWS + BR // 8 * B, 2 * K + 32)], buffer.at[c], sems.at[c]
        )
        for c in range(8)
    ]
    for copy in copies:
        copy.start()
    total = jnp.zeros((K, K), f32)
    for c, copy in enumerate(copies):
        copy.wait()
        scale = jnp.exp2(buffer[c, 2 * K : 2 * K + 32].astype(f32))
        scales[c * 16 : (c + 1) * 16] = scale[:16]
        high, low = buffer[c, :K].astype(f32), buffer[c, K : 2 * K].astype(f32)
        total += (high + low * (1.0 / LOW_SCALE)) * scale[16:17]
    gram[...] = total


def read_shares(gathered):
    return pl.pallas_call(
        share_kernel,
        out_shape=(jax.ShapeDtypeStruct((K, K), f32), jax.ShapeDtypeStruct((BR, K), f32)),
        in_specs=[pl.BlockSpec(memory_space=pl.ANY)],
        out_specs=(pl.BlockSpec(memory_space=pltpu.VMEM),) * 2,
        scratch_shapes=[
            pltpu.VMEM((8, 2 * K + 32, K), jnp.int16),
            pltpu.SemaphoreType.DMA((8,)),
        ],
        compiler_params=pltpu.CompilerParams(vmem_limit_bytes=VMEM_BYTES),
        name="read_shares",
    )(gathered)


def z_kernel(count, targets, rows, blocks, table, tile_scales, *rest):
    outs, scratch = rest[:14], rest[14:]
    total_sum, order, bounds, block_buf, y_buf, sems, out_sems = scratch

    def copies(j):
        s, at = order[j], lax.rem(j, BUFFERS)
        return (
            pltpu.make_async_copy(blocks.at[s], block_buf.at[at], sems.at[0, at]),
            pltpu.make_async_copy(
                table.at[pl.ds(table_row(rows[s]), B)], y_buf.at[at], sems.at[1, at]
            ),
        )

    def begin(j, _):
        for copy in copies(j):
            copy.start()
        return 0

    def group(begin_later, at, size, carry):
        for u in range(size):
            begin_later(at + u + AHEAD)
        for u in range(size):
            for copy in copies(at + u):
                copy.wait()
        for u in range(size):
            buffer = lax.rem(at + u, BUFFERS)
            value = y_buf[buffer].astype(f32)
            high = value.astype(jnp.bfloat16)
            low = (value - high.astype(f32)).astype(jnp.bfloat16)
            product = lax.dot_general(
                block_buf[buffer],
                jnp.concatenate([high, low], axis=1),
                (((0,), (0,)), ((), ())),
                preferred_element_type=f32,
            )
            slot = order[at + u]
            product = (product[:, :K] + product[:, K:]) * tile_scales[pl.ds(rows[slot], 1)]
            total_sum[targets[slot]] += product
        return carry

    run_slots(
        Z_PARTS, count[0], targets, order, bounds, begin, group, 0, total_sum, outs, out_sems
    )


def partial_cols(count, targets, rows, blocks, table, tile_scales):
    return pl.pallas_call(
        z_kernel,
        out_shape=sums_of(Z_PARTS * 2),
        in_specs=[pl.BlockSpec(memory_space=pltpu.SMEM)] * 3
        + [pl.BlockSpec(memory_space=pl.ANY)] * 2
        + [pl.BlockSpec(memory_space=pltpu.VMEM)],
        out_specs=(pl.BlockSpec(memory_space=pl.ANY),) * 14,
        scratch_shapes=scratch_for(2, Z_PARTS, jnp.int16),
        compiler_params=pltpu.CompilerParams(vmem_limit_bytes=VMEM_BYTES),
        cost_estimate=pl.CostEstimate(
            flops=NBLK * B * B * K * 4, bytes_accessed=42 * 1024 * 1024, transcendentals=0
        ),
        name="partial_cols",
    )(count, targets, rows, blocks, table, tile_scales)


def scales_for(bound):
    exponent = jnp.ceil(jnp.log2(jnp.maximum(bound, 1e-30))) - 15.0
    scale, inverse = lax.optimization_barrier((jnp.exp2(exponent), jnp.exp2(-exponent)))
    return scale[0, 0], inverse[0, 0]


def by_rows(value):
    return with_layout_constraint(value, Layout(tuple(range(value.ndim))))


def pack(value, scales):
    return by_rows((value * scales[1]).astype(f16))


def unpack(message, scales):
    return message.astype(f32) * scales[0]


PLACES = (6, 7, 4, 1, 0, 2, 3, 5)
Z_PLACES = (6, 7, 0, 1, 4, 5, 2, 3)


HALF = CHUNK * B


def ring_first(messages, send):
    return lax.optimization_barrier((send(messages[0], 1), send(messages[1], -1)))


def ring_second(received, passing, send, scales, below, above):
    messages = lax.optimization_barrier(
        (
            pack(passing[0] + unpack(received[0][:HALF], below), scales),
            pack(passing[1] + unpack(received[1][:HALF], above), scales),
        )
    )
    sums = send(messages[0], 1), send(messages[1], -1)
    return lax.optimization_barrier((received, sums, messages))


def ring_total(received, sums, staying, scales, below, above):
    def total(which, start=0, stop=HALF):
        direct = received[1 - which][HALF + start : HALF + stop]
        return (
            staying[which][start // (stop - start)]
            + unpack(direct, below if which else above)
            + unpack(sums[which][start:stop], scales)
        )

    return total


def ring_exchange(parts, send, scales):
    received = [send(pack(parts[r], scales), r) for r in (1, 3, 2)]
    up, down, across = (unpack(message, scales) for message in received)
    return parts[0] + up + down + across, received


def exponent_of(largest):
    return jnp.floor(jnp.log2(jnp.maximum(largest, 1e-30))) - 14.0


def whole(value):
    return jnp.clip(jnp.round(value), -32767.0, 32767.0)


def after(value, other):
    return value + (0.0 * other[(0,) * other.ndim]).astype(value.dtype)


def ring_fold(value, send, op):
    across, below, above = send(value, 2), send(value, 1), send(value, -1)
    return op(op(value, across), op(below, above)), below, above


def body(blocks, sketch, block_row, block_col, counts):
    blocks = blocks[0, 0]
    rows, cols = block_row[0, 0], block_col[0, 0]
    count = counts[0, 0]
    row_at, col_at = lax.axis_index("row"), lax.axis_index("col")
    here_x, here_z = row_at // 4, row_at % 4
    here_y, core = col_at // 2, col_at % 2
    sketch_table = sketch.reshape(BC, B, K)

    def send_core(value):
        return lax.ppermute(value, "col", PAIR)

    def send_y(value, shift):
        return lax.ppermute(value, "col", ring(shift))

    def send_x(value, shift):
        return lax.ppermute(value, "row", along_x(shift))

    def send_z(value, shift):
        return lax.ppermute(value, "row", along_z(shift))

    live = jnp.arange(NBLK, dtype=jnp.int32) < count

    def chunk_of(rel, half, places):
        key = (rel & 3) * 2 + half
        chunk = places[7]
        for k in range(7):
            chunk = jnp.where(key == k, places[k], chunk)
        return chunk * CHUNK

    y_target = chunk_of((rows >> 5) - here_y, (rows >> 3) & 1, PLACES) + (rows & 7)
    row_core = (rows >> 4) & 1
    rel_x, rel_z = ((cols >> 5) - here_x) & 3, ((cols >> 3) - here_z) & 3
    is_a = ((cols >> 2) & 1) == 0
    one, two = jnp.where(is_a, rel_x, rel_z), jnp.where(is_a, rel_z, rel_x)
    z_target = chunk_of(one, two >> 1, Z_PLACES) + (two & 1) * 4 + (cols & 3) + jnp.where(is_a, 0, 8 * CHUNK)
    other_target = jnp.where(live & (row_core != core), y_target, -1)
    own_target = jnp.where(live & (row_core == core), y_target, -1)
    z_target = jnp.where(live, z_target, -1)
    count = count[None]

    def flat(values):
        return [v.reshape(-1, K) for v in values]

    *other, other_stat = partial_rows(count, other_target, cols, blocks, sketch_table)
    *from_pair, pair_stat = [send_core(v) for v in (*other, other_stat)]
    *own, own_stat = partial_rows(count, own_target, cols, blocks, sketch_table)
    own, from_pair = flat(own), flat(from_pair)

    first_bound = own_stat + pair_stat
    scales = scales_for(first_bound[:1])
    own_first, pair_first = (v.reshape(2, 2 * HALF, K) for v in (own[0], from_pair[0]))
    first = [pack(own_first[i] + pair_first[i], scales) for i in range(2)]
    received = [send_y(first[0], 1), send_y(first[1], -1)]

    in_first = lax.broadcasted_iota(jnp.int32, (8, K), 0) < 4
    entries = jnp.maximum(own_stat, other_stat) * count[0].astype(f32)
    bounds, _ = lax.optimization_barrier((jnp.where(in_first, first_bound, entries), first))
    bounds, below, above = ring_fold(bounds, send_y, jnp.maximum)
    later, _ = lax.optimization_barrier(((own[1], from_pair[1]), bounds))
    parts = [
        [later[0][at : at + HALF] + later[1][at : at + HALF] for at in (start, start + HALF)]
        for start in (0, 2 * HALF)
    ]
    passing, staying = lax.optimization_barrier(parts)
    around = scales_for(below[:1]), scales_for(above[:1])
    sum_scales = scales_for(bounds[:1] * 4.0)
    received, sums, messages = ring_second(received, passing, send_y, sum_scales, *around)
    y_part = ring_total(received, sums, [[v] for v in staying], sum_scales, *around)
    y_share = jnp.concatenate([y_part(0), y_part(1)], axis=0)

    bounds, _ = lax.optimization_barrier((bounds, messages))
    bounds = jnp.maximum(bounds, send_core(bounds))
    y_scales = scales_for(bounds[:1] * 4.0)
    bounds = ring_fold(ring_fold(bounds, send_x, jnp.maximum)[0], send_z, jnp.maximum)[0]
    z_scales = scales_for(bounds[:1] * bounds[4:5] * (4.0 * 16.0 * B))

    gram = jnp.dot(
        y_share.T, y_share, precision=lax.Precision.HIGH, preferred_element_type=f32
    )
    tiles = y_share.reshape(BR // 8, B, K)
    exponents = exponent_of(jnp.max(jnp.abs(tiles), axis=(1, 2)))
    gram_exponent = exponent_of(jnp.max(jnp.abs(gram)))
    codes = whole(tiles * jnp.exp2(-exponents)[:, None, None]).reshape(-1, K)
    gram = gram * jnp.exp2(-gram_exponent)
    high = whole(gram)
    low = whole((gram - high) * LOW_SCALE)
    scale_rows = jnp.concatenate([exponents, jnp.full((16,), gram_exponent)])
    scale_rows = jnp.broadcast_to(scale_rows[:, None], (32, K)).astype(jnp.int16)
    scale_rows = by_rows(lax.optimization_barrier(scale_rows))
    mine = [v.astype(jnp.int16) for v in (codes, high, low)]
    mine = jnp.concatenate([*mine, scale_rows], axis=0)
    mine, z_scales = lax.optimization_barrier((by_rows(mine), z_scales))
    gathered = lax.all_gather(mine, "col", axis=0, tiled=True)
    gram, tile_scales = read_shares(gathered)
    gram = ring_fold(by_rows(gram), send_x, jnp.add)[0]
    partial = flat(partial_cols(count, z_target, rows, blocks, gathered, tile_scales))
    gram = by_rows(ring_fold(gram, send_z, jnp.add)[0])

    rings = [(partial[:7], send_x, send_z), (partial[7:], send_z, send_x)]
    scales_each = [z_scales, (z_scales[0], after(z_scales[1], gram))]
    received = [
        [send(pack(v, scales), to) for v, to in zip(values[:3], (1, 3, 2))]
        for (values, send, _), scales in zip(rings, scales_each)
    ]
    lower_factor = jnp.linalg.cholesky(gram)
    inverse = lax.linalg.triangular_solve(
        lower_factor, jnp.eye(K, dtype=f32), left_side=True, lower=True
    )
    thirds = []
    for came, (values, _, send) in zip(received, rings):
        quarters = []
        for r in range(4):
            at = slice(r * 4 * B, (r + 1) * 4 * B)
            quarters.append(sum((unpack(message[at], z_scales) for message in came), values[3 + r]))
        thirds.append(ring_exchange(quarters, send, z_scales))
    basis_factor = after(inverse, thirds[0][1][0])
    q_share = jnp.dot(
        y_share, basis_factor.T, precision=lax.Precision.HIGH, preferred_element_type=f32
    )
    z_raw = jnp.concatenate([z for z, _ in thirds], axis=0)
    z_share = jnp.dot(
        z_raw, inverse.T, precision=lax.Precision.HIGH, preferred_element_type=f32
    )
    row_scale = math.sqrt(BR * B * lax.axis_size("row"))
    return (q_share * row_scale, z_share[None])


def solution(mesh):
    in_specs = (
        P("row", "col", None, None, None),
        P("col", None),
        P("row", "col", None),
        P("row", "col", None),
        P("row", "col"),
    )
    out_specs = (P(("row", "col"), None), P("col", "row", None))
    return jax.shard_map(body, mesh=mesh, in_specs=in_specs, out_specs=out_specs, check_vma=False)
```

```python
import math

import jax
import jax.numpy as jnp
from jax import lax
from jax.experimental import pallas as pl
from jax.experimental.layout import Layout, with_layout_constraint
from jax.experimental.pallas import tpu as pltpu
from jax.sharding import PartitionSpec as P

B = 256
K = 128
BR = 128
BC = 128
NBLK = 96
CHUNK = 8
AHEAD = 28
GROUP = 4
BUFFERS = AHEAD + GROUP
VMEM_BYTES = 56 * 1024 * 1024
f32 = jnp.float32
f16 = jnp.float16


def ring(shift):
    return [(c, ((c // 2 + shift) % 4) * 2 + c % 2) for c in range(8)]


def along_x(shift):
    return [(r, ((r // 4 + shift) % 4) * 4 + r % 4) for r in range(16)]


def along_z(shift):
    return [(r, (r // 4) * 4 + (r % 4 + shift) % 4) for r in range(16)]


SHARE_ROWS = BR // 8 * B + 2 * K + 32
LOW_SCALE = 2.0**15

PAIR = [(c, c ^ 1) for c in range(8)]


def run_slots(parts, ends, begin, group, carry, total_sum, outs, out_sems):
    chunks = total_sum.shape[0] // CHUNK

    total = ends[chunks - 1]

    def begin_later(j):
        @pl.when(j < total)
        def _():
            begin(j, 0)

    lax.fori_loop(0, jnp.minimum(total, AHEAD), begin, 0)

    def clear(t, _):
        total_sum[t] = jnp.zeros((B, K), f32)
        return 0

    lax.fori_loop(0, chunks * CHUNK, clear, 0)

    writes = [[] for _ in range(chunks)]
    first = 0
    for ring_at in range(len(outs) // len(parts)):
        for i, tiles in enumerate(parts):
            at = ring_at * len(parts) + i
            for piece in range(0, tiles, CHUNK):
                size = min(CHUNK, tiles)
                sem = sum(len(w) for w in writes)
                writes[first // CHUNK].append(
                    pltpu.make_async_copy(
                        total_sum.at[pl.ds(first, size)],
                        outs[at].at[pl.ds(piece, size)],
                        out_sems.at[sem],
                    )
                )
                first += size

    def write_done(done, chunk):
        def step(c):
            for i, pieces in enumerate(writes):

                @pl.when(c == i)
                def _():
                    for copy in pieces:
                        copy.start()

            return c + 1

        return lax.while_loop(
            lambda c: (c < chunks) & (ends[jnp.minimum(c, chunks - 1)] <= done), step, chunk
        )

    def by_group(size, first):
        def step(g, state):
            chunk, carry = state
            at = first + g * size
            carry = group(begin_later, at, size, carry)
            return write_done(at + size, chunk), carry

        return step

    groups = total // GROUP
    state = write_done(0, 0), carry
    state = lax.fori_loop(0, groups, by_group(GROUP, 0), state)
    state = lax.fori_loop(0, total - groups * GROUP, by_group(1, groups * GROUP), state)
    for pieces in writes:
        for copy in pieces:
            copy.wait()
    return state[1]


def sort_slots(count, targets, chunks, order, bounds):
    def chunk_of(s):
        return jnp.where(targets[s] < 0, chunks, targets[s] // CHUNK)

    for c in range(chunks + 1):
        bounds[c] = 0

    def tally(s, _):
        c = chunk_of(s)
        bounds[c] = bounds[c] + 1
        return 0

    lax.fori_loop(0, count, tally, 0)
    total = 0
    for c in range(chunks):
        here = bounds[c]
        bounds[c] = total
        total = total + here
    bounds[chunks] = total

    def place(s, _):
        c = chunk_of(s)
        at = bounds[c]
        order[at] = s
        bounds[c] = at + 1
        return 0

    lax.fori_loop(0, count, place, 0)


def y_kernel(count, targets, cols, blocks, sketch, *rest):
    outs, stat, scratch = rest[:3], rest[3], rest[4:]
    total_sum, block_buf, sketch_buf, sems, out_sems, order, ends = scratch
    sort_slots(count[0], targets, 8, order, ends)

    def copies(j):
        s, at = order[j], lax.rem(j, BUFFERS)
        return (
            pltpu.make_async_copy(blocks.at[s], block_buf.at[at], sems.at[0, at]),
            pltpu.make_async_copy(sketch.at[cols[s]], sketch_buf.at[at], sems.at[1, at]),
        )

    def begin(j, _):
        for copy in copies(j):
            copy.start()
        return 0

    def group(begin_later, at, size, carry):
        largest, largest_block = carry
        for u in range(size):
            begin_later(at + u + AHEAD)
        for u in range(size):
            for copy in copies(at + u):
                copy.wait()
        for u in range(size):
            target = targets[order[at + u]]
            buffer = lax.rem(at + u, BUFFERS)
            tile = block_buf[buffer]
            value = total_sum[target] + jnp.dot(
                tile, sketch_buf[buffer], preferred_element_type=f32
            )
            total_sum[target] = value
            largest = jnp.maximum(largest, jnp.max(jnp.abs(value).reshape(B // 8, 8, K), axis=0))
            largest_block = jnp.maximum(
                largest_block, jnp.max(jnp.abs(tile).reshape(B // 16, 16, B), axis=0)
            )
        return largest, largest_block

    carry = jnp.zeros((8, K), f32), jnp.zeros((16, B), jnp.bfloat16)
    largest, largest_block = run_slots(
        Y_PARTS, ends, begin, group, carry, total_sum, outs, out_sems
    )
    stat[:4] = jnp.full((4, K), jnp.max(largest))
    stat[4:] = jnp.full((4, K), jnp.max(largest_block.astype(f32)))


Y_PARTS = (32, 16, 16)
Z_PARTS = (16, 16, 8, 8, 4, 4, 4, 4)


def sums_of(parts):
    return tuple(jax.ShapeDtypeStruct((n, B, K), f32) for n in parts)


def scratch_for(halves, parts, y_type):
    return [
        pltpu.VMEM((halves * 8 * CHUNK, B, K), f32),
        pltpu.VMEM((BUFFERS, B, B), jnp.bfloat16),
        pltpu.VMEM((BUFFERS, B, K), y_type),
        pltpu.SemaphoreType.DMA((2, BUFFERS)),
        pltpu.SemaphoreType.DMA((halves * 10,)),
    ]


def partial_rows(count, targets, cols, blocks, sketch):
    return pl.pallas_call(
        y_kernel,
        out_shape=sums_of(Y_PARTS) + (jax.ShapeDtypeStruct((8, K), f32),),
        in_specs=[pl.BlockSpec(memory_space=pltpu.SMEM)] * 3
        + [pl.BlockSpec(memory_space=pl.ANY)] * 2,
        out_specs=(pl.BlockSpec(memory_space=pl.ANY),) * 3
        + (pl.BlockSpec(memory_space=pltpu.VMEM),),
        scratch_shapes=scratch_for(1, Y_PARTS, jnp.bfloat16)
        + [pltpu.SMEM((NBLK + 1,), jnp.int32), pltpu.SMEM((9,), jnp.int32)],
        compiler_params=pltpu.CompilerParams(vmem_limit_bytes=VMEM_BYTES),
        cost_estimate=pl.CostEstimate(
            flops=NBLK * B * B * K, bytes_accessed=60 * 1024 * 1024, transcendentals=0
        ),
        name="partial_rows",
    )(count, targets, cols, blocks, sketch)


def table_row(row):
    return pl.multiple_of((row >> 4) * SHARE_ROWS + (row & 15) * B, 16)


def share_kernel(gathered, gram, scales, buffer, sems):
    copies = [
        pltpu.make_async_copy(
            gathered.at[pl.ds(c * SHARE_ROWS + BR // 8 * B, 2 * K + 32)], buffer.at[c], sems.at[c]
        )
        for c in range(8)
    ]
    for copy in copies:
        copy.start()
    total = jnp.zeros((K, K), f32)
    for c, copy in enumerate(copies):
        copy.wait()
        scale = jnp.exp2(buffer[c, 2 * K : 2 * K + 32].astype(f32))
        scales[c * 16 : (c + 1) * 16] = scale[:16]
        high, low = buffer[c, :K].astype(f32), buffer[c, K : 2 * K].astype(f32)
        total += (high + low * (1.0 / LOW_SCALE)) * scale[16:17]
    gram[...] = total


def read_shares(gathered):
    return pl.pallas_call(
        share_kernel,
        out_shape=(jax.ShapeDtypeStruct((K, K), f32), jax.ShapeDtypeStruct((BR, K), f32)),
        in_specs=[pl.BlockSpec(memory_space=pl.ANY)],
        out_specs=(pl.BlockSpec(memory_space=pltpu.VMEM),) * 2,
        scratch_shapes=[
            pltpu.VMEM((8, 2 * K + 32, K), jnp.int16),
            pltpu.SemaphoreType.DMA((8,)),
        ],
        compiler_params=pltpu.CompilerParams(vmem_limit_bytes=VMEM_BYTES),
        name="read_shares",
    )(gathered)


def z_kernel(order, ends, targets, rows, blocks, table, tile_scales, *rest):
    outs, scratch = rest[:16], rest[16:]
    total_sum, block_buf, y_buf, sems, out_sems = scratch

    def copies(j):
        s, at = order[j], lax.rem(j, BUFFERS)
        return (
            pltpu.make_async_copy(blocks.at[s], block_buf.at[at], sems.at[0, at]),
            pltpu.make_async_copy(
                table.at[pl.ds(table_row(rows[s]), B)], y_buf.at[at], sems.at[1, at]
            ),
        )

    def begin(j, _):
        for copy in copies(j):
            copy.start()
        return 0

    def group(begin_later, at, size, carry):
        for u in range(size):
            begin_later(at + u + AHEAD)
        for u in range(size):
            for copy in copies(at + u):
                copy.wait()
        for u in range(size):
            buffer = lax.rem(at + u, BUFFERS)
            value = y_buf[buffer].astype(f32)
            high = value.astype(jnp.bfloat16)
            low = (value - high.astype(f32)).astype(jnp.bfloat16)
            product = lax.dot_general(
                block_buf[buffer],
                jnp.concatenate([high, low], axis=1),
                (((0,), (0,)), ((), ())),
                preferred_element_type=f32,
            )
            slot = order[at + u]
            product = (product[:, :K] + product[:, K:]) * tile_scales[pl.ds(rows[slot], 1)]
            total_sum[targets[slot]] += product
        return carry

    run_slots(
        Z_PARTS, ends, begin, group, 0, total_sum, outs, out_sems
    )


def partial_cols(plan, rows, blocks, table, tile_scales):
    return pl.pallas_call(
        z_kernel,
        out_shape=sums_of(Z_PARTS * 2),
        in_specs=[pl.BlockSpec(memory_space=pltpu.SMEM)] * 4
        + [pl.BlockSpec(memory_space=pl.ANY)] * 2
        + [pl.BlockSpec(memory_space=pltpu.VMEM)],
        out_specs=(pl.BlockSpec(memory_space=pl.ANY),) * 16,
        scratch_shapes=scratch_for(2, Z_PARTS, jnp.int16),
        compiler_params=pltpu.CompilerParams(vmem_limit_bytes=VMEM_BYTES),
        cost_estimate=pl.CostEstimate(
            flops=NBLK * B * B * K * 4, bytes_accessed=42 * 1024 * 1024, transcendentals=0
        ),
        name="partial_cols",
    )(*plan, rows, blocks, table, tile_scales)


def scales_for(bound):
    exponent = jnp.ceil(jnp.log2(jnp.maximum(bound, 1e-30))) - 15.0
    scale, inverse = lax.optimization_barrier((jnp.exp2(exponent), jnp.exp2(-exponent)))
    return scale[0, 0], inverse[0, 0]


def by_rows(value):
    return with_layout_constraint(value, Layout(tuple(range(value.ndim))))


def pack(value, scales):
    return by_rows((value * scales[1]).astype(f16))


def unpack(message, scales):
    return message.astype(f32) * scales[0]


PLACES = (6, 7, 4, 1, 0, 2, 3, 5)


HALF = CHUNK * B


def ring_first(messages, send):
    return lax.optimization_barrier((send(messages[0], 1), send(messages[1], -1)))


def ring_second(received, passing, send, scales, below, above):
    messages = lax.optimization_barrier(
        (
            pack(passing[0] + unpack(received[0][:HALF], below), scales),
            pack(passing[1] + unpack(received[1][:HALF], above), scales),
        )
    )
    sums = send(messages[0], 1), send(messages[1], -1)
    return lax.optimization_barrier((received, sums, messages))


def ring_total(received, sums, staying, scales, below, above):
    def total(which, start=0, stop=HALF):
        direct = received[1 - which][HALF + start : HALF + stop]
        return (
            staying[which][start // (stop - start)]
            + unpack(direct, below if which else above)
            + unpack(sums[which][start:stop], scales)
        )

    return total


def ring_exchange(parts, send, scales):
    received = [send(pack(parts[r], scales), r) for r in (1, 3, 2)]
    up, down, across = (unpack(message, scales) for message in received)
    return parts[0] + up + down + across, received


def exponent_of(largest):
    return jnp.floor(jnp.log2(jnp.maximum(largest, 1e-30))) - 14.0


def whole(value):
    return jnp.clip(jnp.round(value), -32767.0, 32767.0)


def after(value, other):
    return value + (0.0 * other[(0,) * other.ndim]).astype(value.dtype)


def ring_fold(value, send, op):
    across, below, above = send(value, 2), send(value, 1), send(value, -1)
    return op(op(value, across), op(below, above)), below, above


def body(blocks, sketch, block_row, block_col, counts):
    blocks = blocks[0, 0]
    rows, cols = block_row[0, 0], block_col[0, 0]
    count = counts[0, 0]
    row_at, col_at = lax.axis_index("row"), lax.axis_index("col")
    here_x, here_z = row_at // 4, row_at % 4
    here_y, core = col_at // 2, col_at % 2
    sketch_table = sketch.reshape(BC, B, K)

    def send_core(value):
        return lax.ppermute(value, "col", PAIR)

    def send_y(value, shift):
        return lax.ppermute(value, "col", ring(shift))

    def send_x(value, shift):
        return lax.ppermute(value, "row", along_x(shift))

    def send_z(value, shift):
        return lax.ppermute(value, "row", along_z(shift))

    live = jnp.arange(NBLK, dtype=jnp.int32) < count

    def chunk_of(rel, half):
        key = (rel & 3) * 2 + half
        chunk = PLACES[7]
        for k in range(7):
            chunk = jnp.where(key == k, PLACES[k], chunk)
        return chunk * CHUNK

    y_target = chunk_of((rows >> 5) - here_y, (rows >> 3) & 1) + (rows & 7)
    row_core = (rows >> 4) & 1
    rel_x, rel_z = ((cols >> 5) - here_x) & 3, ((cols >> 3) - here_z) & 3
    is_a = ((cols >> 2) & 1) == 0
    one, two = jnp.where(is_a, rel_x, rel_z), jnp.where(is_a, rel_z, rel_x)
    z_target = chunk_of(one, two >> 1) + (two & 1) * 4 + (cols & 3) + jnp.where(is_a, 0, 8 * CHUNK)
    other_target = jnp.where(live & (row_core != core), y_target, -1)
    own_target = jnp.where(live & (row_core == core), y_target, -1)
    z_target = jnp.where(live, z_target, -1)

    count = count[None]

    def flat(values):
        return [v.reshape(-1, K) for v in values]

    *other, other_stat = partial_rows(count, other_target, cols, blocks, sketch_table)
    *from_pair, pair_stat = [send_core(v) for v in (*other, other_stat)]
    *own, own_stat = partial_rows(count, own_target, cols, blocks, sketch_table)
    own, from_pair = flat(own), flat(from_pair)

    first_bound = own_stat + pair_stat
    scales = scales_for(first_bound[:1])
    own_first, pair_first = (v.reshape(2, 2 * HALF, K) for v in (own[0], from_pair[0]))
    first = [pack(own_first[i] + pair_first[i], scales) for i in range(2)]
    received = [send_y(first[0], 1), send_y(first[1], -1)]

    in_first = lax.broadcasted_iota(jnp.int32, (8, K), 0) < 4
    entries = jnp.maximum(own_stat, other_stat) * count[0].astype(f32)
    bounds, _ = lax.optimization_barrier((jnp.where(in_first, first_bound, entries), first))
    bounds, below, above = ring_fold(bounds, send_y, jnp.maximum)
    later, _ = lax.optimization_barrier(((own[1:], from_pair[1:]), bounds))
    parts = [
        [mine[at : at + HALF] + pair[at : at + HALF] for at in (0, HALF)] for mine, pair in zip(*later)
    ]
    passing, staying = lax.optimization_barrier(parts)
    around = scales_for(below[:1]), scales_for(above[:1])
    sum_scales = scales_for(bounds[:1] * 4.0)
    received, sums, messages = ring_second(received, passing, send_y, sum_scales, *around)
    z_target = after(z_target, staying[0])
    chunk = jnp.where(z_target < 0, 16, z_target // CHUNK)
    slot = jnp.arange(NBLK, dtype=jnp.int32)
    key = chunk * NBLK + slot
    rank = jnp.sum((key[None, :] < key[:, None]).astype(jnp.int32), axis=1)
    order = jnp.sum(jnp.where(rank[None, :] == slot[:, None], slot[None, :], 0), axis=1)
    ends = jnp.arange(16, dtype=jnp.int32)
    ends = jnp.sum((chunk[None, :] <= ends[:, None]).astype(jnp.int32), axis=1)
    z_plan = order, ends, z_target

    y_part = ring_total(received, sums, [[v] for v in staying], sum_scales, *around)
    y_share = jnp.concatenate([y_part(0), y_part(1)], axis=0)

    bounds, _ = lax.optimization_barrier((bounds, messages))
    bounds = jnp.maximum(bounds, send_core(bounds))
    y_scales = scales_for(bounds[:1] * 4.0)
    bounds = ring_fold(ring_fold(bounds, send_x, jnp.maximum)[0], send_z, jnp.maximum)[0]
    z_scales = scales_for(bounds[:1] * bounds[4:5] * (4.0 * 16.0 * B))

    gram = jnp.dot(
        y_share.T, y_share, precision=lax.Precision.HIGH, preferred_element_type=f32
    )
    tiles = y_share.reshape(BR // 8, B, K)
    exponents = exponent_of(jnp.max(jnp.abs(tiles), axis=(1, 2)))
    gram_exponent = exponent_of(jnp.max(jnp.abs(gram)))
    codes = whole(tiles * jnp.exp2(-exponents)[:, None, None]).reshape(-1, K)
    gram = gram * jnp.exp2(-gram_exponent)
    high = whole(gram)
    low = whole((gram - high) * LOW_SCALE)
    scale_rows = jnp.concatenate([exponents, jnp.full((16,), gram_exponent)])
    scale_rows = jnp.broadcast_to(scale_rows[:, None], (32, K)).astype(jnp.int16)
    scale_rows = by_rows(lax.optimization_barrier(scale_rows))
    mine = [v.astype(jnp.int16) for v in (codes, high, low)]
    mine = jnp.concatenate([*mine, scale_rows], axis=0)
    mine, z_scales = lax.optimization_barrier((by_rows(mine), z_scales))
    gathered = lax.all_gather(mine, "col", axis=0, tiled=True)
    gram, tile_scales = read_shares(gathered)
    gram = ring_fold(by_rows(gram), send_x, jnp.add)[0]
    partial = flat(partial_cols(z_plan, rows, blocks, gathered, tile_scales))
    gram = by_rows(ring_fold(gram, send_z, jnp.add)[0])

    rings = [(partial[:8], send_x, send_z), (partial[8:], send_z, send_x)]
    around = z_scales, z_scales
    scales_each = [z_scales, (z_scales[0], after(z_scales[1], gram))]
    messages = [
        [pack(v, scales) for v in values[:2]] for (values, _, _), scales in zip(rings, scales_each)
    ]
    received = [[send(m[0], 1), send(m[1], -1)] for m, (_, send, _) in zip(messages, rings)]
    lower_factor = jnp.linalg.cholesky(gram)
    seconds = [
        ring_second(r, values[2:4], send, z_scales, *around)
        for r, (values, send, _) in zip(received, rings)
    ]
    inverse = lax.linalg.triangular_solve(
        lower_factor, jnp.eye(K, dtype=f32), left_side=True, lower=True
    )
    thirds = []
    for (direct, sums, _), (values, _, send) in zip(seconds, rings):
        total = ring_total(direct, sums, [values[4:6], values[6:]], z_scales, *around)
        quarters = [total(r // 2, r % 2 * 4 * B, (r % 2 + 1) * 4 * B) for r in range(4)]
        thirds.append(ring_exchange(quarters, send, z_scales))
    basis_factor = after(inverse, thirds[0][1][0])
    q_share = jnp.dot(
        y_share, basis_factor.T, precision=lax.Precision.HIGH, preferred_element_type=f32
    )
    z_raw = jnp.concatenate([z for z, _ in thirds], axis=0)
    z_share = jnp.dot(
        z_raw, inverse.T, precision=lax.Precision.HIGH, preferred_element_type=f32
    )
    row_scale = math.sqrt(BR * B * lax.axis_size("row"))
    return (q_share * row_scale, z_share[None])


def solution(mesh):
    in_specs = (
        P("row", "col", None, None, None),
        P("col", None),
        P("row", "col", None),
        P("row", "col", None),
        P("row", "col"),
    )
    out_specs = (P(("row", "col"), None), P("col", "row", None))
    return jax.shard_map(body, mesh=mesh, in_specs=in_specs, out_specs=out_specs, check_vma=False)
```

```python
import math

import jax
import jax.numpy as jnp
from jax import lax
from jax.experimental import pallas as pl
from jax.experimental.layout import Layout, with_layout_constraint
from jax.experimental.pallas import tpu as pltpu
from jax.sharding import PartitionSpec as P

B = 256
K = 128
BR = 128
BC = 128
NBLK = 96
CHUNK = 8
AHEAD = 28
GROUP = 4
BUFFERS = AHEAD + GROUP
VMEM_BYTES = 56 * 1024 * 1024
f32 = jnp.float32
f16 = jnp.float16


def ring(shift):
    return [(c, ((c // 2 + shift) % 4) * 2 + c % 2) for c in range(8)]


def along_x(shift):
    return [(r, ((r // 4 + shift) % 4) * 4 + r % 4) for r in range(16)]


def along_z(shift):
    return [(r, (r // 4) * 4 + (r % 4 + shift) % 4) for r in range(16)]


SHARE_ROWS = BR // 8 * B + 2 * K + 32
LOW_SCALE = 2.0**15

PAIR = [(c, c ^ 1) for c in range(8)]


def run_slots(parts, ends, begin, group, carry, total_sum, outs, out_sems):
    chunks = total_sum.shape[0] // CHUNK

    total = ends[chunks - 1]

    def begin_later(j):
        @pl.when(j < total)
        def _():
            begin(j, 0)

    lax.fori_loop(0, jnp.minimum(total, AHEAD), begin, 0)

    def clear(t, _):
        total_sum[t] = jnp.zeros((B, K), f32)
        return 0

    lax.fori_loop(0, chunks * CHUNK, clear, 0)

    writes = [[] for _ in range(chunks)]
    first = 0
    for ring_at in range(len(outs) // len(parts)):
        for i, tiles in enumerate(parts):
            at = ring_at * len(parts) + i
            for piece in range(0, tiles, CHUNK):
                size = min(CHUNK, tiles)
                sem = sum(len(w) for w in writes)
                writes[first // CHUNK].append(
                    pltpu.make_async_copy(
                        total_sum.at[pl.ds(first, size)],
                        outs[at].at[pl.ds(piece, size)],
                        out_sems.at[sem],
                    )
                )
                first += size

    def write_done(done, chunk):
        def step(c):
            for i, pieces in enumerate(writes):

                @pl.when(c == i)
                def _():
                    for copy in pieces:
                        copy.start()

            return c + 1

        return lax.while_loop(
            lambda c: (c < chunks) & (ends[jnp.minimum(c, chunks - 1)] <= done), step, chunk
        )

    def by_group(size, first):
        def step(g, state):
            chunk, carry = state
            at = first + g * size
            carry = group(begin_later, at, size, carry)
            return write_done(at + size, chunk), carry

        return step

    groups = total // GROUP
    state = write_done(0, 0), carry
    state = lax.fori_loop(0, groups, by_group(GROUP, 0), state)
    state = lax.fori_loop(0, total - groups * GROUP, by_group(1, groups * GROUP), state)
    for pieces in writes:
        for copy in pieces:
            copy.wait()
    return state[1]


def sort_slots(count, targets, chunks, order, bounds):
    def chunk_of(s):
        return jnp.where(targets[s] < 0, chunks, targets[s] // CHUNK)

    for c in range(chunks + 1):
        bounds[c] = 0

    def tally(s, _):
        c = chunk_of(s)
        bounds[c] = bounds[c] + 1
        return 0

    lax.fori_loop(0, count, tally, 0)
    total = 0
    for c in range(chunks):
        here = bounds[c]
        bounds[c] = total
        total = total + here
    bounds[chunks] = total

    def place(s, _):
        c = chunk_of(s)
        at = bounds[c]
        order[at] = s
        bounds[c] = at + 1
        return 0

    lax.fori_loop(0, count, place, 0)


def y_kernel(count, targets, cols, blocks, sketch, *rest):
    outs, stat, scratch = rest[:2], rest[2], rest[3:]
    total_sum, block_buf, sketch_buf, sems, out_sems, order, ends = scratch
    sort_slots(count[0], targets, 8, order, ends)

    def copies(j):
        s, at = order[j], lax.rem(j, BUFFERS)
        return (
            pltpu.make_async_copy(blocks.at[s], block_buf.at[at], sems.at[0, at]),
            pltpu.make_async_copy(sketch.at[cols[s]], sketch_buf.at[at], sems.at[1, at]),
        )

    def begin(j, _):
        for copy in copies(j):
            copy.start()
        return 0

    def group(begin_later, at, size, carry):
        largest, largest_block = carry
        for u in range(size):
            begin_later(at + u + AHEAD)
        for u in range(size):
            for copy in copies(at + u):
                copy.wait()
        for u in range(size):
            target = targets[order[at + u]]
            buffer = lax.rem(at + u, BUFFERS)
            tile = block_buf[buffer]
            value = total_sum[target] + jnp.dot(
                tile, sketch_buf[buffer], preferred_element_type=f32
            )
            total_sum[target] = value
            largest = jnp.maximum(largest, jnp.max(jnp.abs(value).reshape(B // 8, 8, K), axis=0))
            largest_block = jnp.maximum(
                largest_block, jnp.max(jnp.abs(tile).reshape(B // 16, 16, B), axis=0)
            )
        return largest, largest_block

    carry = jnp.zeros((8, K), f32), jnp.zeros((16, B), jnp.bfloat16)
    largest, largest_block = run_slots(
        Y_PARTS, ends, begin, group, carry, total_sum, outs, out_sems
    )
    stat[:4] = jnp.full((4, K), jnp.max(largest))
    stat[4:] = jnp.full((4, K), jnp.max(largest_block.astype(f32)))


Y_PARTS = (32, 32)
Z_PARTS = (16, 16, 8, 8, 4, 4, 4, 4)


def sums_of(parts):
    return tuple(jax.ShapeDtypeStruct((n, B, K), f32) for n in parts)


def scratch_for(halves, parts, y_type):
    return [
        pltpu.VMEM((halves * 8 * CHUNK, B, K), f32),
        pltpu.VMEM((BUFFERS, B, B), jnp.bfloat16),
        pltpu.VMEM((BUFFERS, B, K), y_type),
        pltpu.SemaphoreType.DMA((2, BUFFERS)),
        pltpu.SemaphoreType.DMA((halves * 10,)),
    ]


def partial_rows(count, targets, cols, blocks, sketch):
    return pl.pallas_call(
        y_kernel,
        out_shape=sums_of(Y_PARTS) + (jax.ShapeDtypeStruct((8, K), f32),),
        in_specs=[pl.BlockSpec(memory_space=pltpu.SMEM)] * 3
        + [pl.BlockSpec(memory_space=pl.ANY)] * 2,
        out_specs=(pl.BlockSpec(memory_space=pl.ANY),) * 2
        + (pl.BlockSpec(memory_space=pltpu.VMEM),),
        scratch_shapes=scratch_for(1, Y_PARTS, jnp.bfloat16)
        + [pltpu.SMEM((NBLK + 1,), jnp.int32), pltpu.SMEM((9,), jnp.int32)],
        compiler_params=pltpu.CompilerParams(vmem_limit_bytes=VMEM_BYTES),
        cost_estimate=pl.CostEstimate(
            flops=NBLK * B * B * K, bytes_accessed=60 * 1024 * 1024, transcendentals=0
        ),
        name="partial_rows",
    )(count, targets, cols, blocks, sketch)


def table_row(row):
    return pl.multiple_of((row >> 4) * SHARE_ROWS + (row & 15) * B, 16)


def share_kernel(gathered, gram, scales, buffer, sems):
    copies = [
        pltpu.make_async_copy(
            gathered.at[pl.ds(c * SHARE_ROWS + BR // 8 * B, 2 * K + 32)], buffer.at[c], sems.at[c]
        )
        for c in range(8)
    ]
    for copy in copies:
        copy.start()
    total = jnp.zeros((K, K), f32)
    for c, copy in enumerate(copies):
        copy.wait()
        scale = jnp.exp2(buffer[c, 2 * K : 2 * K + 32].astype(f32))
        scales[c * 16 : (c + 1) * 16] = scale[:16]
        high, low = buffer[c, :K].astype(f32), buffer[c, K : 2 * K].astype(f32)
        total += (high + low * (1.0 / LOW_SCALE)) * scale[16:17]
    gram[...] = total


def read_shares(gathered):
    return pl.pallas_call(
        share_kernel,
        out_shape=(jax.ShapeDtypeStruct((K, K), f32), jax.ShapeDtypeStruct((BR, K), f32)),
        in_specs=[pl.BlockSpec(memory_space=pl.ANY)],
        out_specs=(pl.BlockSpec(memory_space=pltpu.VMEM),) * 2,
        scratch_shapes=[
            pltpu.VMEM((8, 2 * K + 32, K), jnp.int16),
            pltpu.SemaphoreType.DMA((8,)),
        ],
        compiler_params=pltpu.CompilerParams(vmem_limit_bytes=VMEM_BYTES),
        name="read_shares",
    )(gathered)


def z_kernel(order, ends, targets, rows, blocks, table, tile_scales, *rest):
    outs, scratch = rest[:16], rest[16:]
    total_sum, block_buf, y_buf, sems, out_sems = scratch

    def copies(j):
        s, at = order[j], lax.rem(j, BUFFERS)
        return (
            pltpu.make_async_copy(blocks.at[s], block_buf.at[at], sems.at[0, at]),
            pltpu.make_async_copy(
                table.at[pl.ds(table_row(rows[s]), B)], y_buf.at[at], sems.at[1, at]
            ),
        )

    def begin(j, _):
        for copy in copies(j):
            copy.start()
        return 0

    def group(begin_later, at, size, carry):
        for u in range(size):
            begin_later(at + u + AHEAD)
        for u in range(size):
            for copy in copies(at + u):
                copy.wait()
        for u in range(size):
            buffer = lax.rem(at + u, BUFFERS)
            value = y_buf[buffer].astype(f32)
            high = value.astype(jnp.bfloat16)
            low = (value - high.astype(f32)).astype(jnp.bfloat16)
            product = lax.dot_general(
                block_buf[buffer],
                jnp.concatenate([high, low], axis=1),
                (((0,), (0,)), ((), ())),
                preferred_element_type=f32,
            )
            slot = order[at + u]
            product = (product[:, :K] + product[:, K:]) * tile_scales[pl.ds(rows[slot], 1)]
            total_sum[targets[slot]] += product
        return carry

    run_slots(
        Z_PARTS, ends, begin, group, 0, total_sum, outs, out_sems
    )


def partial_cols(plan, rows, blocks, table, tile_scales):
    return pl.pallas_call(
        z_kernel,
        out_shape=sums_of(Z_PARTS * 2),
        in_specs=[pl.BlockSpec(memory_space=pltpu.SMEM)] * 4
        + [pl.BlockSpec(memory_space=pl.ANY)] * 2
        + [pl.BlockSpec(memory_space=pltpu.VMEM)],
        out_specs=(pl.BlockSpec(memory_space=pl.ANY),) * 16,
        scratch_shapes=scratch_for(2, Z_PARTS, jnp.int16),
        compiler_params=pltpu.CompilerParams(vmem_limit_bytes=VMEM_BYTES),
        cost_estimate=pl.CostEstimate(
            flops=NBLK * B * B * K * 4, bytes_accessed=42 * 1024 * 1024, transcendentals=0
        ),
        name="partial_cols",
    )(*plan, rows, blocks, table, tile_scales)


def scales_for(bound):
    exponent = jnp.ceil(jnp.log2(jnp.maximum(bound, 1e-30))) - 15.0
    scale, inverse = lax.optimization_barrier((jnp.exp2(exponent), jnp.exp2(-exponent)))
    return scale[0, 0], inverse[0, 0]


def by_rows(value):
    return with_layout_constraint(value, Layout(tuple(range(value.ndim))))


def pack(value, scales):
    return by_rows((value * scales[1]).astype(f16))


def unpack(message, scales):
    return message.astype(f32) * scales[0]


PLACES = (6, 7, 4, 1, 0, 2, 3, 5)


HALF = CHUNK * B


def ring_first(messages, send):
    return lax.optimization_barrier((send(messages[0], 1), send(messages[1], -1)))


def ring_second(received, passing, send, scales, below, above):
    messages = lax.optimization_barrier(
        (
            pack(passing[0] + unpack(received[0][:HALF], below), scales),
            pack(passing[1] + unpack(received[1][:HALF], above), scales),
        )
    )
    sums = send(messages[0], 1), send(messages[1], -1)
    return lax.optimization_barrier((received, sums, messages))


def ring_total(received, sums, staying, scales, below, above):
    def total(which, start=0, stop=HALF):
        direct = received[1 - which][HALF + start : HALF + stop]
        return (
            staying[which][start // (stop - start)]
            + unpack(direct, below if which else above)
            + unpack(sums[which][start:stop], scales)
        )

    return total


def ring_exchange(parts, send, scales):
    received = [send(pack(parts[r], scales), r) for r in (1, 3, 2)]
    up, down, across = (unpack(message, scales) for message in received)
    return parts[0] + up + down + across, received


def exponent_of(largest):
    return jnp.floor(jnp.log2(jnp.maximum(largest, 1e-30))) - 14.0


def whole(value):
    return jnp.clip(jnp.round(value), -32767.0, 32767.0)


def after(value, other):
    return value + (0.0 * other[(0,) * other.ndim]).astype(value.dtype)


def ring_fold(value, send, op):
    across, below, above = send(value, 2), send(value, 1), send(value, -1)
    return op(op(value, across), op(below, above)), below, above


def body(blocks, sketch, block_row, block_col, counts):
    blocks = blocks[0, 0]
    rows, cols = block_row[0, 0], block_col[0, 0]
    count = counts[0, 0]
    row_at, col_at = lax.axis_index("row"), lax.axis_index("col")
    here_x, here_z = row_at // 4, row_at % 4
    here_y, core = col_at // 2, col_at % 2
    sketch_table = sketch.reshape(BC, B, K)

    def send_core(value):
        return lax.ppermute(value, "col", PAIR)

    def send_y(value, shift):
        return lax.ppermute(value, "col", ring(shift))

    def send_x(value, shift):
        return lax.ppermute(value, "row", along_x(shift))

    def send_z(value, shift):
        return lax.ppermute(value, "row", along_z(shift))

    live = jnp.arange(NBLK, dtype=jnp.int32) < count

    def chunk_of(rel, half):
        key = (rel & 3) * 2 + half
        chunk = PLACES[7]
        for k in range(7):
            chunk = jnp.where(key == k, PLACES[k], chunk)
        return chunk * CHUNK

    y_target = chunk_of((rows >> 5) - here_y, (rows >> 3) & 1) + (rows & 7)
    row_core = (rows >> 4) & 1
    rel_x, rel_z = ((cols >> 5) - here_x) & 3, ((cols >> 3) - here_z) & 3
    is_a = ((cols >> 2) & 1) == 0
    one, two = jnp.where(is_a, rel_x, rel_z), jnp.where(is_a, rel_z, rel_x)
    z_target = chunk_of(one, two >> 1) + (two & 1) * 4 + (cols & 3) + jnp.where(is_a, 0, 8 * CHUNK)
    other_target = jnp.where(live & (row_core != core), y_target, -1)
    own_target = jnp.where(live & (row_core == core), y_target, -1)
    z_target = jnp.where(live, z_target, -1)

    count = count[None]

    def flat(values):
        return [v.reshape(-1, K) for v in values]

    *other, other_stat = partial_rows(count, other_target, cols, blocks, sketch_table)
    *from_pair, pair_stat = [send_core(v) for v in (*other, other_stat)]
    *own, own_stat = partial_rows(count, own_target, cols, blocks, sketch_table)
    own, from_pair = flat(own), flat(from_pair)

    first_bound = own_stat + pair_stat
    scales = scales_for(first_bound[:1])
    own_first, pair_first = (v.reshape(2, 2 * HALF, K) for v in (own[0], from_pair[0]))
    first = [pack(own_first[i] + pair_first[i], scales) for i in range(2)]
    received = [send_y(first[0], 1), send_y(first[1], -1)]

    in_first = lax.broadcasted_iota(jnp.int32, (8, K), 0) < 4
    entries = jnp.maximum(own_stat, other_stat) * count[0].astype(f32)
    bounds, _ = lax.optimization_barrier((jnp.where(in_first, first_bound, entries), first))
    bounds, below, above = ring_fold(bounds, send_y, jnp.maximum)
    later, _ = lax.optimization_barrier(((own[1], from_pair[1]), bounds))
    parts = [
        [later[0][at : at + HALF] + later[1][at : at + HALF] for at in (start, start + HALF)]
        for start in (0, 2 * HALF)
    ]
    passing, staying = lax.optimization_barrier(parts)
    around = scales_for(below[:1]), scales_for(above[:1])
    sum_scales = scales_for(bounds[:1] * 4.0)
    received, sums, messages = ring_second(received, passing, send_y, sum_scales, *around)
    z_target = after(z_target, staying[0])
    chunk = jnp.where(z_target < 0, 16, z_target // CHUNK)
    slot = jnp.arange(NBLK, dtype=jnp.int32)
    key = chunk * NBLK + slot
    rank = jnp.sum((key[None, :] < key[:, None]).astype(jnp.int32), axis=1)
    order = jnp.sum(jnp.where(rank[None, :] == slot[:, None], slot[None, :], 0), axis=1)
    ends = jnp.arange(16, dtype=jnp.int32)
    ends = jnp.sum((chunk[None, :] <= ends[:, None]).astype(jnp.int32), axis=1)
    z_plan = order, ends, z_target

    y_part = ring_total(received, sums, [[v] for v in staying], sum_scales, *around)
    y_share = jnp.concatenate([y_part(0), y_part(1)], axis=0)

    bounds, _ = lax.optimization_barrier((bounds, messages))
    bounds = jnp.maximum(bounds, send_core(bounds))
    y_scales = scales_for(bounds[:1] * 4.0)
    bounds = ring_fold(ring_fold(bounds, send_x, jnp.maximum)[0], send_z, jnp.maximum)[0]
    z_scales = scales_for(bounds[:1] * bounds[4:5] * (4.0 * 16.0 * B))

    gram = jnp.dot(
        y_share.T, y_share, precision=lax.Precision.HIGH, preferred_element_type=f32
    )
    tiles = y_share.reshape(BR // 8, B, K)
    exponents = exponent_of(jnp.max(jnp.abs(tiles), axis=(1, 2)))
    gram_exponent = exponent_of(jnp.max(jnp.abs(gram)))
    codes = whole(tiles * jnp.exp2(-exponents)[:, None, None]).reshape(-1, K)
    gram = gram * jnp.exp2(-gram_exponent)
    high = whole(gram)
    low = whole((gram - high) * LOW_SCALE)
    scale_rows = jnp.concatenate([exponents, jnp.full((16,), gram_exponent)])
    scale_rows = jnp.broadcast_to(scale_rows[:, None], (32, K)).astype(jnp.int16)
    scale_rows = by_rows(lax.optimization_barrier(scale_rows))
    mine = [v.astype(jnp.int16) for v in (codes, high, low)]
    mine = jnp.concatenate([*mine, scale_rows], axis=0)
    mine, z_scales = lax.optimization_barrier((by_rows(mine), z_scales))
    gathered = lax.all_gather(mine, "col", axis=0, tiled=True)
    gram, tile_scales = read_shares(gathered)
    gram = ring_fold(by_rows(gram), send_x, jnp.add)[0]
    partial = flat(partial_cols(z_plan, rows, blocks, gathered, tile_scales))
    gram = by_rows(ring_fold(gram, send_z, jnp.add)[0])

    rings = [(partial[:8], send_x, send_z), (partial[8:], send_z, send_x)]
    around = z_scales, z_scales
    scales_each = [z_scales, (z_scales[0], after(z_scales[1], gram))]
    messages = [
        [pack(v, scales) for v in values[:2]] for (values, _, _), scales in zip(rings, scales_each)
    ]
    received = [[send(m[0], 1), send(m[1], -1)] for m, (_, send, _) in zip(messages, rings)]
    lower_factor = jnp.linalg.cholesky(gram)
    seconds = [
        ring_second(r, values[2:4], send, z_scales, *around)
        for r, (values, send, _) in zip(received, rings)
    ]
    inverse = lax.linalg.triangular_solve(
        lower_factor, jnp.eye(K, dtype=f32), left_side=True, lower=True
    )
    thirds = []
    for (direct, sums, _), (values, _, send) in zip(seconds, rings):
        total = ring_total(direct, sums, [values[4:6], values[6:]], z_scales, *around)
        quarters = [total(r // 2, r % 2 * 4 * B, (r % 2 + 1) * 4 * B) for r in range(4)]
        thirds.append(ring_exchange(quarters, send, z_scales))
    basis_factor = after(inverse, thirds[0][1][0])
    q_share = jnp.dot(
        y_share, basis_factor.T, precision=lax.Precision.HIGH, preferred_element_type=f32
    )
    z_raw = jnp.concatenate([z for z, _ in thirds], axis=0)
    z_share = jnp.dot(
        z_raw, inverse.T, precision=lax.Precision.HIGH, preferred_element_type=f32
    )
    row_scale = math.sqrt(BR * B * lax.axis_size("row"))
    return (q_share * row_scale, z_share[None])


def solution(mesh):
    in_specs = (
        P("row", "col", None, None, None),
        P("col", None),
        P("row", "col", None),
        P("row", "col", None),
        P("row", "col"),
    )
    out_specs = (P(("row", "col"), None), P("col", "row", None))
    return jax.shard_map(body, mesh=mesh, in_specs=in_specs, out_specs=out_specs, check_vma=False)
```
